1024 devices in a mesh: seq: 32 (over y, x_hi, core), mp: 32 (over z, x_lo).
Axes of the slice: x: 8 (x_hi: 2, x_lo: 4; x = x_hi * 4 + x_lo), y: 8, z: 8, core: 2. Of those that a mesh axis runs over, the one named last changes fastest.
Arguments:
- fields: float32 [16, 256, 256, 256], P(None, 'seq', 'mp'), may hold values from -6 to 6
- lagged_source: bfloat16 [13, 256, 256, 256], P(None, 'seq', 'mp'), may hold values from -6 to 6
- embed_weight: bfloat16 [65536, 1024], P('mp'), may hold values from -0.0234375 to 0.0234375
- position: bfloat16 [4096, 1024], P('seq'), may hold values from -6 to 6
- norm_gain: float32 [1024], replicated, may hold values from 0.1 to 1.9
- head_weight: bfloat16 [1024, 45056], P(None, 'mp'), may hold values from -0.1875 to 0.1875
Outputs:
- fields_next: float32 [16, 256, 256, 256], P(None, 'seq', 'mp')
- source_terms: bfloat16 [4096, 45056], P('seq', 'mp')
The draws below stay inside these ranges and needn't reach their ends.
All inputs are finite; a program needn't handle non-finite values.
Results may differ from the reference program's by a relative error of at most 0.0054.
Values may be sent and summed in bfloat16 or wider, within the bound.
No kernel may reach another device: no remote copies, remote signals or barrier semaphores. Data moves between devices by JAX's collectives and lax.ppermute only.
A program may use at most 64 MiB of HBM per device.

```python
import jax
import jax.numpy as jnp
from jax import lax

SPEC = 13
NF = 16
PATCH = 16
WIDTH = 1024
NZ = 256
NX = 256
NY = 256
ZB = 2
PX = 16
PY = 16
PZL = 8
GROUPS = 4
TOKENS = 4096
FEAT = 65536
OUTF = 45056
N_SEQ = 32
N_MP = 32


def block_levels(own_key, dims, pieces, smallest, top_value):
    level, own = 1.0, jax.random.fold_in(own_key, 6)
    for dim, parts in pieces:
        draws = jnp.exp(jax.random.uniform(jax.random.fold_in(own, dim), (parts,), jnp.float32, smallest / len(pieces), top_value / len(pieces)))
        level = level * jnp.repeat(draws, dims[dim] // parts).reshape([-1 if axis == dim else 1 for axis in range(len(dims))])
    return level


def gaussian(rng, shape, spread, reach, pieces=(), kind=jnp.bfloat16):
    drawn = spread * jax.random.normal(rng, shape, jnp.float32)
    if pieces:
        drawn = drawn * block_levels(rng, shape, pieces, -0.22, 0.18)
    return jnp.clip(drawn, -reach, reach).astype(kind)


def setup_inputs(seed: int = 0) -> dict:
    key_of = jax.random.split(jax.random.key(seed), 7)
    fields = gaussian(key_of[0], (NF, NX, NY, NZ), 1.0, 6.0, ((1, 32), (2, 32)), jnp.float32)
    lagged_source = gaussian(key_of[1], (SPEC, NX, NY, NZ), 1.0, 6.0, ((1, 32), (2, 32)))
    embed_weight = gaussian(key_of[2], (FEAT, WIDTH), FEAT ** -0.5, 0.0234375, ((0, 32),))
    position = gaussian(key_of[3], (TOKENS, WIDTH), 1.0, 6.0, ((0, 32),))
    norm_gain = jnp.clip(1.0 + 0.18 * jax.random.normal(key_of[4], (WIDTH,), jnp.float32), 0.1, 1.9)
    head_weight = gaussian(key_of[5], (WIDTH, OUTF), WIDTH ** -0.5, 0.1875, ((1, 32),))
    return {"fields": fields, "lagged_source": lagged_source, "embed_weight": embed_weight, "position": position, "norm_gain": norm_gain, "head_weight": head_weight}


time_step = 0.25
diffusivity = 0.2
epsilon = 1e-05

def tendency(extended):
    padded = jnp.pad(extended, ((0, 0), (0, 0), (0, 0), (1, 1)))
    centre = padded[:, 1:-1, 1:-1, 1:-1]
    x_plus = padded[:, 2:, 1:-1, 1:-1]
    x_minus = padded[:, :-2, 1:-1, 1:-1]
    y_plus = padded[:, 1:-1, 2:, 1:-1]
    y_minus = padded[:, 1:-1, :-2, 1:-1]
    z_plus = padded[:, 1:-1, 1:-1, 2:]
    z_minus = padded[:, 1:-1, 1:-1, :-2]
    laplacian = x_plus + x_minus + y_plus + y_minus + z_plus + z_minus - 6.0 * centre
    advection = centre[0:1] * (x_plus - x_minus) + centre[1:2] * (y_plus - y_minus) + centre[2:3] * (z_plus - z_minus)
    return diffusivity * laplacian - 0.5 * advection

def cycle_pad(values):
    return jnp.pad(values, ((0, 0), (1, 1), (1, 1), (0, 0)))

def advance(fields, lagged_source):
    section_one = fields + time_step * tendency(cycle_pad(fields))
    averaged = 0.5 * (fields + section_one + time_step * tendency(cycle_pad(section_one)))
    source = jnp.concatenate([jnp.zeros((3,) + fields.shape[1:], jnp.float32), lagged_source.astype(jnp.float32)], 0)
    return averaged + time_step * source

def closure(fields, embed_weight, position, norm_gain, head_weight):
    cells = fields.astype(jnp.bfloat16)
    half_patch = PATCH // 2
    z_rest = NZ // ZB
    tok_dev = TOKENS // N_SEQ

    def one_block(block_index):
        zgroup = block_index // PY
        y_row = block_index % PY
        starts = (jnp.int32(0), jnp.int32(0), (y_row * PATCH).astype(jnp.int32), (zgroup * z_rest).astype(jnp.int32))
        slab_cells = lax.dynamic_slice(cells, starts, (NF, NX, PATCH, z_rest))
        slab_cells = slab_cells.reshape(NF, PX, 2, half_patch, 2, half_patch, PZL, PATCH)
        slab_cells = slab_cells.transpose(1, 6, 0, 3, 2, 4, 5, 7).reshape(PX * PZL, N_MP, GROUPS, 2, 2, half_patch, PATCH)
        patch_rows = slab_cells.transpose(0, 1, 3, 4, 2, 5, 6).reshape(tok_dev, FEAT)
        embedded = jnp.dot(patch_rows, embed_weight, preferred_element_type=jnp.float32)
        start_row = (block_index * tok_dev).astype(jnp.int32)
        position_rows = lax.dynamic_slice_in_dim(position, start_row, tok_dev, 0).astype(jnp.float32)
        hidden = embedded + position_rows
        row_mean = lax.optimization_barrier(jnp.mean(hidden, -1, keepdims=True))
        row_square = lax.optimization_barrier(jnp.mean(hidden * hidden, -1, keepdims=True))
        variance = row_square - row_mean * row_mean
        normed = ((hidden - row_mean) * lax.rsqrt(variance + epsilon) * norm_gain).astype(jnp.bfloat16)
        return jnp.dot(normed, head_weight, preferred_element_type=jnp.float32).astype(jnp.bfloat16)
    blocks = lax.map(one_block, jnp.arange(N_SEQ, dtype=jnp.int32))
    return blocks.reshape(TOKENS, OUTF)

def reference(fields, lagged_source, embed_weight, position, norm_gain, head_weight):
    fields_next = advance(fields, lagged_source)
    source_terms = closure(fields, embed_weight, position, norm_gain, head_weight)
    return (fields_next, source_terms)
```

```python
import jax
import jax.numpy as jnp
from jax import lax
from jax.experimental import pallas as pl
from jax.experimental.pallas import tpu as pltpu
from jax.sharding import Mesh
from jax.sharding import PartitionSpec as P

PATCH = 16
time_step = 0.25
diffusivity = 0.2
epsilon = 1e-05

F32 = jnp.float32
BF16 = jnp.bfloat16
ALL = ("sq", "core", "mp")


def block_transpose(tile):
    row = lax.broadcasted_iota(jnp.int32, (8, 128), 0)
    lane_block = lax.broadcasted_iota(jnp.int32, (8, 128), 1) // PATCH
    skewed = pltpu.roll(tile, 0, 1, stride=PATCH, stride_axis=0)
    source_row = (lane_block + row) & 7
    turned = jnp.take_along_axis(skewed, source_row, axis=0)
    unskewed = pltpu.roll(turned, 0, 1, stride=PATCH, stride_axis=0)
    return jnp.take_along_axis(unskewed, (8 - row) & 7, axis=0)


def pack_kernel(fields_ref, packed_ref, y_low_ref, y_high_ref):
    for half in range(2):
        for g in range(4):
            tiles = []
            for c in range(2):
                tile = fields_ref[0, half * 4 + g, :, c * 128 : (c + 1) * 128]
                tiles.append(block_transpose(tile))
            both = jnp.concatenate(tiles, axis=0)
            packed_ref[half, :, g * 128 : (g + 1) * 128] = both.astype(BF16)
    for k in range(2):
        y_low_ref[k, 0] = fields_ref[0, :, k, :].astype(BF16)
        y_high_ref[k, 0] = fields_ref[0, :, 6 + k, :].astype(BF16)


def pack(fields):
    return pl.pallas_call(
        pack_kernel,
        grid=(16,),
        in_specs=[pl.BlockSpec((1, 8, 8, 256), lambda f: (f, 0, 0, 0))],
        out_specs=[
            pl.BlockSpec((2, 16, 512), lambda f: (f, 0, 0)),
            pl.BlockSpec((2, 1, 8, 256), lambda f: (0, f, 0, 0)),
            pl.BlockSpec((2, 1, 8, 256), lambda f: (0, f, 0, 0)),
        ],
        out_shape=[
            jax.ShapeDtypeStruct((32, 16, 512), BF16),
            jax.ShapeDtypeStruct((2, 16, 8, 256), BF16),
            jax.ShapeDtypeStruct((2, 16, 8, 256), BF16),
        ],
        cost_estimate=pl.CostEstimate(flops=1000000, bytes_accessed=2 << 20, transcendentals=0),
    )(fields)


def embed_kernel(core_ref, patches_ref, weight_ref, out_ref):
    columns = weight_ref.shape[-1]
    total = jnp.zeros((256, columns), F32)
    for b in range(2):
        left = patches_ref[:, b].reshape(256, 512)
        total = total + jnp.dot(left, weight_ref[0, b], preferred_element_type=F32)
    total = total.reshape(16, 2, 2, 4, columns)
    for a in range(2):
        for c in range(2):
            out_ref[a, c] = total[:, c, a].astype(BF16)


def embed(patches, weight, core):
    steps = 4
    columns = 1024 // steps
    return pl.pallas_call(
        embed_kernel,
        grid_spec=pltpu.PrefetchScalarGridSpec(
            num_scalar_prefetch=1,
            grid=(steps,),
            in_specs=[
                pl.BlockSpec((16, 2, 16, 512), lambda n, core: (0, 0, 0, 0)),
                pl.BlockSpec((1, 2, 512, columns), lambda n, core: (core[0], 0, 0, n)),
            ],
            out_specs=pl.BlockSpec((2, 2, 16, 4, columns), lambda n, core: (0, 0, 0, 0, n)),
        ),
        out_shape=jax.ShapeDtypeStruct((2, 2, 16, 4, 1024), BF16),
        compiler_params=pltpu.CompilerParams(vmem_limit_bytes=32 << 20),
        cost_estimate=pl.CostEstimate(flops=540000000, bytes_accessed=3 << 20, transcendentals=0),
    )(core, patches, weight)


def advance_kernel(
    edge_ref, fields_ref, source_ref, yl_ref, yh_ref, xl_ref, xh_ref, cl_ref, ch_ref,
    out_ref, ylo, yhi, xlo, xhi, clo, chi, one_ref, face_ref,
):
    ylo[...] = yl_ref[...].astype(F32)
    yhi[...] = yh_ref[...].astype(F32)
    xlo[...] = xl_ref[...].astype(F32)
    xhi[...] = xh_ref[...].astype(F32)
    clo[...] = cl_ref[...].astype(F32)
    chi[...] = ch_ref[...].astype(F32)
    row = lax.broadcasted_iota(jnp.int32, (8, 256), 0)
    lane = lax.broadcasted_iota(jnp.int32, (8, 256), 1)
    first_row, last_row = row == 0, row == 7
    first_lane, last_lane = lane == 0, lane == 255

    def shifted(tile, low, high):
        before = jnp.where(first_row, low, pltpu.roll(tile, 1, 0))
        after = jnp.where(last_row, high, pltpu.roll(tile, 7, 0))
        return before, after

    def tendency(centre, velocity, xm, xp, ym, yp):
        zm = jnp.where(first_lane, 0.0, pltpu.roll(centre, 1, 1))
        zp = jnp.where(last_lane, 0.0, pltpu.roll(centre, 255, 1))
        laplacian = xp + xm + yp + ym + zp + zm - 6.0 * centre
        advection = velocity[0] * (xp - xm) + velocity[1] * (yp - ym) + velocity[2] * (zp - zm)
        return diffusivity * laplacian - 0.5 * advection

    def at8(f):
        return pl.ds(pl.multiple_of(f * 8, 8), 8)

    def first_stage(f, carry):
        mine = at8(f)
        for i in range(8):
            centre = fields_ref[f, i]
            xm = fields_ref[f, i - 1] if i > 0 else xlo[1, mine]
            xp = fields_ref[f, i + 1] if i < 7 else xhi[0, mine]
            low = ylo[1, pl.ds(f * 8 + i, 1)]
            high = yhi[0, pl.ds(f * 8 + i, 1)]
            ym, yp = shifted(centre, low, high)
            velocity = [fields_ref[k, i] for k in range(3)]
            one_ref[f, i] = centre + time_step * tendency(centre, velocity, xm, xp, ym, yp)
        for side in range(2):
            halo = xlo if side == 0 else xhi
            corner = clo if side == 0 else chi
            near = 1 if side == 0 else 0
            centre = halo[near, mine]
            outer = halo[1 - near, mine]
            inner = fields_ref[f, 0 if side == 0 else 7]
            xm, xp = (outer, inner) if side == 0 else (inner, outer)
            ym, yp = shifted(centre, corner[0, pl.ds(f, 1)], corner[1, pl.ds(f, 1)])
            velocity = [halo[near, k * 8 : k * 8 + 8] for k in range(3)]
            value = centre + time_step * tendency(centre, velocity, xm, xp, ym, yp)
            face_ref[side, mine] = value * edge_ref[side]
        for side in range(2):
            halo = ylo if side == 0 else yhi
            near = 1 if side == 0 else 0
            centre = halo[near, mine]
            outer = halo[1 - near, mine]
            inner = fields_ref[f, :, 0 if side == 0 else 7, :]
            ym, yp = (outer, inner) if side == 0 else (inner, outer)
            xm, xp = shifted(centre, clo[side, pl.ds(f, 1)], chi[side, pl.ds(f, 1)])
            velocity = [halo[near, k * 8 : k * 8 + 8] for k in range(3)]
            value = centre + time_step * tendency(centre, velocity, xm, xp, ym, yp)
            face_ref[2 + side, mine] = value * edge_ref[2 + side]
        return carry

    lax.fori_loop(0, 16, first_stage, 0)

    def second_stage(f, with_source):
        mine = at8(f)
        for i in range(8):
            centre = one_ref[f, i]
            xm = one_ref[f, i - 1] if i > 0 else face_ref[0, mine]
            xp = one_ref[f, i + 1] if i < 7 else face_ref[1, mine]
            low = face_ref[2, pl.ds(f * 8 + i, 1)]
            high = face_ref[3, pl.ds(f * 8 + i, 1)]
            ym, yp = shifted(centre, low, high)
            velocity = [one_ref[k, i] for k in range(3)]
            value = 0.5 * (fields_ref[f, i] + centre + time_step * tendency(centre, velocity, xm, xp, ym, yp))
            if with_source:
                value = value + time_step * source_ref[f - 3, i].astype(F32)
            out_ref[f, i] = value

    for f in range(3):
        second_stage(f, False)

    def species(f, carry):
        second_stage(f, True)
        return carry

    lax.fori_loop(3, 16, species, 0)


def advance(edges, fields, lagged_source, y_low, y_high, x_low, x_high, corner_low, corner_high):
    vmem = pl.BlockSpec(memory_space=pltpu.VMEM)
    return pl.pallas_call(
        advance_kernel,
        in_specs=[pl.BlockSpec(memory_space=pltpu.SMEM)] + [vmem] * 8,
        out_specs=vmem,
        out_shape=jax.ShapeDtypeStruct((16, 8, 8, 256), F32),
        scratch_shapes=[pltpu.VMEM((2, 128, 256), F32)] * 4
        + [pltpu.VMEM((2, 16, 256), F32)] * 2
        + [pltpu.VMEM((16, 8, 8, 256), F32), pltpu.VMEM((4, 128, 256), F32)],
        compiler_params=pltpu.CompilerParams(vmem_limit_bytes=32 << 20),
        cost_estimate=pl.CostEstimate(flops=100000000, bytes_accessed=4 << 20, transcendentals=0),
    )(edges, fields, lagged_source, y_low, y_high, x_low, x_high, corner_low, corner_high)


def along(value, axes, step):
    count = 1
    for axis in axes:
        count *= lax.axis_size(axis)
    pairs = [(i, i + step) for i in range(count) if 0 <= i + step < count]
    return lax.ppermute(value, axes, pairs)


def row_norm(hidden, norm_gain):
    row_mean = jnp.mean(hidden, -1, keepdims=True)
    row_square = jnp.mean(hidden * hidden, -1, keepdims=True)
    variance = row_square - row_mean * row_mean
    return ((hidden - row_mean) * lax.rsqrt(variance + epsilon) * norm_gain).astype(BF16)


def on_device(fields, lagged_source, embed_weight, position, norm_gain, head_weight):
    core = lax.axis_index("core")
    mp = lax.axis_index("mp")
    seq = lax.axis_index("sq") * 2 + core
    x_axes = ("sq", "core")

    packed, y_first, y_last = pack(fields)
    patches = lax.all_to_all(packed, "mp", 0, 0, tiled=True)

    y_low = along(y_last.reshape(2, 128, 256), ("mp",), 1)
    y_high = along(y_first.reshape(2, 128, 256), ("mp",), -1)

    weight = embed_weight.reshape(2, 2, 512, 1024)
    partial_sums = embed(
        patches.reshape(16, 2, 16, 512), weight, core.astype(jnp.int32).reshape(1)
    )
    pieces = lax.all_to_all(partial_sums.reshape(64, 4, 1024), ("core", "mp"), 0, 0, tiled=True)

    def x_edge(rows, which):
        cells = rows.astype(BF16).transpose(1, 0, 2, 3).reshape(2, 128, 256)
        corners = jnp.stack([side[k].reshape(16, 8, 256)[:, which] for side, k in ((y_low, 1), (y_high, 0))])
        return jnp.concatenate([cells.reshape(256, 256), corners.reshape(32, 256)], 0)

    (x_source, y_low, y_high, _) = lax.optimization_barrier((fields, y_low, y_high, partial_sums))
    x_low = along(x_edge(x_source[:, 6:8], 7), x_axes, 1)
    x_high = along(x_edge(x_source[:, 0:2], 0), x_axes, -1)

    edges = jnp.stack([seq > 0, seq < 31, mp > 0, mp < 31]).astype(F32)
    fields_next = advance(
        edges, fields, lagged_source, y_low, y_high,
        x_low[:256].reshape(2, 128, 256), x_high[:256].reshape(2, 128, 256),
        x_low[256:].reshape(2, 16, 256), x_high[256:].reshape(2, 16, 256),
    )

    rows = jnp.sum(pieces.astype(F32), 0)
    swap = [(s * 32 + m, m * 32 + s) for s in range(32) for m in range(32)]
    rows = lax.ppermute(rows, ALL, swap)
    own_position = lax.dynamic_slice_in_dim(position, mp * 4, 4, 0).astype(F32)
    normed = row_norm(rows + own_position, norm_gain)
    everyone = jnp.broadcast_to(normed[None], (32, 4, 1024))
    normed = lax.all_to_all(everyone, "mp", 0, 0, tiled=True).reshape(128, 1024)
    source_terms = jnp.dot(normed, head_weight, preferred_element_type=F32).astype(BF16)
    return fields_next, source_terms


def solution(mesh):
    split = Mesh(mesh.devices.reshape(16, 2, 32), ALL)
    seq = ("sq", "core")
    placed = (
        P(None, seq, "mp", None),
        P(None, seq, "mp", None),
        P("mp", None),
        P(seq, None),
        P(),
        P(None, "mp"),
    )
    return jax.shard_map(
        on_device,
        mesh=split,
        in_specs=placed,
        out_specs=(P(None, seq, "mp", None), P(seq, "mp")),
        check_vma=False,
    )
```

```python
import jax
import jax.numpy as jnp
from jax import lax
from jax.experimental import pallas as pl
from jax.experimental.pallas import tpu as pltpu
from jax.sharding import Mesh
from jax.sharding import PartitionSpec as P

PATCH = 16
time_step = 0.25
diffusivity = 0.2
epsilon = 1e-05

F32 = jnp.float32
BF16 = jnp.bfloat16
ALL = ("sq", "core", "mp")


def block_transpose(tiles):
    row = lax.broadcasted_iota(jnp.int32, (8, 128), 0)
    lane_block = lax.broadcasted_iota(jnp.int32, (8, 128), 1) // PATCH
    for s in (4, 2, 1):
        row_bit = (row // s) & 1
        keep, down = row_bit == ((lane_block // s) & 1), row_bit == 1
        after = [pltpu.roll(t, s, 0) for t in tiles]
        after = [pltpu.roll(t, 128 - PATCH * s, 1) for t in after]
        if s == 4:
            tiles = [jnp.where(keep, t, a) for t, a in zip(tiles, after)]
        else:
            before = [pltpu.roll(t, 8 - s, 0) for t in tiles]
            before = [pltpu.roll(t, PATCH * s, 1) for t in before]
            tiles = [
                jnp.where(keep, t, jnp.where(down, a, b)) for t, a, b in zip(tiles, after, before)
            ]
    return tiles


PACK_STEPS = 4


def pack_kernel(fields_hbm, packed_hbm, fields_ref, packed_ref, in_sem, out_sem):
    count = 16 // PACK_STEPS
    loads, stores = [], []
    for step in range(PACK_STEPS):
        some = pl.ds(step * count, count)
        loads.append(pltpu.make_async_copy(fields_hbm.at[some], fields_ref.at[some], in_sem.at[step]))
        some = pl.ds(step * 2 * count, 2 * count)
        stores.append(pltpu.make_async_copy(packed_ref.at[some], packed_hbm.at[some], out_sem.at[step]))
    for load in loads:
        load.start()
    for step in range(PACK_STEPS):
        loads[step].wait()
        places = [
            (step * count + k, half, g) for k in range(count) for half in range(2) for g in range(4)
        ]
        tiles = block_transpose(
            [
                fields_ref[f, half * 4 + g, :, c * 128 : (c + 1) * 128]
                for f, half, g in places
                for c in range(2)
            ]
        )
        for n, (f, half, g) in enumerate(places):
            both = jnp.concatenate(tiles[2 * n : 2 * n + 2], axis=0)
            packed_ref[f * 2 + half, :, g * 128 : (g + 1) * 128] = both.astype(BF16)
        stores[step].start()
    for store in stores:
        store.wait()


def pack(fields):
    return pl.pallas_call(
        pack_kernel,
        in_specs=[pl.BlockSpec(memory_space=pl.ANY)],
        out_specs=pl.BlockSpec(memory_space=pl.ANY),
        out_shape=jax.ShapeDtypeStruct((32, 16, 512), BF16),
        scratch_shapes=[
            pltpu.VMEM((16, 8, 8, 256), F32),
            pltpu.VMEM((32, 16, 512), BF16),
            pltpu.SemaphoreType.DMA((PACK_STEPS,)),
            pltpu.SemaphoreType.DMA((PACK_STEPS,)),
        ],
        cost_estimate=pl.CostEstimate(flops=1000000, bytes_accessed=2 << 20, transcendentals=0),
    )(fields)


VMEM = pl.BlockSpec(memory_space=pltpu.VMEM)
SMALL = pltpu.CompilerParams(vmem_limit_bytes=16 << 20)


def y_edge_kernel(fields_ref, first_ref, last_ref):
    for k in range(2):
        first_ref[k] = fields_ref[:, :, k, :].reshape(128, 256).astype(BF16)
        last_ref[k] = fields_ref[:, :, 6 + k, :].reshape(128, 256).astype(BF16)


def y_edges(fields):
    return pl.pallas_call(
        y_edge_kernel,
        in_specs=[VMEM],
        out_specs=[VMEM, VMEM],
        out_shape=[jax.ShapeDtypeStruct((2, 128, 256), BF16)] * 2,
        cost_estimate=pl.CostEstimate(flops=100000, bytes_accessed=2 << 20, transcendentals=0),
    )(fields)


def x_edge_kernel(head_ref, tail_ref, y_low_ref, y_high_ref, first_ref, last_ref, rows):
    rows[0] = y_low_ref[1].astype(F32)
    rows[1] = y_high_ref[0].astype(F32)
    for cells, out_ref, i in ((head_ref, first_ref, 0), (tail_ref, last_ref, 7)):
        for k in range(2):
            out_ref[k * 128 : (k + 1) * 128] = cells[:, k].reshape(128, 256).astype(BF16)
        for k in range(2):
            corner = rows[k].reshape(16, 8, 256)[:, i]
            out_ref[256 + k * 16 : 272 + k * 16] = corner.astype(BF16)


def x_edges(fields, y_low, y_high):
    return pl.pallas_call(
        x_edge_kernel,
        grid=(1,),
        in_specs=[
            pl.BlockSpec((16, 2, 8, 256), lambda n: (0, 0, 0, 0)),
            pl.BlockSpec((16, 2, 8, 256), lambda n: (0, 3, 0, 0)),
            pl.BlockSpec((2, 128, 256), lambda n: (0, 0, 0)),
            pl.BlockSpec((2, 128, 256), lambda n: (0, 0, 0)),
        ],
        out_specs=[pl.BlockSpec((288, 256), lambda n: (0, 0))] * 2,
        out_shape=[jax.ShapeDtypeStruct((288, 256), BF16)] * 2,
        scratch_shapes=[pltpu.VMEM((2, 128, 256), F32)],
        compiler_params=SMALL,
        cost_estimate=pl.CostEstimate(flops=100000, bytes_accessed=1 << 20, transcendentals=0),
    )(fields, fields, y_low, y_high)


def embed_kernel(patches_ref, weight_ref, out_ref):
    left = [patches_ref[:, b].reshape(256, 512) for b in range(2)]
    for n in range(4):
        columns = slice(n * 256, (n + 1) * 256)
        total = jnp.dot(left[0], weight_ref[0, :, columns], preferred_element_type=F32)
        total = total + jnp.dot(left[1], weight_ref[1, :, columns], preferred_element_type=F32)
        total = total.reshape(16, 2, 2, 4, 256)
        for a in range(2):
            for c in range(2):
                out_ref[a, c, :, :, columns] = total[:, c, a].astype(BF16)


def embed(patches, weight):
    return pl.pallas_call(
        embed_kernel,
        in_specs=[VMEM, VMEM],
        out_specs=VMEM,
        out_shape=jax.ShapeDtypeStruct((2, 2, 16, 4, 1024), BF16),
        compiler_params=SMALL,
        cost_estimate=pl.CostEstimate(flops=540000000, bytes_accessed=3 << 20, transcendentals=0),
    )(patches, weight)


def norm_kernel(place_ref, rows_ref, position_ref, gain_ref, out_ref):
    block = position_ref[...].astype(F32).reshape(4, 4, 1024)
    hidden = rows_ref[...]
    for k in range(4):
        hidden = hidden + jnp.where(place_ref[1] == k, block[k], 0.0)
    row_mean = jnp.mean(hidden, -1, keepdims=True)
    row_square = jnp.mean(hidden * hidden, -1, keepdims=True)
    variance = row_square - row_mean * row_mean
    normed = (hidden - row_mean) * lax.rsqrt(variance + epsilon) * gain_ref[...]
    out_ref[...] = jnp.broadcast_to(normed.astype(BF16)[None], (32, 4, 1024))


def norm(rows, position, norm_gain, mp):
    return pl.pallas_call(
        norm_kernel,
        grid_spec=pltpu.PrefetchScalarGridSpec(
            num_scalar_prefetch=1,
            grid=(1,),
            in_specs=[
                pl.BlockSpec((4, 1024), lambda n, place: (0, 0)),
                pl.BlockSpec((16, 1024), lambda n, place: (place[0], 0)),
                pl.BlockSpec((1, 1024), lambda n, place: (0, 0)),
            ],
            out_specs=pl.BlockSpec((32, 4, 1024), lambda n, place: (0, 0, 0)),
        ),
        out_shape=jax.ShapeDtypeStruct((32, 4, 1024), BF16),
        compiler_params=SMALL,
        cost_estimate=pl.CostEstimate(flops=100000, bytes_accessed=300000, transcendentals=0),
    )(jnp.stack([mp // 4, mp % 4]).astype(jnp.int32), rows, position, norm_gain.reshape(1, 1024))


def head_kernel(normed_ref, weight_ref, out_ref):
    left = normed_ref[...].astype(F32).reshape(128, 1024).astype(BF16)
    for start, size in ((0, 512), (512, 512), (1024, 384)):
        columns = slice(start, start + size)
        out_ref[:, columns] = jnp.dot(
            left, weight_ref[:, columns], preferred_element_type=F32
        ).astype(BF16)


def head(normed, head_weight):
    return pl.pallas_call(
        head_kernel,
        in_specs=[VMEM, VMEM],
        out_specs=VMEM,
        out_shape=jax.ShapeDtypeStruct((128, 1408), BF16),
        compiler_params=SMALL,
        cost_estimate=pl.CostEstimate(flops=370000000, bytes_accessed=4 << 20, transcendentals=0),
    )(normed, head_weight)


def advance_kernel(
    edge_ref, fields_ref, source_ref, yl_ref, yh_ref, xl_ref, xh_ref,
    out_ref, ylo, yhi, xlo, xhi, clo, chi, one_ref, face_ref,
):
    ylo[...] = yl_ref[...].astype(F32)
    yhi[...] = yh_ref[...].astype(F32)
    for payload, cells, corners in ((xl_ref, xlo, clo), (xh_ref, xhi, chi)):
        cells[...] = payload[0:256].astype(F32).reshape(2, 128, 256)
        corners[...] = payload[256:288].astype(F32).reshape(2, 16, 256)
    row = lax.broadcasted_iota(jnp.int32, (8, 256), 0)
    lane = lax.broadcasted_iota(jnp.int32, (8, 256), 1)
    first_row, last_row = row == 0, row == 7
    first_lane, last_lane = lane == 0, lane == 255

    def shifted(tile, low, high):
        before = jnp.where(first_row, low, pltpu.roll(tile, 1, 0))
        after = jnp.where(last_row, high, pltpu.roll(tile, 7, 0))
        return before, after

    def tendency(centre, velocity, xm, xp, ym, yp):
        zm = jnp.where(first_lane, 0.0, pltpu.roll(centre, 1, 1))
        zp = jnp.where(last_lane, 0.0, pltpu.roll(centre, 255, 1))
        laplacian = xp + xm + yp + ym + zp + zm - 6.0 * centre
        advection = velocity[0] * (xp - xm) + velocity[1] * (yp - ym) + velocity[2] * (zp - zm)
        return diffusivity * laplacian - 0.5 * advection

    def at8(f):
        return pl.ds(pl.multiple_of(f * 8, 8), 8)

    def first_stage(f, carry):
        mine = at8(f)
        for i in range(8):
            centre = fields_ref[f, i]
            xm = fields_ref[f, i - 1] if i > 0 else xlo[1, mine]
            xp = fields_ref[f, i + 1] if i < 7 else xhi[0, mine]
            low = ylo[1, pl.ds(f * 8 + i, 1)]
            high = yhi[0, pl.ds(f * 8 + i, 1)]
            ym, yp = shifted(centre, low, high)
            velocity = [fields_ref[k, i] for k in range(3)]
            one_ref[f, i] = centre + time_step * tendency(centre, velocity, xm, xp, ym, yp)
        for side in range(2):
            halo = xlo if side == 0 else xhi
            corner = clo if side == 0 else chi
            near = 1 if side == 0 else 0
            centre = halo[near, mine]
            outer = halo[1 - near, mine]
            inner = fields_ref[f, 0 if side == 0 else 7]
            xm, xp = (outer, inner) if side == 0 else (inner, outer)
            ym, yp = shifted(centre, corner[0, pl.ds(f, 1)], corner[1, pl.ds(f, 1)])
            velocity = [halo[near, k * 8 : k * 8 + 8] for k in range(3)]
            value = centre + time_step * tendency(centre, velocity, xm, xp, ym, yp)
            face_ref[side, mine] = value * edge_ref[side]
        for side in range(2):
            halo = ylo if side == 0 else yhi
            near = 1 if side == 0 else 0
            centre = halo[near, mine]
            outer = halo[1 - near, mine]
            inner = fields_ref[f, :, 0 if side == 0 else 7, :]
            ym, yp = (outer, inner) if side == 0 else (inner, outer)
            xm, xp = shifted(centre, clo[side, pl.ds(f, 1)], chi[side, pl.ds(f, 1)])
            velocity = [halo[near, k * 8 : k * 8 + 8] for k in range(3)]
            value = centre + time_step * tendency(centre, velocity, xm, xp, ym, yp)
            face_ref[2 + side, mine] = value * edge_ref[2 + side]
        return carry

    lax.fori_loop(0, 16, first_stage, 0)

    def second_stage(f, with_source):
        mine = at8(f)
        for i in range(8):
            centre = one_ref[f, i]
            xm = one_ref[f, i - 1] if i > 0 else face_ref[0, mine]
            xp = one_ref[f, i + 1] if i < 7 else face_ref[1, mine]
            low = face_ref[2, pl.ds(f * 8 + i, 1)]
            high = face_ref[3, pl.ds(f * 8 + i, 1)]
            ym, yp = shifted(centre, low, high)
            velocity = [one_ref[k, i] for k in range(3)]
            value = 0.5 * (fields_ref[f, i] + centre + time_step * tendency(centre, velocity, xm, xp, ym, yp))
            if with_source:
                value = value + time_step * source_ref[f - 3, i].astype(F32)
            out_ref[f, i] = value

    for f in range(3):
        second_stage(f, False)

    def species(f, carry):
        second_stage(f, True)
        return carry

    lax.fori_loop(3, 16, species, 0)


def advance(edges, fields, lagged_source, y_low, y_high, x_low, x_high):
    return pl.pallas_call(
        advance_kernel,
        in_specs=[pl.BlockSpec(memory_space=pltpu.SMEM)] + [VMEM] * 6,
        out_specs=VMEM,
        out_shape=jax.ShapeDtypeStruct((16, 8, 8, 256), F32),
        scratch_shapes=[pltpu.VMEM((2, 128, 256), F32)] * 4
        + [pltpu.VMEM((2, 16, 256), F32)] * 2
        + [pltpu.VMEM((16, 8, 8, 256), F32), pltpu.VMEM((4, 128, 256), F32)],
        compiler_params=SMALL,
        cost_estimate=pl.CostEstimate(flops=100000000, bytes_accessed=4 << 20, transcendentals=0),
    )(edges, fields, lagged_source, y_low, y_high, x_low, x_high)


def along(value, axes, step):
    count = 1
    for axis in axes:
        count *= lax.axis_size(axis)
    pairs = [(i, i + step) for i in range(count) if 0 <= i + step < count]
    return lax.ppermute(value, axes, pairs)


def on_device(fields, lagged_source, embed_weight, position, norm_gain, head_weight):
    core = lax.axis_index("core")
    mp = lax.axis_index("mp")
    seq = lax.axis_index("sq") * 2 + core
    x_axes = ("sq", "core")

    patches = lax.all_to_all(pack(fields), "mp", 0, 0, tiled=True)

    y_first, y_last = y_edges(fields)
    y_low = along(y_last, ("mp",), 1)
    y_high = along(y_first, ("mp",), -1)
    weight = lax.dynamic_slice_in_dim(embed_weight, core * 1024, 1024, 0).reshape(2, 512, 1024)
    patches, weight, y_low, y_high = lax.optimization_barrier((patches, weight, y_low, y_high))

    partial_sums = embed(patches.reshape(16, 2, 16, 512), weight)
    pieces = lax.all_to_all(partial_sums.reshape(64, 4, 1024), ("core", "mp"), 0, 0, tiled=True)

    x_first, x_last = x_edges(fields, y_low, y_high)
    x_low = along(x_last, x_axes, 1)
    x_high = along(x_first, x_axes, -1)
    pieces, x_low, x_high = lax.optimization_barrier((pieces, x_low, x_high))

    rows = jnp.sum(pieces.astype(F32), 0)
    swap = [(s * 32 + m, m * 32 + s) for s in range(32) for m in range(32)]
    rows = lax.ppermute(rows, ALL, swap)
    everyone = norm(rows, position, norm_gain, mp)
    normed = lax.all_to_all(everyone, "mp", 0, 0, tiled=True)

    edges = jnp.stack([seq > 0, seq < 31, mp > 0, mp < 31]).astype(F32)
    edges, _ = lax.optimization_barrier((edges, everyone))
    fields_next = advance(edges, fields, lagged_source, y_low, y_high, x_low, x_high)
    normed, fields_next = lax.optimization_barrier((normed, fields_next))

    return fields_next, head(normed, head_weight)


def solution(mesh):
    split = Mesh(mesh.devices.reshape(16, 2, 32), ALL)
    seq = ("sq", "core")
    placed = (
        P(None, seq, "mp", None),
        P(None, seq, "mp", None),
        P("mp", None),
        P(seq, None),
        P(),
        P(None, "mp"),
    )
    return jax.shard_map(
        on_device,
        mesh=split,
        in_specs=placed,
        out_specs=(P(None, seq, "mp", None), P(seq, "mp")),
        check_vma=False,
    )
```

```python
import jax
import jax.numpy as jnp
from jax import lax
from jax.experimental import pallas as pl
from jax.experimental.pallas import tpu as pltpu
from jax.sharding import Mesh
from jax.sharding import PartitionSpec as P

PATCH = 16
time_step = 0.25
diffusivity = 0.2
epsilon = 1e-05

F32 = jnp.float32
BF16 = jnp.bfloat16
ALL = ("sq", "core", "mp")


def block_transpose(tiles):
    row = lax.broadcasted_iota(jnp.int32, (8, 128), 0)
    lane_block = lax.broadcasted_iota(jnp.int32, (8, 128), 1) // PATCH
    for s in (4, 2, 1):
        row_bit = (row // s) & 1
        keep, down = row_bit == ((lane_block // s) & 1), row_bit == 1
        after = [pltpu.roll(t, s, 0) for t in tiles]
        after = [pltpu.roll(t, 128 - PATCH * s, 1) for t in after]
        if s == 4:
            tiles = [jnp.where(keep, t, a) for t, a in zip(tiles, after)]
        else:
            before = [pltpu.roll(t, 8 - s, 0) for t in tiles]
            before = [pltpu.roll(t, PATCH * s, 1) for t in before]
            tiles = [
                jnp.where(keep, t, jnp.where(down, a, b)) for t, a, b in zip(tiles, after, before)
            ]
    return tiles


PACK_STEPS = 4


def pack_kernel(fields_hbm, packed_hbm, fields_ref, packed_ref, in_sem, out_sem):
    count = 16 // PACK_STEPS
    loads, stores = [], []
    for step in range(PACK_STEPS):
        some = pl.ds(step * count, count)
        loads.append(pltpu.make_async_copy(fields_hbm.at[some], fields_ref.at[some], in_sem.at[step]))
        some = pl.ds(step * 2 * count, 2 * count)
        stores.append(pltpu.make_async_copy(packed_ref.at[some], packed_hbm.at[some], out_sem.at[step]))
    for load in loads:
        load.start()
    for step in range(PACK_STEPS):
        loads[step].wait()
        places = [
            (step * count + k, half, g) for k in range(count) for half in range(2) for g in range(4)
        ]
        tiles = block_transpose(
            [
                fields_ref[f, half * 4 + g, :, c * 128 : (c + 1) * 128]
                for f, half, g in places
                for c in range(2)
            ]
        )
        for n, (f, half, g) in enumerate(places):
            both = jnp.concatenate(tiles[2 * n : 2 * n + 2], axis=0)
            packed_ref[f * 2 + half, :, g * 128 : (g + 1) * 128] = both.astype(BF16)
        stores[step].start()
    for store in stores:
        store.wait()


def pack(fields):
    return pl.pallas_call(
        pack_kernel,
        in_specs=[pl.BlockSpec(memory_space=pl.ANY)],
        out_specs=pl.BlockSpec(memory_space=pl.ANY),
        out_shape=jax.ShapeDtypeStruct((32, 16, 512), BF16),
        scratch_shapes=[
            pltpu.VMEM((16, 8, 8, 256), F32),
            pltpu.VMEM((32, 16, 512), BF16),
            pltpu.SemaphoreType.DMA((PACK_STEPS,)),
            pltpu.SemaphoreType.DMA((PACK_STEPS,)),
        ],
        cost_estimate=pl.CostEstimate(flops=1000000, bytes_accessed=2 << 20, transcendentals=0),
    )(fields)


VMEM = pl.BlockSpec(memory_space=pltpu.VMEM)
SMALL = pltpu.CompilerParams(vmem_limit_bytes=16 << 20)


def y_edge_kernel(fields_ref, first_ref, last_ref):
    for k in range(2):
        first_ref[k] = fields_ref[:, :, k, :].reshape(128, 256).astype(BF16)
        last_ref[k] = fields_ref[:, :, 6 + k, :].reshape(128, 256).astype(BF16)


def y_edges(fields):
    return pl.pallas_call(
        y_edge_kernel,
        in_specs=[VMEM],
        out_specs=[VMEM, VMEM],
        out_shape=[jax.ShapeDtypeStruct((2, 128, 256), BF16)] * 2,
        cost_estimate=pl.CostEstimate(flops=100000, bytes_accessed=2 << 20, transcendentals=0),
    )(fields)


def x_edge_kernel(head_ref, tail_ref, y_low_ref, y_high_ref, first_ref, last_ref, rows):
    rows[0] = y_low_ref[1].astype(F32)
    rows[1] = y_high_ref[0].astype(F32)
    for cells, out_ref, i in ((head_ref, first_ref, 0), (tail_ref, last_ref, 7)):
        for k in range(2):
            out_ref[k * 128 : (k + 1) * 128] = cells[:, k].reshape(128, 256).astype(BF16)
        for k in range(2):
            corner = rows[k].reshape(16, 8, 256)[:, i]
            out_ref[256 + k * 16 : 272 + k * 16] = corner.astype(BF16)


def x_edges(fields, y_low, y_high):
    return pl.pallas_call(
        x_edge_kernel,
        grid=(1,),
        in_specs=[
            pl.BlockSpec((16, 2, 8, 256), lambda n: (0, 0, 0, 0)),
            pl.BlockSpec((16, 2, 8, 256), lambda n: (0, 3, 0, 0)),
            pl.BlockSpec((2, 128, 256), lambda n: (0, 0, 0)),
            pl.BlockSpec((2, 128, 256), lambda n: (0, 0, 0)),
        ],
        out_specs=[pl.BlockSpec((288, 256), lambda n: (0, 0))] * 2,
        out_shape=[jax.ShapeDtypeStruct((288, 256), BF16)] * 2,
        scratch_shapes=[pltpu.VMEM((2, 128, 256), F32)],
        compiler_params=SMALL,
        cost_estimate=pl.CostEstimate(flops=100000, bytes_accessed=1 << 20, transcendentals=0),
    )(fields, fields, y_low, y_high)


EMBED_STEPS = 4


def embed_kernel(patches_ref, weight_ref, out_hbm, out_ref, sem):
    left = [patches_ref[:, b].reshape(256, 512) for b in range(2)]
    size = 1024 // EMBED_STEPS
    stores = []
    for n in range(EMBED_STEPS):
        columns = pl.ds(n * size, size)
        total = jnp.dot(left[0], weight_ref[0, :, columns], preferred_element_type=F32)
        total = total + jnp.dot(left[1], weight_ref[1, :, columns], preferred_element_type=F32)
        total = total.reshape(16, 2, 2, 4, size)
        for a in range(2):
            for c in range(2):
                out_ref[a, c, :, :, columns] = total[:, c, a].astype(BF16)
        store = pltpu.make_async_copy(
            out_ref.at[:, :, :, :, columns], out_hbm.at[:, :, :, :, columns], sem.at[n]
        )
        store.start()
        stores.append(store)
    for store in stores:
        store.wait()


def embed(patches, weight):
    return pl.pallas_call(
        embed_kernel,
        in_specs=[VMEM, VMEM],
        out_specs=pl.BlockSpec(memory_space=pltpu.HBM),
        out_shape=pltpu.HBM((2, 2, 16, 4, 1024), BF16),
        scratch_shapes=[
            pltpu.VMEM((2, 2, 16, 4, 1024), BF16),
            pltpu.SemaphoreType.DMA((EMBED_STEPS,)),
        ],
        compiler_params=SMALL,
        cost_estimate=pl.CostEstimate(flops=540000000, bytes_accessed=3 << 20, transcendentals=0),
    )(patches, weight)


def norm_kernel(place_ref, rows_ref, position_ref, gain_ref, out_ref):
    block = position_ref[...].astype(F32).reshape(4, 4, 1024)
    hidden = rows_ref[...]
    for k in range(4):
        hidden = hidden + jnp.where(place_ref[1] == k, block[k], 0.0)
    row_mean = jnp.mean(hidden, -1, keepdims=True)
    row_square = jnp.mean(hidden * hidden, -1, keepdims=True)
    variance = row_square - row_mean * row_mean
    normed = (hidden - row_mean) * lax.rsqrt(variance + epsilon) * gain_ref[...]
    out_ref[...] = jnp.broadcast_to(normed.astype(BF16)[None], (32, 4, 1024))


def norm(rows, position, norm_gain, place):
    return pl.pallas_call(
        norm_kernel,
        grid_spec=pltpu.PrefetchScalarGridSpec(
            num_scalar_prefetch=1,
            grid=(1,),
            in_specs=[
                pl.BlockSpec((4, 1024), lambda n, place: (0, 0)),
                pl.BlockSpec((16, 1024), lambda n, place: (place[0], 0)),
                pl.BlockSpec((1, 1024), lambda n, place: (0, 0)),
            ],
            out_specs=pl.BlockSpec((32, 4, 1024), lambda n, place: (0, 0, 0)),
        ),
        out_shape=jax.ShapeDtypeStruct((32, 4, 1024), BF16),
        compiler_params=SMALL,
        cost_estimate=pl.CostEstimate(flops=100000, bytes_accessed=300000, transcendentals=0),
    )(jnp.stack([place // 4, place % 4]).astype(jnp.int32), rows, position, norm_gain.reshape(1, 1024))


HEAD_COLUMNS = ((0, 384), (384, 384), (768, 384), (1152, 256))


def head_kernel(order_ref, normed_ref, weight_hbm, out_hbm, rows_ref, weight_ref, out_ref, in_sem, out_sem):
    loads, stores = [], []
    for n, (start, size) in enumerate(HEAD_COLUMNS):
        columns = pl.ds(start, size)
        loads.append(
            pltpu.make_async_copy(weight_hbm.at[:, columns], weight_ref.at[:, columns], in_sem.at[n])
        )
        stores.append(
            pltpu.make_async_copy(out_ref.at[:, columns], out_hbm.at[:, columns], out_sem.at[n])
        )
    for load in loads:
        load.start()
    for s in range(32):
        rows_ref[4 * s : 4 * s + 4] = normed_ref[order_ref[s]].astype(F32)
    left = rows_ref[...].astype(BF16)
    for n, (start, size) in enumerate(HEAD_COLUMNS):
        columns = pl.ds(start, size)
        loads[n].wait()
        product = jnp.dot(left, weight_ref[:, columns], preferred_element_type=F32)
        out_ref[:, columns] = product.astype(BF16)
        stores[n].start()
    for store in stores:
        store.wait()


def head(order, normed, head_weight):
    count = len(HEAD_COLUMNS)
    return pl.pallas_call(
        head_kernel,
        in_specs=[pl.BlockSpec(memory_space=pltpu.SMEM), VMEM, pl.BlockSpec(memory_space=pl.ANY)],
        out_specs=pl.BlockSpec(memory_space=pl.ANY),
        out_shape=jax.ShapeDtypeStruct((128, 1408), BF16),
        scratch_shapes=[
            pltpu.VMEM((128, 1024), F32),
            pltpu.VMEM((1024, 1408), BF16),
            pltpu.VMEM((128, 1408), BF16),
            pltpu.SemaphoreType.DMA((count,)),
            pltpu.SemaphoreType.DMA((count,)),
        ],
        compiler_params=pltpu.CompilerParams(vmem_limit_bytes=62 << 20),
        cost_estimate=pl.CostEstimate(flops=370000000, bytes_accessed=4 << 20, transcendentals=0),
    )(order, normed, head_weight)


def advance_kernel(
    edge_ref, fields_ref, source_ref, yl_ref, yh_ref, xl_ref, xh_ref,
    out_ref, ylo, yhi, xlo, xhi, clo, chi, one_ref, face_ref,
):
    ylo[...] = yl_ref[...].astype(F32)
    yhi[...] = yh_ref[...].astype(F32)
    for payload, cells, corners in ((xl_ref, xlo, clo), (xh_ref, xhi, chi)):
        cells[...] = payload[0:256].astype(F32).reshape(2, 128, 256)
        corners[...] = payload[256:288].astype(F32).reshape(2, 16, 256)
    row = lax.broadcasted_iota(jnp.int32, (8, 256), 0)
    lane = lax.broadcasted_iota(jnp.int32, (8, 256), 1)
    first_row, last_row = row == 0, row == 7
    first_lane, last_lane = lane == 0, lane == 255

    def shifted(tile, low, high):
        before = jnp.where(first_row, low, pltpu.roll(tile, 1, 0))
        after = jnp.where(last_row, high, pltpu.roll(tile, 7, 0))
        return before, after

    def tendency(centre, velocity, xm, xp, ym, yp):
        zm = jnp.where(first_lane, 0.0, pltpu.roll(centre, 1, 1))
        zp = jnp.where(last_lane, 0.0, pltpu.roll(centre, 255, 1))
        laplacian = xp + xm + yp + ym + zp + zm - 6.0 * centre
        advection = velocity[0] * (xp - xm) + velocity[1] * (yp - ym) + velocity[2] * (zp - zm)
        return diffusivity * laplacian - 0.5 * advection

    def at8(f):
        return pl.ds(pl.multiple_of(f * 8, 8), 8)

    def first_stage(f, carry):
        mine = at8(f)
        for i in range(8):
            centre = fields_ref[f, i]
            xm = fields_ref[f, i - 1] if i > 0 else xlo[1, mine]
            xp = fields_ref[f, i + 1] if i < 7 else xhi[0, mine]
            low = ylo[1, pl.ds(f * 8 + i, 1)]
            high = yhi[0, pl.ds(f * 8 + i, 1)]
            ym, yp = shifted(centre, low, high)
            velocity = [fields_ref[k, i] for k in range(3)]
            one_ref[f, i] = centre + time_step * tendency(centre, velocity, xm, xp, ym, yp)
        for side in range(2):
            halo = xlo if side == 0 else xhi
            corner = clo if side == 0 else chi
            near = 1 if side == 0 else 0
            centre = halo[near, mine]
            outer = halo[1 - near, mine]
            inner = fields_ref[f, 0 if side == 0 else 7]
            xm, xp = (outer, inner) if side == 0 else (inner, outer)
            ym, yp = shifted(centre, corner[0, pl.ds(f, 1)], corner[1, pl.ds(f, 1)])
            velocity = [halo[near, k * 8 : k * 8 + 8] for k in range(3)]
            value = centre + time_step * tendency(centre, velocity, xm, xp, ym, yp)
            face_ref[side, mine] = value * edge_ref[side]
        for side in range(2):
            halo = ylo if side == 0 else yhi
            near = 1 if side == 0 else 0
            centre = halo[near, mine]
            outer = halo[1 - near, mine]
            inner = fields_ref[f, :, 0 if side == 0 else 7, :]
            ym, yp = (outer, inner) if side == 0 else (inner, outer)
            xm, xp = shifted(centre, clo[side, pl.ds(f, 1)], chi[side, pl.ds(f, 1)])
            velocity = [halo[near, k * 8 : k * 8 + 8] for k in range(3)]
            value = centre + time_step * tendency(centre, velocity, xm, xp, ym, yp)
            face_ref[2 + side, mine] = value * edge_ref[2 + side]
        return carry

    lax.fori_loop(0, 16, first_stage, 0)

    def second_stage(f, with_source):
        mine = at8(f)
        for i in range(8):
            centre = one_ref[f, i]
            xm = one_ref[f, i - 1] if i > 0 else face_ref[0, mine]
            xp = one_ref[f, i + 1] if i < 7 else face_ref[1, mine]
            low = face_ref[2, pl.ds(f * 8 + i, 1)]
            high = face_ref[3, pl.ds(f * 8 + i, 1)]
            ym, yp = shifted(centre, low, high)
            velocity = [one_ref[k, i] for k in range(3)]
            value = 0.5 * (fields_ref[f, i] + centre + time_step * tendency(centre, velocity, xm, xp, ym, yp))
            if with_source:
                value = value + time_step * source_ref[f - 3, i].astype(F32)
            out_ref[f, i] = value

    for f in range(3):
        second_stage(f, False)

    def species(f, carry):
        second_stage(f, True)
        return carry

    lax.fori_loop(3, 16, species, 0)


def advance(edges, fields, lagged_source, y_low, y_high, x_low, x_high):
    return pl.pallas_call(
        advance_kernel,
        in_specs=[pl.BlockSpec(memory_space=pltpu.SMEM)] + [VMEM] * 6,
        out_specs=VMEM,
        out_shape=jax.ShapeDtypeStruct((16, 8, 8, 256), F32),
        scratch_shapes=[pltpu.VMEM((2, 128, 256), F32)] * 4
        + [pltpu.VMEM((2, 16, 256), F32)] * 2
        + [pltpu.VMEM((16, 8, 8, 256), F32), pltpu.VMEM((4, 128, 256), F32)],
        compiler_params=SMALL,
        cost_estimate=pl.CostEstimate(flops=100000000, bytes_accessed=4 << 20, transcendentals=0),
    )(edges, fields, lagged_source, y_low, y_high, x_low, x_high)


def along(value, axes, step):
    count = 1
    for axis in axes:
        count *= lax.axis_size(axis)
    pairs = [(i, i + step) for i in range(count) if 0 <= i + step < count]
    return lax.ppermute(value, axes, pairs)


X_LANDING = ((0, 1, 3, 2), (1, 0, 3, 2), (0, 1, 2, 3), (0, 1, 3, 2))


def landing(s, m):
    return (s // 4 + 4) % 8 * 4 + X_LANDING[m % 4][s % 4]


def on_device(fields, lagged_source, embed_weight, position, norm_gain, head_weight):
    core = lax.axis_index("core")
    mp = lax.axis_index("mp")
    seq = lax.axis_index("sq") * 2 + core
    x_axes = ("sq", "core")

    patches = lax.all_to_all(pack(fields), "mp", 0, 0, tiled=True)

    y_first, y_last = y_edges(fields)
    y_low = along(y_last, ("mp",), 1)
    y_high = along(y_first, ("mp",), -1)
    weight = lax.dynamic_slice_in_dim(embed_weight, core * 1024, 1024, 0).reshape(2, 512, 1024)
    patches, weight, y_low, y_high = lax.optimization_barrier((patches, weight, y_low, y_high))

    partial_sums = embed(patches.reshape(16, 2, 16, 512), weight)
    pieces = lax.all_to_all(partial_sums.reshape(64, 4, 1024), ("core", "mp"), 0, 0, tiled=True)

    x_first, x_last = x_edges(fields, y_low, y_high)
    x_low = along(x_last, x_axes, 1)
    x_high = along(x_first, x_axes, -1)
    pieces, x_low, x_high = lax.optimization_barrier((pieces, x_low, x_high))

    rows = jnp.sum(pieces.astype(F32), 0)
    swap = [(s * 32 + m, m * 32 + landing(s, m)) for s in range(32) for m in range(32)]
    rows = lax.ppermute(rows, ALL, swap)
    held = [[0] * 32 for m in range(32)]
    for m in range(32):
        for s in range(32):
            held[m][landing(s, m)] = s
    place = jnp.array(held, jnp.int32)[seq, mp]
    order = jnp.array([[landing(s, m) for s in range(32)] for m in range(32)], jnp.int32)[seq]
    everyone = norm(rows, position, norm_gain, place)
    normed = lax.all_to_all(everyone, "mp", 0, 0, tiled=True)

    edges = jnp.stack([seq > 0, seq < 31, mp > 0, mp < 31]).astype(F32)
    edges, _ = lax.optimization_barrier((edges, everyone))
    fields_next = advance(edges, fields, lagged_source, y_low, y_high, x_low, x_high)
    normed, fields_next = lax.optimization_barrier((normed, fields_next))

    return fields_next, head(order, normed, head_weight)


def solution(mesh):
    split = Mesh(mesh.devices.reshape(16, 2, 32), ALL)
    seq = ("sq", "core")
    placed = (
        P(None, seq, "mp", None),
        P(None, seq, "mp", None),
        P("mp", None),
        P(seq, None),
        P(),
        P(None, "mp"),
    )
    return jax.shard_map(
        on_device,
        mesh=split,
        in_specs=placed,
        out_specs=(P(None, seq, "mp", None), P(seq, "mp")),
        check_vma=False,
    )
```

```python
import jax
import jax.numpy as jnp
from jax import lax
from jax.experimental import pallas as pl
from jax.experimental.pallas import tpu as pltpu
from jax.sharding import Mesh
from jax.sharding import PartitionSpec as P

PATCH = 16
time_step = 0.25
diffusivity = 0.2
epsilon = 1e-05

F32 = jnp.float32
BF16 = jnp.bfloat16
ALL = ("sq", "core", "mp")


def block_transpose(tiles):
    row = lax.broadcasted_iota(jnp.int32, (8, 128), 0)
    lane_block = lax.broadcasted_iota(jnp.int32, (8, 128), 1) // PATCH
    for s in (4, 2, 1):
        row_bit = (row // s) & 1
        keep, down = row_bit == ((lane_block // s) & 1), row_bit == 1
        after = [pltpu.roll(t, s, 0) for t in tiles]
        after = [pltpu.roll(t, 128 - PATCH * s, 1) for t in after]
        if s == 4:
            tiles = [jnp.where(keep, t, a) for t, a in zip(tiles, after)]
        else:
            before = [pltpu.roll(t, 8 - s, 0) for t in tiles]
            before = [pltpu.roll(t, PATCH * s, 1) for t in before]
            tiles = [
                jnp.where(keep, t, jnp.where(down, a, b)) for t, a, b in zip(tiles, after, before)
            ]
    return tiles


PACK_STEPS = 4


def pack_kernel(fields_hbm, packed_hbm, fields_ref, packed_ref, in_sem, out_sem):
    count = 16 // PACK_STEPS
    loads, stores = [], []
    for step in range(PACK_STEPS):
        some = pl.ds(step * count, count)
        loads.append(pltpu.make_async_copy(fields_hbm.at[some], fields_ref.at[some], in_sem.at[step]))
        some = pl.ds(step * 2 * count, 2 * count)
        stores.append(pltpu.make_async_copy(packed_ref.at[some], packed_hbm.at[some], out_sem.at[step]))
    for load in loads:
        load.start()
    for step in range(PACK_STEPS):
        loads[step].wait()
        places = [
            (step * count + k, half, g) for k in range(count) for half in range(2) for g in range(4)
        ]
        tiles = block_transpose(
            [
                fields_ref[f, half * 4 + g, :, c * 128 : (c + 1) * 128]
                for f, half, g in places
                for c in range(2)
            ]
        )
        for n, (f, half, g) in enumerate(places):
            both = jnp.concatenate(tiles[2 * n : 2 * n + 2], axis=0)
            packed_ref[f * 2 + half, :, g * 128 : (g + 1) * 128] = both.astype(BF16)
        stores[step].start()
    for store in stores:
        store.wait()


def pack(fields):
    return pl.pallas_call(
        pack_kernel,
        in_specs=[pl.BlockSpec(memory_space=pl.ANY)],
        out_specs=pl.BlockSpec(memory_space=pl.ANY),
        out_shape=jax.ShapeDtypeStruct((32, 16, 512), BF16),
        scratch_shapes=[
            pltpu.VMEM((16, 8, 8, 256), F32),
            pltpu.VMEM((32, 16, 512), BF16),
            pltpu.SemaphoreType.DMA((PACK_STEPS,)),
            pltpu.SemaphoreType.DMA((PACK_STEPS,)),
        ],
        cost_estimate=pl.CostEstimate(flops=1000000, bytes_accessed=2 << 20, transcendentals=0),
    )(fields)


VMEM = pl.BlockSpec(memory_space=pltpu.VMEM)
SMALL = pltpu.CompilerParams(vmem_limit_bytes=16 << 20)


def y_edge_kernel(fields_ref, first_ref, last_ref):
    for k in range(2):
        first_ref[k] = fields_ref[:, :, k, :].reshape(128, 256).astype(BF16)
        last_ref[k] = fields_ref[:, :, 6 + k, :].reshape(128, 256).astype(BF16)


def y_edges(fields):
    return pl.pallas_call(
        y_edge_kernel,
        in_specs=[VMEM],
        out_specs=[VMEM, VMEM],
        out_shape=[jax.ShapeDtypeStruct((2, 128, 256), BF16)] * 2,
        cost_estimate=pl.CostEstimate(flops=100000, bytes_accessed=2 << 20, transcendentals=0),
    )(fields)


def x_edge_kernel(head_ref, tail_ref, y_low_ref, y_high_ref, first_ref, last_ref, rows):
    rows[0] = y_low_ref[1].astype(F32)
    rows[1] = y_high_ref[0].astype(F32)
    for cells, out_ref, i in ((head_ref, first_ref, 0), (tail_ref, last_ref, 7)):
        for k in range(2):
            out_ref[k * 128 : (k + 1) * 128] = cells[:, k].reshape(128, 256).astype(BF16)
        for k in range(2):
            corner = rows[k].reshape(16, 8, 256)[:, i]
            out_ref[256 + k * 16 : 272 + k * 16] = corner.astype(BF16)


def x_edges(fields, y_low, y_high):
    return pl.pallas_call(
        x_edge_kernel,
        grid=(1,),
        in_specs=[
            pl.BlockSpec((16, 2, 8, 256), lambda n: (0, 0, 0, 0)),
            pl.BlockSpec((16, 2, 8, 256), lambda n: (0, 3, 0, 0)),
            pl.BlockSpec((2, 128, 256), lambda n: (0, 0, 0)),
            pl.BlockSpec((2, 128, 256), lambda n: (0, 0, 0)),
        ],
        out_specs=[pl.BlockSpec((288, 256), lambda n: (0, 0))] * 2,
        out_shape=[jax.ShapeDtypeStruct((288, 256), BF16)] * 2,
        scratch_shapes=[pltpu.VMEM((2, 128, 256), F32)],
        cost_estimate=pl.CostEstimate(flops=100000, bytes_accessed=1 << 20, transcendentals=0),
    )(fields, fields, y_low, y_high)


EMBED_STEPS = 4


def embed_kernel(
    member_ref, core_ref, patches_hbm, weight_hbm, out_hbm,
    patches_ref, weight_ref, out_ref, patch_sem, in_sem, out_sem,
):
    size = 1024 // EMBED_STEPS
    arrive = pltpu.make_async_copy(patches_hbm, patches_ref, patch_sem)
    arrive.start()
    loads = []
    for n in range(EMBED_STEPS):
        columns = pl.ds(n * size, size)
        load = pltpu.make_async_copy(
            weight_hbm.at[core_ref[0], :, :, columns], weight_ref.at[:, :, columns], in_sem.at[n]
        )
        load.start()
        loads.append(load)
    arrive.wait()
    left = [patches_ref[:, b].reshape(256, 512) for b in range(2)]
    stores = []
    for n in range(EMBED_STEPS):
        columns = pl.ds(n * size, size)
        loads[n].wait()
        total = jnp.dot(left[0], weight_ref[0, :, columns], preferred_element_type=F32)
        total = total + jnp.dot(left[1], weight_ref[1, :, columns], preferred_element_type=F32)
        total = total.reshape(16, 2, 2, 4, size).astype(BF16)
        for a in range(2):
            for c in range(2):
                for py in range(16):
                    out_ref[a, member_ref[a * 32 + c * 16 + py], :, columns] = total[py, c, a]
        store = pltpu.make_async_copy(
            out_ref.at[:, :, :, columns], out_hbm.at[:, :, :, columns], out_sem.at[n]
        )
        store.start()
        stores.append(store)
    for store in stores:
        store.wait()


def embed(member, core, patches, weight):
    smem = pl.BlockSpec(memory_space=pltpu.SMEM)
    anywhere = pl.BlockSpec(memory_space=pl.ANY)
    return pl.pallas_call(
        embed_kernel,
        in_specs=[smem, smem, anywhere, anywhere],
        out_specs=anywhere,
        out_shape=jax.ShapeDtypeStruct((2, 32, 4, 1024), BF16),
        scratch_shapes=[
            pltpu.VMEM((16, 2, 16, 512), BF16),
            pltpu.VMEM((2, 512, 1024), BF16),
            pltpu.VMEM((2, 32, 4, 1024), BF16),
            pltpu.SemaphoreType.DMA,
            pltpu.SemaphoreType.DMA((EMBED_STEPS,)),
            pltpu.SemaphoreType.DMA((EMBED_STEPS,)),
        ],
        cost_estimate=pl.CostEstimate(flops=540000000, bytes_accessed=3 << 20, transcendentals=0),
    )(member, core, patches, weight)


def norm_kernel(place_ref, rows_ref, position_ref, gain_ref, out_ref):
    block = position_ref[...].astype(F32).reshape(4, 4, 1024)
    hidden = rows_ref[...]
    for k in range(4):
        hidden = hidden + jnp.where(place_ref[1] == k, block[k], 0.0)
    row_mean = jnp.mean(hidden, -1, keepdims=True)
    row_square = jnp.mean(hidden * hidden, -1, keepdims=True)
    variance = row_square - row_mean * row_mean
    normed = (hidden - row_mean) * lax.rsqrt(variance + epsilon) * gain_ref[...]
    out_ref[...] = jnp.broadcast_to(normed.astype(BF16)[None], (32, 4, 1024))


def norm(rows, position, norm_gain, place):
    return pl.pallas_call(
        norm_kernel,
        grid_spec=pltpu.PrefetchScalarGridSpec(
            num_scalar_prefetch=1,
            grid=(1,),
            in_specs=[
                pl.BlockSpec((4, 1024), lambda n, place: (0, 0)),
                pl.BlockSpec((16, 1024), lambda n, place: (place[0], 0)),
                pl.BlockSpec((1, 1024), lambda n, place: (0, 0)),
            ],
            out_specs=pl.BlockSpec((32, 4, 1024), lambda n, place: (0, 0, 0)),
        ),
        out_shape=jax.ShapeDtypeStruct((32, 4, 1024), BF16),
        cost_estimate=pl.CostEstimate(flops=100000, bytes_accessed=300000, transcendentals=0),
    )(jnp.stack([place // 4, place % 4]).astype(jnp.int32), rows, position, norm_gain.reshape(1, 1024))


def arrange_kernel(source_ref, normed_ref, out_ref):
    gathered = normed_ref[...].astype(F32).reshape(128, 1024).astype(BF16)
    column = lax.broadcasted_iota(jnp.int32, (128, 128), 1)
    order = jnp.where(column == source_ref[...], 1.0, 0.0).astype(BF16)
    out_ref[...] = jnp.dot(order, gathered, preferred_element_type=F32).astype(BF16)


def arrange(source, normed):
    return pl.pallas_call(
        arrange_kernel,
        in_specs=[VMEM, VMEM],
        out_specs=VMEM,
        out_shape=jax.ShapeDtypeStruct((128, 1024), BF16),
        compiler_params=SMALL,
        cost_estimate=pl.CostEstimate(flops=34000000, bytes_accessed=1 << 19, transcendentals=0),
    )(source, normed)


def advance_kernel(
    edge_ref, fields_ref, source_ref, yl_ref, yh_ref, xl_ref, xh_ref,
    out_ref, ylo, yhi, xlo, xhi, clo, chi, one_ref, face_ref,
):
    ylo[...] = yl_ref[...].astype(F32)
    yhi[...] = yh_ref[...].astype(F32)
    for payload, cells, corners in ((xl_ref, xlo, clo), (xh_ref, xhi, chi)):
        cells[...] = payload[0:256].astype(F32).reshape(2, 128, 256)
        corners[...] = payload[256:288].astype(F32).reshape(2, 16, 256)
    row = lax.broadcasted_iota(jnp.int32, (8, 256), 0)
    lane = lax.broadcasted_iota(jnp.int32, (8, 256), 1)
    first_row, last_row = row == 0, row == 7
    first_lane, last_lane = lane == 0, lane == 255

    def shifted(tile, low, high):
        before = jnp.where(first_row, low, pltpu.roll(tile, 1, 0))
        after = jnp.where(last_row, high, pltpu.roll(tile, 7, 0))
        return before, after

    def tendency(centre, velocity, xm, xp, ym, yp):
        zm = jnp.where(first_lane, 0.0, pltpu.roll(centre, 1, 1))
        zp = jnp.where(last_lane, 0.0, pltpu.roll(centre, 255, 1))
        laplacian = xp + xm + yp + ym + zp + zm - 6.0 * centre
        advection = velocity[0] * (xp - xm) + velocity[1] * (yp - ym) + velocity[2] * (zp - zm)
        return diffusivity * laplacian - 0.5 * advection

    def at8(f):
        return pl.ds(pl.multiple_of(f * 8, 8), 8)

    def first_stage(f, carry):
        mine = at8(f)
        for i in range(8):
            centre = fields_ref[f, i]
            xm = fields_ref[f, i - 1] if i > 0 else xlo[1, mine]
            xp = fields_ref[f, i + 1] if i < 7 else xhi[0, mine]
            low = ylo[1, pl.ds(f * 8 + i, 1)]
            high = yhi[0, pl.ds(f * 8 + i, 1)]
            ym, yp = shifted(centre, low, high)
            velocity = [fields_ref[k, i] for k in range(3)]
            one_ref[f, i] = centre + time_step * tendency(centre, velocity, xm, xp, ym, yp)
        for side in range(2):
            halo = xlo if side == 0 else xhi
            corner = clo if side == 0 else chi
            near = 1 if side == 0 else 0
            centre = halo[near, mine]
            outer = halo[1 - near, mine]
            inner = fields_ref[f, 0 if side == 0 else 7]
            xm, xp = (outer, inner) if side == 0 else (inner, outer)
            ym, yp = shifted(centre, corner[0, pl.ds(f, 1)], corner[1, pl.ds(f, 1)])
            velocity = [halo[near, k * 8 : k * 8 + 8] for k in range(3)]
            value = centre + time_step * tendency(centre, velocity, xm, xp, ym, yp)
            face_ref[side, mine] = value * edge_ref[side]
        for side in range(2):
            halo = ylo if side == 0 else yhi
            near = 1 if side == 0 else 0
            centre = halo[near, mine]
            outer = halo[1 - near, mine]
            inner = fields_ref[f, :, 0 if side == 0 else 7, :]
            ym, yp = (outer, inner) if side == 0 else (inner, outer)
            xm, xp = shifted(centre, clo[side, pl.ds(f, 1)], chi[side, pl.ds(f, 1)])
            velocity = [halo[near, k * 8 : k * 8 + 8] for k in range(3)]
            value = centre + time_step * tendency(centre, velocity, xm, xp, ym, yp)
            face_ref[2 + side, mine] = value * edge_ref[2 + side]
        return carry

    lax.fori_loop(0, 16, first_stage, 0)

    def second_stage(f, with_source):
        mine = at8(f)
        for i in range(8):
            centre = one_ref[f, i]
            xm = one_ref[f, i - 1] if i > 0 else face_ref[0, mine]
            xp = one_ref[f, i + 1] if i < 7 else face_ref[1, mine]
            low = face_ref[2, pl.ds(f * 8 + i, 1)]
            high = face_ref[3, pl.ds(f * 8 + i, 1)]
            ym, yp = shifted(centre, low, high)
            velocity = [one_ref[k, i] for k in range(3)]
            value = 0.5 * (fields_ref[f, i] + centre + time_step * tendency(centre, velocity, xm, xp, ym, yp))
            if with_source:
                value = value + time_step * source_ref[f - 3, i].astype(F32)
            out_ref[f, i] = value

    for f in range(3):
        second_stage(f, False)

    def species(f, carry):
        second_stage(f, True)
        return carry

    lax.fori_loop(3, 16, species, 0)


def advance(edges, fields, lagged_source, y_low, y_high, x_low, x_high):
    return pl.pallas_call(
        advance_kernel,
        in_specs=[pl.BlockSpec(memory_space=pltpu.SMEM)] + [VMEM] * 6,
        out_specs=VMEM,
        out_shape=jax.ShapeDtypeStruct((16, 8, 8, 256), F32),
        scratch_shapes=[pltpu.VMEM((2, 128, 256), F32)] * 4
        + [pltpu.VMEM((2, 16, 256), F32)] * 2
        + [pltpu.VMEM((16, 8, 8, 256), F32), pltpu.VMEM((4, 128, 256), F32)],
        cost_estimate=pl.CostEstimate(flops=100000000, bytes_accessed=4 << 20, transcendentals=0),
    )(edges, fields, lagged_source, y_low, y_high, x_low, x_high)


def along(value, axes, step):
    count = 1
    for axis in axes:
        count *= lax.axis_size(axis)
    pairs = [(i, i + step) for i in range(count) if 0 <= i + step < count]
    return lax.ppermute(value, axes, pairs)


def route(s, t):
    z = (t // 4 - s // 4) % 8
    differ = (s ^ t) & 1
    if ((s ^ t) >> 1) & 1:
        return z * 4 + 3 * differ, z * 4 + 3 - 3 * differ
    return z * 4 + 1 + differ, z * 4 + 1 + differ


ROUTES = [[route(s, t) for t in range(32)] for s in range(32)]
SWAP = [(s * 32 + ROUTES[s][t][0], t * 32 + ROUTES[s][t][1]) for s in range(32) for t in range(32)]
MEMBER = [[ROUTES[2 * p + a][t][0] for a in range(2) for t in range(32)] for p in range(16)]
SOURCE = [[ROUTES[s][t][1] * 4 + k for s in range(32) for k in range(4)] for t in range(32)]
PLACE = [sorted(range(32), key=lambda s: ROUTES[s][t][1]) for t in range(32)]


def on_device(fields, lagged_source, embed_weight, position, norm_gain, head_weight):
    core = lax.axis_index("core")
    mp = lax.axis_index("mp")
    seq = lax.axis_index("sq") * 2 + core
    x_axes = ("sq", "core")

    patches = lax.all_to_all(pack(fields), "mp", 0, 0, tiled=True)

    y_first, y_last = y_edges(fields)
    y_low = along(y_last, ("mp",), 1)
    y_high = along(y_first, ("mp",), -1)
    member = jnp.array(MEMBER, jnp.int32)[lax.axis_index("sq")]
    patches, member, y_low, y_high = lax.optimization_barrier((patches, member, y_low, y_high))

    weight = embed_weight.reshape(2, 2, 512, 1024)
    patches = patches.reshape(16, 2, 16, 512)
    partial_sums = embed(member, core.astype(jnp.int32).reshape(1), patches, weight)
    pieces = lax.all_to_all(partial_sums.reshape(64, 4, 1024), ("core", "mp"), 0, 0, tiled=True)

    x_first, x_last = x_edges(fields, y_low, y_high)
    x_low = along(x_last, x_axes, 1)
    x_high = along(x_first, x_axes, -1)
    source = jnp.array(SOURCE, jnp.int32)[seq].reshape(128, 1)
    place = jnp.array(PLACE, jnp.int32)[seq, mp]
    pieces, x_low, x_high, source, place = lax.optimization_barrier(
        (pieces, x_low, x_high, source, place)
    )

    rows = jnp.sum(pieces.astype(F32), 0)
    rows = lax.ppermute(rows, ALL, SWAP)
    everyone = norm(rows, position, norm_gain, place)
    normed = lax.all_to_all(everyone, "mp", 0, 0, tiled=True)

    edges = jnp.stack([seq > 0, seq < 31, mp > 0, mp < 31]).astype(F32)
    edges, _ = lax.optimization_barrier((edges, everyone))
    fields_next = advance(edges, fields, lagged_source, y_low, y_high, x_low, x_high)
    normed, fields_next = lax.optimization_barrier((normed, fields_next))

    left = arrange(source, normed)
    source_terms = jnp.dot(left, head_weight, preferred_element_type=F32).astype(BF16)
    return fields_next, source_terms


def solution(mesh):
    split = Mesh(mesh.devices.reshape(16, 2, 32), ALL)
    seq = ("sq", "core")
    placed = (
        P(None, seq, "mp", None),
        P(None, seq, "mp", None),
        P("mp", None),
        P(seq, None),
        P(),
        P(None, "mp"),
    )
    return jax.shard_map(
        on_device,
        mesh=split,
        in_specs=placed,
        out_specs=(P(None, seq, "mp", None), P(seq, "mp")),
        check_vma=False,
    )
```

```python
import jax
import jax.numpy as jnp
from jax import lax
from jax.experimental import pallas as pl
from jax.experimental.pallas import tpu as pltpu
from jax.sharding import Mesh
from jax.sharding import PartitionSpec as P

PATCH = 16
time_step = 0.25
diffusivity = 0.2
epsilon = 1e-05

F32 = jnp.float32
BF16 = jnp.bfloat16
ALL = ("sq", "core", "mp")


def block_transpose(tiles):
    row = lax.broadcasted_iota(jnp.int32, (8, 128), 0)
    lane_block = lax.broadcasted_iota(jnp.int32, (8, 128), 1) // PATCH
    for s in (4, 2, 1):
        row_bit = (row // s) & 1
        keep, down = row_bit == ((lane_block // s) & 1), row_bit == 1
        after = [pltpu.roll(t, s, 0) for t in tiles]
        after = [pltpu.roll(t, 128 - PATCH * s, 1) for t in after]
        if s == 4:
            tiles = [jnp.where(keep, t, a) for t, a in zip(tiles, after)]
        else:
            before = [pltpu.roll(t, 8 - s, 0) for t in tiles]
            before = [pltpu.roll(t, PATCH * s, 1) for t in before]
            tiles = [
                jnp.where(keep, t, jnp.where(down, a, b)) for t, a, b in zip(tiles, after, before)
            ]
    return tiles


PACK_STEPS = 4


def pack_kernel(fields_hbm, packed_hbm, fields_ref, packed_ref, in_sem, out_sem):
    count = 16 // PACK_STEPS
    loads, stores = [], []
    for step in range(PACK_STEPS):
        some = pl.ds(step * count, count)
        loads.append(pltpu.make_async_copy(fields_hbm.at[some], fields_ref.at[some], in_sem.at[step]))
        some = pl.ds(step * 2 * count, 2 * count)
        stores.append(pltpu.make_async_copy(packed_ref.at[some], packed_hbm.at[some], out_sem.at[step]))
    for load in loads:
        load.start()
    for step in range(PACK_STEPS):
        loads[step].wait()
        places = [
            (step * count + k, half, g) for k in range(count) for half in range(2) for g in range(4)
        ]
        tiles = block_transpose(
            [
                fields_ref[f, half * 4 + g, :, c * 128 : (c + 1) * 128]
                for f, half, g in places
                for c in range(2)
            ]
        )
        for n, (f, half, g) in enumerate(places):
            both = jnp.concatenate(tiles[2 * n : 2 * n + 2], axis=0)
            packed_ref[f * 2 + half, :, g * 128 : (g + 1) * 128] = both.astype(BF16)
        stores[step].start()
    for store in stores:
        store.wait()


def pack(fields):
    return pl.pallas_call(
        pack_kernel,
        in_specs=[pl.BlockSpec(memory_space=pl.ANY)],
        out_specs=pl.BlockSpec(memory_space=pl.ANY),
        out_shape=jax.ShapeDtypeStruct((32, 16, 512), BF16),
        scratch_shapes=[
            pltpu.VMEM((16, 8, 8, 256), F32),
            pltpu.VMEM((32, 16, 512), BF16),
            pltpu.SemaphoreType.DMA((PACK_STEPS,)),
            pltpu.SemaphoreType.DMA((PACK_STEPS,)),
        ],
        cost_estimate=pl.CostEstimate(flops=1000000, bytes_accessed=2 << 20, transcendentals=0),
    )(fields)


VMEM = pl.BlockSpec(memory_space=pltpu.VMEM)
ROOM = pltpu.CompilerParams(vmem_limit_bytes=16 << 20)


def y_edge_kernel(fields_ref, first_ref, last_ref):
    for k in range(2):
        first_ref[k] = fields_ref[:, :, k, :].reshape(128, 256).astype(BF16)
        last_ref[k] = fields_ref[:, :, 6 + k, :].reshape(128, 256).astype(BF16)


def y_edges(fields):
    return pl.pallas_call(
        y_edge_kernel,
        in_specs=[VMEM],
        out_specs=[VMEM, VMEM],
        out_shape=[jax.ShapeDtypeStruct((2, 128, 256), BF16)] * 2,
        cost_estimate=pl.CostEstimate(flops=100000, bytes_accessed=2 << 20, transcendentals=0),
    )(fields)


def x_edge_kernel(head_ref, tail_ref, y_low_ref, y_high_ref, first_ref, last_ref, rows):
    rows[0] = y_low_ref[1].astype(F32)
    rows[1] = y_high_ref[0].astype(F32)
    for cells, out_ref, i in ((head_ref, first_ref, 0), (tail_ref, last_ref, 7)):
        for k in range(2):
            out_ref[k * 128 : (k + 1) * 128] = cells[:, k].reshape(128, 256).astype(BF16)
        for k in range(2):
            corner = rows[k].reshape(16, 8, 256)[:, i]
            out_ref[256 + k * 16 : 272 + k * 16] = corner.astype(BF16)


def x_edges(fields, y_low, y_high):
    return pl.pallas_call(
        x_edge_kernel,
        grid=(1,),
        in_specs=[
            pl.BlockSpec((16, 2, 8, 256), lambda n: (0, 0, 0, 0)),
            pl.BlockSpec((16, 2, 8, 256), lambda n: (0, 3, 0, 0)),
            pl.BlockSpec((2, 128, 256), lambda n: (0, 0, 0)),
            pl.BlockSpec((2, 128, 256), lambda n: (0, 0, 0)),
        ],
        out_specs=[pl.BlockSpec((288, 256), lambda n: (0, 0))] * 2,
        out_shape=[jax.ShapeDtypeStruct((288, 256), BF16)] * 2,
        scratch_shapes=[pltpu.VMEM((2, 128, 256), F32)],
        cost_estimate=pl.CostEstimate(flops=100000, bytes_accessed=1 << 20, transcendentals=0),
    )(fields, fields, y_low, y_high)


def route(s, t):
    z = ((t >> 2) - (s >> 2)) & 7
    differ = (s ^ t) & 1
    cross = ((s ^ t) >> 1) & 1
    near = 1 + differ
    m = z * 4 + near + cross * (2 * differ - 1)
    mu = z * 4 + near + cross * (2 - 4 * differ)
    return m, mu


def arrived_from(t, mu):
    y = ((t >> 2) - (mu >> 2)) & 7
    cross = 1 - ((mu ^ (mu >> 1)) & 1)
    differ = (mu & 1) ^ 1
    return y * 4 + (((t >> 1) ^ cross) & 1) * 2 + ((t ^ differ) & 1)


def embed_kernel(
    who_ref, patches_ref, weight_hbm, out_hbm, weight_ref, total_ref, out_ref, in_sem, out_sem
):
    seq = who_ref[0]
    loads = []
    for b in range(2):
        load = pltpu.make_async_copy(weight_hbm.at[seq & 1, b], weight_ref.at[b], in_sem.at[b])
        load.start()
        loads.append(load)
    size = 256
    left = patches_ref[:, 0].reshape(256, 512)
    loads[0].wait()
    for n in range(4):
        columns = pl.ds(n * size, size)
        total_ref[:, columns] = jnp.dot(
            left, weight_ref[0, :, columns], preferred_element_type=F32
        )
    left = patches_ref[:, 1].reshape(256, 512)
    loads[1].wait()
    stores = []
    for n in range(4):
        columns = pl.ds(n * size, size)
        product = jnp.dot(left, weight_ref[1, :, columns], preferred_element_type=F32)
        total = (total_ref[:, columns] + product).reshape(16, 2, 2, 4, size)
        for a in range(2):
            for t in range(32):
                member, _ = route((seq & 30) + a, t)
                out_ref[a, member, :, columns] = total[t % 16, t // 16, a].astype(BF16)
        store = pltpu.make_async_copy(
            out_ref.at[:, :, :, columns], out_hbm.at[:, :, :, columns], out_sem.at[n]
        )
        store.start()
        stores.append(store)
    for store in stores:
        store.wait()


def embed(who, patches, weight):
    anywhere = pl.BlockSpec(memory_space=pl.ANY)
    return pl.pallas_call(
        embed_kernel,
        in_specs=[pl.BlockSpec(memory_space=pltpu.SMEM), VMEM, anywhere],
        out_specs=anywhere,
        out_shape=pltpu.HBM((2, 32, 4, 1024), BF16),
        scratch_shapes=[
            pltpu.VMEM((2, 512, 1024), BF16),
            pltpu.VMEM((256, 1024), F32),
            pltpu.VMEM((2, 32, 4, 1024), BF16),
            pltpu.SemaphoreType.DMA((2,)),
            pltpu.SemaphoreType.DMA((4,)),
        ],
        compiler_params=pltpu.CompilerParams(vmem_limit_bytes=58 << 20),
        cost_estimate=pl.CostEstimate(flops=540000000, bytes_accessed=3 << 20, transcendentals=0),
    )(who, patches, weight)


def norm_kernel(who_ref, rows_ref, position_ref, gain_ref, out_ref):
    part = arrived_from(who_ref[0], who_ref[1]) & 3
    block = position_ref[...].astype(F32).reshape(4, 4, 1024)
    hidden = rows_ref[...]
    for k in range(4):
        hidden = hidden + jnp.where(part == k, block[k], 0.0)
    row_mean = jnp.mean(hidden, -1, keepdims=True)
    row_square = jnp.mean(hidden * hidden, -1, keepdims=True)
    variance = row_square - row_mean * row_mean
    normed = (hidden - row_mean) * lax.rsqrt(variance + epsilon) * gain_ref[...]
    out_ref[...] = jnp.broadcast_to(normed.astype(BF16)[None], (32, 4, 1024))


def norm(who, rows, position, norm_gain):
    return pl.pallas_call(
        norm_kernel,
        grid_spec=pltpu.PrefetchScalarGridSpec(
            num_scalar_prefetch=1,
            grid=(1,),
            in_specs=[
                pl.BlockSpec((4, 1024), lambda n, who: (0, 0)),
                pl.BlockSpec((16, 1024), lambda n, who: (arrived_from(who[0], who[1]) >> 2, 0)),
                pl.BlockSpec((1, 1024), lambda n, who: (0, 0)),
            ],
            out_specs=pl.BlockSpec((32, 4, 1024), lambda n, who: (0, 0, 0)),
        ),
        out_shape=jax.ShapeDtypeStruct((32, 4, 1024), BF16),
        compiler_params=ROOM,
        cost_estimate=pl.CostEstimate(flops=100000, bytes_accessed=300000, transcendentals=0),
    )(who, rows, position, norm_gain.reshape(1, 1024))


def arrange_kernel(who_ref, normed_ref, out_ref):
    gathered = normed_ref[...].astype(F32).reshape(128, 1024).astype(BF16)
    row = lax.broadcasted_iota(jnp.int32, (128, 128), 0)
    column = lax.broadcasted_iota(jnp.int32, (128, 128), 1)
    _, mu = route(row >> 2, who_ref[0])
    order = jnp.where(column == mu * 4 + (row & 3), 1.0, 0.0).astype(BF16)
    out_ref[...] = jnp.dot(order, gathered, preferred_element_type=F32).astype(BF16)


def arrange(who, normed):
    return pl.pallas_call(
        arrange_kernel,
        in_specs=[pl.BlockSpec(memory_space=pltpu.SMEM), VMEM],
        out_specs=VMEM,
        out_shape=jax.ShapeDtypeStruct((128, 1024), BF16),
        compiler_params=ROOM,
        cost_estimate=pl.CostEstimate(flops=34000000, bytes_accessed=1 << 19, transcendentals=0),
    )(who, normed)


def advance_kernel(
    edge_ref, fields_ref, source_ref, yl_ref, yh_ref, xl_ref, xh_ref,
    out_ref, ylo, yhi, xlo, xhi, clo, chi, one_ref, face_ref,
):
    ylo[...] = yl_ref[...].astype(F32)
    yhi[...] = yh_ref[...].astype(F32)
    for payload, cells, corners in ((xl_ref, xlo, clo), (xh_ref, xhi, chi)):
        cells[...] = payload[0:256].astype(F32).reshape(2, 128, 256)
        corners[...] = payload[256:288].astype(F32).reshape(2, 16, 256)
    row = lax.broadcasted_iota(jnp.int32, (8, 256), 0)
    lane = lax.broadcasted_iota(jnp.int32, (8, 256), 1)
    first_row, last_row = row == 0, row == 7
    first_lane, last_lane = lane == 0, lane == 255

    def shifted(tile, low, high):
        before = jnp.where(first_row, low, pltpu.roll(tile, 1, 0))
        after = jnp.where(last_row, high, pltpu.roll(tile, 7, 0))
        return before, after

    def tendency(centre, velocity, xm, xp, ym, yp):
        zm = jnp.where(first_lane, 0.0, pltpu.roll(centre, 1, 1))
        zp = jnp.where(last_lane, 0.0, pltpu.roll(centre, 255, 1))
        laplacian = xp + xm + yp + ym + zp + zm - 6.0 * centre
        advection = velocity[0] * (xp - xm) + velocity[1] * (yp - ym) + velocity[2] * (zp - zm)
        return diffusivity * laplacian - 0.5 * advection

    def at8(f):
        return pl.ds(pl.multiple_of(f * 8, 8), 8)

    def first_stage(f, carry):
        mine = at8(f)
        for i in range(8):
            centre = fields_ref[f, i]
            xm = fields_ref[f, i - 1] if i > 0 else xlo[1, mine]
            xp = fields_ref[f, i + 1] if i < 7 else xhi[0, mine]
            low = ylo[1, pl.ds(f * 8 + i, 1)]
            high = yhi[0, pl.ds(f * 8 + i, 1)]
            ym, yp = shifted(centre, low, high)
            velocity = [fields_ref[k, i] for k in range(3)]
            one_ref[f, i] = centre + time_step * tendency(centre, velocity, xm, xp, ym, yp)
        for side in range(2):
            halo = xlo if side == 0 else xhi
            corner = clo if side == 0 else chi
            near = 1 if side == 0 else 0
            centre = halo[near, mine]
            outer = halo[1 - near, mine]
            inner = fields_ref[f, 0 if side == 0 else 7]
            xm, xp = (outer, inner) if side == 0 else (inner, outer)
            ym, yp = shifted(centre, corner[0, pl.ds(f, 1)], corner[1, pl.ds(f, 1)])
            velocity = [halo[near, k * 8 : k * 8 + 8] for k in range(3)]
            value = centre + time_step * tendency(centre, velocity, xm, xp, ym, yp)
            face_ref[side, mine] = value * edge_ref[side]
        for side in range(2):
            halo = ylo if side == 0 else yhi
            near = 1 if side == 0 else 0
            centre = halo[near, mine]
            outer = halo[1 - near, mine]
            inner = fields_ref[f, :, 0 if side == 0 else 7, :]
            ym, yp = (outer, inner) if side == 0 else (inner, outer)
            xm, xp = shifted(centre, clo[side, pl.ds(f, 1)], chi[side, pl.ds(f, 1)])
            velocity = [halo[near, k * 8 : k * 8 + 8] for k in range(3)]
            value = centre + time_step * tendency(centre, velocity, xm, xp, ym, yp)
            face_ref[2 + side, mine] = value * edge_ref[2 + side]
        return carry

    lax.fori_loop(0, 16, first_stage, 0)

    def second_stage(f, with_source):
        mine = at8(f)
        for i in range(8):
            centre = one_ref[f, i]
            xm = one_ref[f, i - 1] if i > 0 else face_ref[0, mine]
            xp = one_ref[f, i + 1] if i < 7 else face_ref[1, mine]
            low = face_ref[2, pl.ds(f * 8 + i, 1)]
            high = face_ref[3, pl.ds(f * 8 + i, 1)]
            ym, yp = shifted(centre, low, high)
            velocity = [one_ref[k, i] for k in range(3)]
            value = 0.5 * (fields_ref[f, i] + centre + time_step * tendency(centre, velocity, xm, xp, ym, yp))
            if with_source:
                value = value + time_step * source_ref[f - 3, i].astype(F32)
            out_ref[f, i] = value

    for f in range(3):
        second_stage(f, False)

    def species(f, carry):
        second_stage(f, True)
        return carry

    lax.fori_loop(3, 16, species, 0)


def advance(edges, fields, lagged_source, y_low, y_high, x_low, x_high):
    return pl.pallas_call(
        advance_kernel,
        in_specs=[pl.BlockSpec(memory_space=pltpu.SMEM)] + [VMEM] * 6,
        out_specs=VMEM,
        out_shape=jax.ShapeDtypeStruct((16, 8, 8, 256), F32),
        scratch_shapes=[pltpu.VMEM((2, 128, 256), F32)] * 4
        + [pltpu.VMEM((2, 16, 256), F32)] * 2
        + [pltpu.VMEM((16, 8, 8, 256), F32), pltpu.VMEM((4, 128, 256), F32)],
        cost_estimate=pl.CostEstimate(flops=100000000, bytes_accessed=4 << 20, transcendentals=0),
    )(edges, fields, lagged_source, y_low, y_high, x_low, x_high)


def along(value, axes, step):
    count = 1
    for axis in axes:
        count *= lax.axis_size(axis)
    pairs = [(i, i + step) for i in range(count) if 0 <= i + step < count]
    return lax.ppermute(value, axes, pairs)


SWAP = [
    (s * 32 + route(s, t)[0], t * 32 + route(s, t)[1]) for s in range(32) for t in range(32)
]


def on_device(fields, lagged_source, embed_weight, position, norm_gain, head_weight):
    core = lax.axis_index("core")
    mp = lax.axis_index("mp")
    seq = lax.axis_index("sq") * 2 + core
    x_axes = ("sq", "core")

    patches = lax.all_to_all(pack(fields), "mp", 0, 0, tiled=True)

    y_first, y_last = y_edges(fields)
    y_low = along(y_last, ("mp",), 1)
    y_high = along(y_first, ("mp",), -1)
    who = jnp.stack([seq, mp]).astype(jnp.int32)
    edges = jnp.stack([seq > 0, seq < 31, mp > 0, mp < 31]).astype(F32)
    patches, who, edges, y_low, y_high = lax.optimization_barrier(
        (patches, who, edges, y_low, y_high)
    )

    weight = embed_weight.reshape(2, 2, 512, 1024)
    patches = patches.reshape(16, 2, 16, 512)
    partial_sums = embed(who, patches, weight)
    pieces = lax.all_to_all(partial_sums.reshape(64, 4, 1024), ("core", "mp"), 0, 0, tiled=True)

    x_first, x_last = x_edges(fields, y_low, y_high)
    x_low = along(x_last, x_axes, 1)
    x_high = along(x_first, x_axes, -1)
    pieces, x_low, x_high = lax.optimization_barrier((pieces, x_low, x_high))

    rows = jnp.sum(pieces.astype(F32), 0)
    rows = lax.ppermute(rows, ALL, SWAP)
    everyone = norm(who, rows, position, norm_gain)
    normed = lax.all_to_all(everyone, "mp", 0, 0, tiled=True)

    edges, _ = lax.optimization_barrier((edges, everyone))
    fields_next = advance(edges, fields, lagged_source, y_low, y_high, x_low, x_high)
    normed, fields_next = lax.optimization_barrier((normed, fields_next))

    left = arrange(who, normed)
    source_terms = jnp.dot(left, head_weight, preferred_element_type=F32).astype(BF16)
    return fields_next, source_terms


def solution(mesh):
    split = Mesh(mesh.devices.reshape(16, 2, 32), ALL)
    seq = ("sq", "core")
    placed = (
        P(None, seq, "mp", None),
        P(None, seq, "mp", None),
        P("mp", None),
        P(seq, None),
        P(),
        P(None, "mp"),
    )
    return jax.shard_map(
        on_device,
        mesh=split,
        in_specs=placed,
        out_specs=(P(None, seq, "mp", None), P(seq, "mp")),
        check_vma=False,
    )
```

```python
import jax
import jax.numpy as jnp
from jax import lax
from jax.experimental import pallas as pl
from jax.experimental.pallas import tpu as pltpu
from jax.sharding import Mesh
from jax.sharding import PartitionSpec as P

PATCH = 16
time_step = 0.25
diffusivity = 0.2
epsilon = 1e-05

F32 = jnp.float32
BF16 = jnp.bfloat16
ALL = ("sq", "core", "mp")


def block_transpose(tiles):
    row = lax.broadcasted_iota(jnp.int32, (8, 128), 0)
    lane_block = lax.broadcasted_iota(jnp.int32, (8, 128), 1) // PATCH
    for s in (4, 2, 1):
        row_bit = (row // s) & 1
        keep, down = row_bit == ((lane_block // s) & 1), row_bit == 1
        after = [pltpu.roll(t, s, 0) for t in tiles]
        after = [pltpu.roll(t, 128 - PATCH * s, 1) for t in after]
        if s == 4:
            tiles = [jnp.where(keep, t, a) for t, a in zip(tiles, after)]
        else:
            before = [pltpu.roll(t, 8 - s, 0) for t in tiles]
            before = [pltpu.roll(t, PATCH * s, 1) for t in before]
            tiles = [
                jnp.where(keep, t, jnp.where(down, a, b)) for t, a, b in zip(tiles, after, before)
            ]
    return tiles


PACK_STEPS = 4


def pack_kernel(fields_hbm, packed_hbm, fields_ref, packed_ref, in_sem, out_sem):
    count = 16 // PACK_STEPS
    loads, stores = [], []
    for step in range(PACK_STEPS):
        some = pl.ds(step * count, count)
        loads.append(pltpu.make_async_copy(fields_hbm.at[some], fields_ref.at[some], in_sem.at[step]))
        some = pl.ds(step * 2 * count, 2 * count)
        stores.append(pltpu.make_async_copy(packed_ref.at[some], packed_hbm.at[some], out_sem.at[step]))
    for load in loads:
        load.start()
    for step in range(PACK_STEPS):
        loads[step].wait()
        places = [
            (step * count + k, half, g) for k in range(count) for half in range(2) for g in range(4)
        ]
        tiles = block_transpose(
            [
                fields_ref[f, half * 4 + g, :, c * 128 : (c + 1) * 128]
                for f, half, g in places
                for c in range(2)
            ]
        )
        for n, (f, half, g) in enumerate(places):
            both = jnp.concatenate(tiles[2 * n : 2 * n + 2], axis=0)
            packed_ref[f * 2 + half, :, g * 128 : (g + 1) * 128] = both.astype(BF16)
        stores[step].start()
    for store in stores:
        store.wait()


def pack(fields):
    return pl.pallas_call(
        pack_kernel,
        in_specs=[pl.BlockSpec(memory_space=pl.ANY)],
        out_specs=pl.BlockSpec(memory_space=pl.ANY),
        out_shape=jax.ShapeDtypeStruct((32, 16, 512), BF16),
        scratch_shapes=[
            pltpu.VMEM((16, 8, 8, 256), F32),
            pltpu.VMEM((32, 16, 512), BF16),
            pltpu.SemaphoreType.DMA((PACK_STEPS,)),
            pltpu.SemaphoreType.DMA((PACK_STEPS,)),
        ],
        cost_estimate=pl.CostEstimate(flops=1000000, bytes_accessed=2 << 20, transcendentals=0),
    )(fields)


VMEM = pl.BlockSpec(memory_space=pltpu.VMEM)
ROOM = pltpu.CompilerParams(vmem_limit_bytes=16 << 20)


def y_edge_kernel(fields_ref, first_ref, last_ref):
    for k in range(2):
        first_ref[k] = fields_ref[:, :, k, :].reshape(128, 256).astype(BF16)
        last_ref[k] = fields_ref[:, :, 6 + k, :].reshape(128, 256).astype(BF16)


def y_edges(fields):
    return pl.pallas_call(
        y_edge_kernel,
        in_specs=[VMEM],
        out_specs=[VMEM, VMEM],
        out_shape=[jax.ShapeDtypeStruct((2, 128, 256), BF16)] * 2,
        cost_estimate=pl.CostEstimate(flops=100000, bytes_accessed=2 << 20, transcendentals=0),
    )(fields)


def x_edge_kernel(head_ref, tail_ref, y_low_ref, y_high_ref, first_ref, last_ref, rows):
    rows[0] = y_low_ref[1].astype(F32)
    rows[1] = y_high_ref[0].astype(F32)
    for cells, out_ref, i in ((head_ref, first_ref, 0), (tail_ref, last_ref, 7)):
        for k in range(2):
            out_ref[k * 128 : (k + 1) * 128] = cells[:, k].reshape(128, 256).astype(BF16)
        for k in range(2):
            corner = rows[k].reshape(16, 8, 256)[:, i]
            out_ref[256 + k * 16 : 272 + k * 16] = corner.astype(BF16)


def x_edges(fields, y_low, y_high):
    return pl.pallas_call(
        x_edge_kernel,
        grid=(1,),
        in_specs=[
            pl.BlockSpec((16, 2, 8, 256), lambda n: (0, 0, 0, 0)),
            pl.BlockSpec((16, 2, 8, 256), lambda n: (0, 3, 0, 0)),
            pl.BlockSpec((2, 128, 256), lambda n: (0, 0, 0)),
            pl.BlockSpec((2, 128, 256), lambda n: (0, 0, 0)),
        ],
        out_specs=[pl.BlockSpec((288, 256), lambda n: (0, 0))] * 2,
        out_shape=[jax.ShapeDtypeStruct((288, 256), BF16)] * 2,
        scratch_shapes=[pltpu.VMEM((2, 128, 256), F32)],
        cost_estimate=pl.CostEstimate(flops=100000, bytes_accessed=1 << 20, transcendentals=0),
    )(fields, fields, y_low, y_high)


def route(s, t):
    z = ((t >> 2) - (s >> 2)) & 7
    differ = (s ^ t) & 1
    cross = ((s ^ t) >> 1) & 1
    near = 1 + differ
    m = z * 4 + near + cross * (2 * differ - 1)
    mu = z * 4 + near + cross * (2 - 4 * differ)
    return m, mu


def arrived_from(t, mu):
    y = ((t >> 2) - (mu >> 2)) & 7
    cross = 1 - ((mu ^ (mu >> 1)) & 1)
    differ = (mu & 1) ^ 1
    return y * 4 + (((t >> 1) ^ cross) & 1) * 2 + ((t ^ differ) & 1)


def embed_kernel(who_ref, patches_ref, weight_ref, out_hbm, out_ref, out_sem):
    seq = who_ref[0]
    left = [patches_ref[:, b].reshape(256, 512) for b in range(2)]
    size = 256
    stores = []
    for n in range(4):
        columns = pl.ds(n * size, size)
        total = jnp.dot(left[0], weight_ref[0, :, columns], preferred_element_type=F32)
        total = total + jnp.dot(left[1], weight_ref[1, :, columns], preferred_element_type=F32)
        total = total.reshape(16, 2, 2, 4, size)
        for a in range(2):
            for t in range(32):
                member, _ = route((seq & 30) + a, t)
                out_ref[a, member, :, columns] = total[t % 16, t // 16, a].astype(BF16)
        store = pltpu.make_async_copy(
            out_ref.at[:, :, :, columns], out_hbm.at[:, :, :, columns], out_sem.at[n]
        )
        store.start()
        stores.append(store)
    for store in stores:
        store.wait()


def embed(who, patches, weight):
    return pl.pallas_call(
        embed_kernel,
        in_specs=[pl.BlockSpec(memory_space=pltpu.SMEM), VMEM, VMEM],
        out_specs=pl.BlockSpec(memory_space=pl.ANY),
        out_shape=pltpu.HBM((2, 32, 4, 1024), BF16),
        scratch_shapes=[pltpu.VMEM((2, 32, 4, 1024), BF16), pltpu.SemaphoreType.DMA((4,))],
        compiler_params=ROOM,
        cost_estimate=pl.CostEstimate(flops=540000000, bytes_accessed=3 << 20, transcendentals=0),
    )(who, patches, weight)


def norm_kernel(who_ref, rows_ref, position_ref, gain_ref, out_ref):
    part = arrived_from(who_ref[0], who_ref[1]) & 3
    block = position_ref[...].astype(F32).reshape(4, 4, 1024)
    hidden = rows_ref[...]
    for k in range(4):
        hidden = hidden + jnp.where(part == k, block[k], 0.0)
    row_mean = jnp.mean(hidden, -1, keepdims=True)
    row_square = jnp.mean(hidden * hidden, -1, keepdims=True)
    variance = row_square - row_mean * row_mean
    normed = (hidden - row_mean) * lax.rsqrt(variance + epsilon) * gain_ref[...]
    out_ref[...] = jnp.broadcast_to(normed.astype(BF16)[None], (32, 4, 1024))


def norm(who, rows, position, norm_gain):
    return pl.pallas_call(
        norm_kernel,
        grid_spec=pltpu.PrefetchScalarGridSpec(
            num_scalar_prefetch=1,
            grid=(1,),
            in_specs=[
                pl.BlockSpec((4, 1024), lambda n, who: (0, 0)),
                pl.BlockSpec((16, 1024), lambda n, who: (arrived_from(who[0], who[1]) >> 2, 0)),
                pl.BlockSpec((1, 1024), lambda n, who: (0, 0)),
            ],
            out_specs=pl.BlockSpec((32, 4, 1024), lambda n, who: (0, 0, 0)),
        ),
        out_shape=jax.ShapeDtypeStruct((32, 4, 1024), BF16),
        compiler_params=ROOM,
        cost_estimate=pl.CostEstimate(flops=100000, bytes_accessed=300000, transcendentals=0),
    )(who, rows, position, norm_gain.reshape(1, 1024))


def head_kernel(who_ref, normed_ref, weight_ref, out_hbm, out_ref, out_sem):
    gathered = normed_ref[...].astype(F32).reshape(128, 1024).astype(BF16)
    row = lax.broadcasted_iota(jnp.int32, (128, 128), 0)
    column = lax.broadcasted_iota(jnp.int32, (128, 128), 1)
    _, mu = route(row >> 2, who_ref[0])
    order = jnp.where(column == mu * 4 + (row & 3), 1.0, 0.0).astype(BF16)
    left = jnp.dot(order, gathered, preferred_element_type=F32).astype(BF16)
    stores = []
    for n, (start, size) in enumerate(HEAD_COLUMNS):
        columns = pl.ds(start, size)
        product = jnp.dot(left, weight_ref[:, columns], preferred_element_type=F32)
        out_ref[:, columns] = product.astype(BF16)
        store = pltpu.make_async_copy(out_ref.at[:, columns], out_hbm.at[:, columns], out_sem.at[n])
        store.start()
        stores.append(store)
    for store in stores:
        store.wait()


HEAD_COLUMNS = ((0, 512), (512, 512), (1024, 384))


def head(who, normed, head_weight):
    return pl.pallas_call(
        head_kernel,
        in_specs=[pl.BlockSpec(memory_space=pltpu.SMEM), VMEM, VMEM],
        out_specs=pl.BlockSpec(memory_space=pl.ANY),
        out_shape=jax.ShapeDtypeStruct((128, 1408), BF16),
        scratch_shapes=[
            pltpu.VMEM((128, 1408), BF16),
            pltpu.SemaphoreType.DMA((len(HEAD_COLUMNS),)),
        ],
        compiler_params=ROOM,
        cost_estimate=pl.CostEstimate(flops=370000000, bytes_accessed=4 << 20, transcendentals=0),
    )(who, normed, head_weight)


def advance_kernel(
    edge_ref, fields_ref, source_ref, yl_ref, yh_ref, xl_ref, xh_ref,
    out_ref, ylo, yhi, xlo, xhi, clo, chi, one_ref, face_ref,
):
    ylo[...] = yl_ref[...].astype(F32)
    yhi[...] = yh_ref[...].astype(F32)
    for payload, cells, corners in ((xl_ref, xlo, clo), (xh_ref, xhi, chi)):
        cells[...] = payload[0:256].astype(F32).reshape(2, 128, 256)
        corners[...] = payload[256:288].astype(F32).reshape(2, 16, 256)
    row = lax.broadcasted_iota(jnp.int32, (8, 256), 0)
    lane = lax.broadcasted_iota(jnp.int32, (8, 256), 1)
    first_row, last_row = row == 0, row == 7
    first_lane, last_lane = lane == 0, lane == 255

    def shifted(tile, low, high):
        before = jnp.where(first_row, low, pltpu.roll(tile, 1, 0))
        after = jnp.where(last_row, high, pltpu.roll(tile, 7, 0))
        return before, after

    def tendency(centre, velocity, xm, xp, ym, yp):
        zm = jnp.where(first_lane, 0.0, pltpu.roll(centre, 1, 1))
        zp = jnp.where(last_lane, 0.0, pltpu.roll(centre, 255, 1))
        laplacian = xp + xm + yp + ym + zp + zm - 6.0 * centre
        advection = velocity[0] * (xp - xm) + velocity[1] * (yp - ym) + velocity[2] * (zp - zm)
        return diffusivity * laplacian - 0.5 * advection

    def at8(f):
        return pl.ds(pl.multiple_of(f * 8, 8), 8)

    def first_stage(f, carry):
        mine = at8(f)
        for i in range(8):
            centre = fields_ref[f, i]
            xm = fields_ref[f, i - 1] if i > 0 else xlo[1, mine]
            xp = fields_ref[f, i + 1] if i < 7 else xhi[0, mine]
            low = ylo[1, pl.ds(f * 8 + i, 1)]
            high = yhi[0, pl.ds(f * 8 + i, 1)]
            ym, yp = shifted(centre, low, high)
            velocity = [fields_ref[k, i] for k in range(3)]
            one_ref[f, i] = centre + time_step * tendency(centre, velocity, xm, xp, ym, yp)
        for side in range(2):
            halo = xlo if side == 0 else xhi
            corner = clo if side == 0 else chi
            near = 1 if side == 0 else 0
            centre = halo[near, mine]
            outer = halo[1 - near, mine]
            inner = fields_ref[f, 0 if side == 0 else 7]
            xm, xp = (outer, inner) if side == 0 else (inner, outer)
            ym, yp = shifted(centre, corner[0, pl.ds(f, 1)], corner[1, pl.ds(f, 1)])
            velocity = [halo[near, k * 8 : k * 8 + 8] for k in range(3)]
            value = centre + time_step * tendency(centre, velocity, xm, xp, ym, yp)
            face_ref[side, mine] = value * edge_ref[side]
        for side in range(2):
            halo = ylo if side == 0 else yhi
            near = 1 if side == 0 else 0
            centre = halo[near, mine]
            outer = halo[1 - near, mine]
            inner = fields_ref[f, :, 0 if side == 0 else 7, :]
            ym, yp = (outer, inner) if side == 0 else (inner, outer)
            xm, xp = shifted(centre, clo[side, pl.ds(f, 1)], chi[side, pl.ds(f, 1)])
            velocity = [halo[near, k * 8 : k * 8 + 8] for k in range(3)]
            value = centre + time_step * tendency(centre, velocity, xm, xp, ym, yp)
            face_ref[2 + side, mine] = value * edge_ref[2 + side]
        return carry

    lax.fori_loop(0, 16, first_stage, 0)

    def second_stage(f, with_source):
        mine = at8(f)
        for i in range(8):
            centre = one_ref[f, i]
            xm = one_ref[f, i - 1] if i > 0 else face_ref[0, mine]
            xp = one_ref[f, i + 1] if i < 7 else face_ref[1, mine]
            low = face_ref[2, pl.ds(f * 8 + i, 1)]
            high = face_ref[3, pl.ds(f * 8 + i, 1)]
            ym, yp = shifted(centre, low, high)
            velocity = [one_ref[k, i] for k in range(3)]
            value = 0.5 * (fields_ref[f, i] + centre + time_step * tendency(centre, velocity, xm, xp, ym, yp))
            if with_source:
                value = value + time_step * source_ref[f - 3, i].astype(F32)
            out_ref[f, i] = value

    for f in range(3):
        second_stage(f, False)

    def species(f, carry):
        second_stage(f, True)
        return carry

    lax.fori_loop(3, 16, species, 0)


def advance(edges, fields, lagged_source, y_low, y_high, x_low, x_high):
    return pl.pallas_call(
        advance_kernel,
        in_specs=[pl.BlockSpec(memory_space=pltpu.SMEM)] + [VMEM] * 6,
        out_specs=VMEM,
        out_shape=jax.ShapeDtypeStruct((16, 8, 8, 256), F32),
        scratch_shapes=[pltpu.VMEM((2, 128, 256), F32)] * 4
        + [pltpu.VMEM((2, 16, 256), F32)] * 2
        + [pltpu.VMEM((16, 8, 8, 256), F32), pltpu.VMEM((4, 128, 256), F32)],
        cost_estimate=pl.CostEstimate(flops=100000000, bytes_accessed=4 << 20, transcendentals=0),
    )(edges, fields, lagged_source, y_low, y_high, x_low, x_high)


def along(value, axes, step):
    count = 1
    for axis in axes:
        count *= lax.axis_size(axis)
    pairs = [(i, i + step) for i in range(count) if 0 <= i + step < count]
    return lax.ppermute(value, axes, pairs)


SWAP = [
    (s * 32 + route(s, t)[0], t * 32 + route(s, t)[1]) for s in range(32) for t in range(32)
]


def on_device(fields, lagged_source, embed_weight, position, norm_gain, head_weight):
    core = lax.axis_index("core")
    mp = lax.axis_index("mp")
    seq = lax.axis_index("sq") * 2 + core
    x_axes = ("sq", "core")

    patches = lax.all_to_all(pack(fields), "mp", 0, 0, tiled=True)

    y_first, y_last = y_edges(fields)
    y_low = along(y_last, ("mp",), 1)
    y_high = along(y_first, ("mp",), -1)
    who = jnp.stack([seq, mp]).astype(jnp.int32)
    edges = jnp.stack([seq > 0, seq < 31, mp > 0, mp < 31]).astype(F32)
    weight = lax.dynamic_slice_in_dim(embed_weight, core * 1024, 1024, 0).reshape(2, 512, 1024)
    patches, who, edges, weight, y_low, y_high = lax.optimization_barrier(
        (patches, who, edges, weight, y_low, y_high)
    )

    patches = patches.reshape(16, 2, 16, 512)
    partial_sums = embed(who, patches, weight)
    pieces = lax.all_to_all(partial_sums.reshape(64, 4, 1024), ("core", "mp"), 0, 0, tiled=True)

    x_first, x_last = x_edges(fields, y_low, y_high)
    x_low = along(x_last, x_axes, 1)
    x_high = along(x_first, x_axes, -1)
    pieces, x_low, x_high = lax.optimization_barrier((pieces, x_low, x_high))

    rows = jnp.sum(pieces.astype(F32), 0)
    rows = lax.ppermute(rows, ALL, SWAP)
    everyone = norm(who, rows, position, norm_gain)
    normed = lax.all_to_all(everyone, "mp", 0, 0, tiled=True)

    edges, _ = lax.optimization_barrier((edges, everyone))
    fields_next = advance(edges, fields, lagged_source, y_low, y_high, x_low, x_high)
    normed, fields_next = lax.optimization_barrier((normed, fields_next))

    return fields_next, head(who, normed, head_weight)


def solution(mesh):
    split = Mesh(mesh.devices.reshape(16, 2, 32), ALL)
    seq = ("sq", "core")
    placed = (
        P(None, seq, "mp", None),
        P(None, seq, "mp", None),
        P("mp", None),
        P(seq, None),
        P(),
        P(None, "mp"),
    )
    return jax.shard_map(
        on_device,
        mesh=split,
        in_specs=placed,
        out_specs=(P(None, seq, "mp", None), P(seq, "mp")),
        check_vma=False,
    )
```

```python
import jax
import jax.numpy as jnp
from jax import lax
from jax.experimental import pallas as pl
from jax.experimental.pallas import tpu as pltpu
from jax.sharding import Mesh
from jax.sharding import PartitionSpec as P

PATCH = 16
time_step = 0.25
diffusivity = 0.2
epsilon = 1e-05

F32 = jnp.float32
BF16 = jnp.bfloat16
ALL = ("sq", "core", "mp")


def block_transpose(tiles):
    row = lax.broadcasted_iota(jnp.int32, (8, 128), 0)
    lane_block = lax.broadcasted_iota(jnp.int32, (8, 128), 1) // PATCH
    for s in (4, 2, 1):
        row_bit = (row // s) & 1
        keep, down = row_bit == ((lane_block // s) & 1), row_bit == 1
        after = [pltpu.roll(t, s, 0) for t in tiles]
        after = [pltpu.roll(t, 128 - PATCH * s, 1) for t in after]
        if s == 4:
            tiles = [jnp.where(keep, t, a) for t, a in zip(tiles, after)]
        else:
            before = [pltpu.roll(t, 8 - s, 0) for t in tiles]
            before = [pltpu.roll(t, PATCH * s, 1) for t in before]
            tiles = [
                jnp.where(keep, t, jnp.where(down, a, b)) for t, a, b in zip(tiles, after, before)
            ]
    return tiles


PACK_STEPS = 4


def pack_kernel(fields_hbm, packed_hbm, fields_ref, packed_ref, in_sem, out_sem):
    count = 16 // PACK_STEPS
    loads, stores = [], []
    for step in range(PACK_STEPS):
        some = pl.ds(step * count, count)
        loads.append(pltpu.make_async_copy(fields_hbm.at[some], fields_ref.at[some], in_sem.at[step]))
        some = pl.ds(step * 2 * count, 2 * count)
        stores.append(pltpu.make_async_copy(packed_ref.at[some], packed_hbm.at[some], out_sem.at[step]))
    for load in loads:
        load.start()
    for step in range(PACK_STEPS):
        loads[step].wait()
        places = [
            (step * count + k, half, g) for k in range(count) for half in range(2) for g in range(4)
        ]
        tiles = block_transpose(
            [
                fields_ref[f, half * 4 + g, :, c * 128 : (c + 1) * 128]
                for f, half, g in places
                for c in range(2)
            ]
        )
        for n, (f, half, g) in enumerate(places):
            both = jnp.concatenate(tiles[2 * n : 2 * n + 2], axis=0)
            packed_ref[f * 2 + half, :, g * 128 : (g + 1) * 128] = both.astype(BF16)
        stores[step].start()
    for store in stores:
        store.wait()


def pack(fields):
    return pl.pallas_call(
        pack_kernel,
        in_specs=[pl.BlockSpec(memory_space=pl.ANY)],
        out_specs=pl.BlockSpec(memory_space=pl.ANY),
        out_shape=jax.ShapeDtypeStruct((32, 16, 512), BF16),
        scratch_shapes=[
            pltpu.VMEM((16, 8, 8, 256), F32),
            pltpu.VMEM((32, 16, 512), BF16),
            pltpu.SemaphoreType.DMA((PACK_STEPS,)),
            pltpu.SemaphoreType.DMA((PACK_STEPS,)),
        ],
        cost_estimate=pl.CostEstimate(flops=1000000, bytes_accessed=2 << 20, transcendentals=0),
    )(fields)


VMEM = pl.BlockSpec(memory_space=pltpu.VMEM)
ROOM = pltpu.CompilerParams(vmem_limit_bytes=16 << 20)


def y_edge_kernel(fields_ref, first_ref, last_ref):
    for k in range(2):
        first_ref[k] = fields_ref[:, :, k, :].reshape(128, 256).astype(BF16)
        last_ref[k] = fields_ref[:, :, 6 + k, :].reshape(128, 256).astype(BF16)


def y_edges(fields):
    return pl.pallas_call(
        y_edge_kernel,
        in_specs=[VMEM],
        out_specs=[VMEM, VMEM],
        out_shape=[jax.ShapeDtypeStruct((2, 128, 256), BF16)] * 2,
        cost_estimate=pl.CostEstimate(flops=100000, bytes_accessed=2 << 20, transcendentals=0),
    )(fields)


def x_edge_kernel(head_ref, tail_ref, y_low_ref, y_high_ref, first_ref, last_ref, rows):
    rows[0] = y_low_ref[1].astype(F32)
    rows[1] = y_high_ref[0].astype(F32)
    for cells, out_ref, i in ((head_ref, first_ref, 0), (tail_ref, last_ref, 7)):
        for k in range(2):
            out_ref[k * 128 : (k + 1) * 128] = cells[:, k].reshape(128, 256).astype(BF16)
        for k in range(2):
            corner = rows[k].reshape(16, 8, 256)[:, i]
            out_ref[256 + k * 16 : 272 + k * 16] = corner.astype(BF16)


def x_edges(fields, y_low, y_high):
    return pl.pallas_call(
        x_edge_kernel,
        grid=(1,),
        in_specs=[
            pl.BlockSpec((16, 2, 8, 256), lambda n: (0, 0, 0, 0)),
            pl.BlockSpec((16, 2, 8, 256), lambda n: (0, 3, 0, 0)),
            pl.BlockSpec((2, 128, 256), lambda n: (0, 0, 0)),
            pl.BlockSpec((2, 128, 256), lambda n: (0, 0, 0)),
        ],
        out_specs=[pl.BlockSpec((288, 256), lambda n: (0, 0))] * 2,
        out_shape=[jax.ShapeDtypeStruct((288, 256), BF16)] * 2,
        scratch_shapes=[pltpu.VMEM((2, 128, 256), F32)],
        cost_estimate=pl.CostEstimate(flops=100000, bytes_accessed=1 << 20, transcendentals=0),
    )(fields, fields, y_low, y_high)


def route(s, t):
    z = ((t >> 2) - (s >> 2)) & 7
    differ = (s ^ t) & 1
    cross = ((s ^ t) >> 1) & 1
    near = 1 + differ
    m = z * 4 + near + cross * (2 * differ - 1)
    mu = z * 4 + near + cross * (2 - 4 * differ)
    return m, mu


def arrived_from(t, mu):
    y = ((t >> 2) - (mu >> 2)) & 7
    cross = 1 - ((mu ^ (mu >> 1)) & 1)
    differ = (mu & 1) ^ 1
    return y * 4 + (((t >> 1) ^ cross) & 1) * 2 + ((t ^ differ) & 1)


def embed_kernel(who_ref, patches_ref, weight_ref, keep_ref, send_hbm, send_ref, out_sem):
    seq = who_ref[0]
    other = (seq & 1) == 1
    left = [patches_ref[:, b].reshape(256, 512) for b in range(2)]
    size = 256
    stores = []
    for n in range(4):
        columns = pl.ds(n * size, size)
        total = jnp.dot(left[0], weight_ref[0, :, columns], preferred_element_type=F32)
        total = total + jnp.dot(left[1], weight_ref[1, :, columns], preferred_element_type=F32)
        total = total.reshape(16, 2, 8, size)
        for t in range(32):
            rows = total[t % 16, t // 16]
            rows = jnp.where(other, pltpu.roll(rows, 4, 0), rows)
            keep_ref[route(seq, t)[0], :, columns] = rows[0:4]
            send_ref[route(seq ^ 1, t)[0], :, columns] = rows[4:8].astype(BF16)
        store = pltpu.make_async_copy(
            send_ref.at[:, :, columns], send_hbm.at[:, :, columns], out_sem.at[n]
        )
        store.start()
        stores.append(store)
    for store in stores:
        store.wait()


def embed(who, patches, weight):
    return pl.pallas_call(
        embed_kernel,
        in_specs=[pl.BlockSpec(memory_space=pltpu.SMEM), VMEM, VMEM],
        out_specs=[VMEM, pl.BlockSpec(memory_space=pl.ANY)],
        out_shape=[
            jax.ShapeDtypeStruct((32, 4, 1024), F32),
            pltpu.HBM((32, 4, 1024), BF16),
        ],
        scratch_shapes=[pltpu.VMEM((32, 4, 1024), BF16), pltpu.SemaphoreType.DMA((4,))],
        compiler_params=ROOM,
        cost_estimate=pl.CostEstimate(flops=540000000, bytes_accessed=3 << 20, transcendentals=0),
    )(who, patches, weight)


def norm_kernel(who_ref, rows_ref, position_ref, gain_ref, out_ref):
    part = arrived_from(who_ref[0], who_ref[1]) & 3
    block = position_ref[...].astype(F32).reshape(4, 4, 1024)
    hidden = rows_ref[...]
    for k in range(4):
        hidden = hidden + jnp.where(part == k, block[k], 0.0)
    row_mean = jnp.mean(hidden, -1, keepdims=True)
    row_square = jnp.mean(hidden * hidden, -1, keepdims=True)
    variance = row_square - row_mean * row_mean
    normed = (hidden - row_mean) * lax.rsqrt(variance + epsilon) * gain_ref[...]
    out_ref[...] = jnp.broadcast_to(normed.astype(BF16)[None], (32, 4, 1024))


def norm(who, rows, position, norm_gain):
    return pl.pallas_call(
        norm_kernel,
        grid_spec=pltpu.PrefetchScalarGridSpec(
            num_scalar_prefetch=1,
            grid=(1,),
            in_specs=[
                pl.BlockSpec((4, 1024), lambda n, who: (0, 0)),
                pl.BlockSpec((16, 1024), lambda n, who: (arrived_from(who[0], who[1]) >> 2, 0)),
                pl.BlockSpec((1, 1024), lambda n, who: (0, 0)),
            ],
            out_specs=pl.BlockSpec((32, 4, 1024), lambda n, who: (0, 0, 0)),
        ),
        out_shape=jax.ShapeDtypeStruct((32, 4, 1024), BF16),
        compiler_params=ROOM,
        cost_estimate=pl.CostEstimate(flops=100000, bytes_accessed=300000, transcendentals=0),
    )(who, rows, position, norm_gain.reshape(1, 1024))


def head_kernel(who_ref, normed_ref, weight_ref, out_hbm, out_ref, out_sem):
    gathered = normed_ref[...].astype(F32).reshape(128, 1024).astype(BF16)
    row = lax.broadcasted_iota(jnp.int32, (128, 128), 0)
    column = lax.broadcasted_iota(jnp.int32, (128, 128), 1)
    _, mu = route(row >> 2, who_ref[0])
    order = jnp.where(column == mu * 4 + (row & 3), 1.0, 0.0).astype(BF16)
    left = jnp.dot(order, gathered, preferred_element_type=F32).astype(BF16)
    stores = []
    for n, (start, size) in enumerate(HEAD_COLUMNS):
        columns = pl.ds(start, size)
        product = jnp.dot(left, weight_ref[:, columns], preferred_element_type=F32)
        out_ref[:, columns] = product.astype(BF16)
        store = pltpu.make_async_copy(out_ref.at[:, columns], out_hbm.at[:, columns], out_sem.at[n])
        store.start()
        stores.append(store)
    for store in stores:
        store.wait()


HEAD_COLUMNS = ((0, 512), (512, 512), (1024, 384))


def head(who, normed, head_weight):
    return pl.pallas_call(
        head_kernel,
        in_specs=[pl.BlockSpec(memory_space=pltpu.SMEM), VMEM, VMEM],
        out_specs=pl.BlockSpec(memory_space=pl.ANY),
        out_shape=jax.ShapeDtypeStruct((128, 1408), BF16),
        scratch_shapes=[
            pltpu.VMEM((128, 1408), BF16),
            pltpu.SemaphoreType.DMA((len(HEAD_COLUMNS),)),
        ],
        compiler_params=ROOM,
        cost_estimate=pl.CostEstimate(flops=370000000, bytes_accessed=4 << 20, transcendentals=0),
    )(who, normed, head_weight)


def advance_kernel(
    edge_ref, fields_ref, source_ref, yl_ref, yh_ref, xl_ref, xh_ref,
    out_ref, ylo, yhi, xlo, xhi, clo, chi, one_ref, face_ref,
):
    ylo[...] = yl_ref[...].astype(F32)
    yhi[...] = yh_ref[...].astype(F32)
    for payload, cells, corners in ((xl_ref, xlo, clo), (xh_ref, xhi, chi)):
        cells[...] = payload[0:256].astype(F32).reshape(2, 128, 256)
        corners[...] = payload[256:288].astype(F32).reshape(2, 16, 256)
    row = lax.broadcasted_iota(jnp.int32, (8, 256), 0)
    lane = lax.broadcasted_iota(jnp.int32, (8, 256), 1)
    first_row, last_row = row == 0, row == 7
    first_lane, last_lane = lane == 0, lane == 255

    def shifted(tile, low, high):
        before = jnp.where(first_row, low, pltpu.roll(tile, 1, 0))
        after = jnp.where(last_row, high, pltpu.roll(tile, 7, 0))
        return before, after

    def tendency(centre, velocity, xm, xp, ym, yp):
        zm = jnp.where(first_lane, 0.0, pltpu.roll(centre, 1, 1))
        zp = jnp.where(last_lane, 0.0, pltpu.roll(centre, 255, 1))
        laplacian = xp + xm + yp + ym + zp + zm - 6.0 * centre
        advection = velocity[0] * (xp - xm) + velocity[1] * (yp - ym) + velocity[2] * (zp - zm)
        return diffusivity * laplacian - 0.5 * advection

    def at8(f):
        return pl.ds(pl.multiple_of(f * 8, 8), 8)

    def first_stage(f, carry):
        mine = at8(f)
        for i in range(8):
            centre = fields_ref[f, i]
            xm = fields_ref[f, i - 1] if i > 0 else xlo[1, mine]
            xp = fields_ref[f, i + 1] if i < 7 else xhi[0, mine]
            low = ylo[1, pl.ds(f * 8 + i, 1)]
            high = yhi[0, pl.ds(f * 8 + i, 1)]
            ym, yp = shifted(centre, low, high)
            velocity = [fields_ref[k, i] for k in range(3)]
            one_ref[f, i] = centre + time_step * tendency(centre, velocity, xm, xp, ym, yp)
        for side in range(2):
            halo = xlo if side == 0 else xhi
            corner = clo if side == 0 else chi
            near = 1 if side == 0 else 0
            centre = halo[near, mine]
            outer = halo[1 - near, mine]
            inner = fields_ref[f, 0 if side == 0 else 7]
            xm, xp = (outer, inner) if side == 0 else (inner, outer)
            ym, yp = shifted(centre, corner[0, pl.ds(f, 1)], corner[1, pl.ds(f, 1)])
            velocity = [halo[near, k * 8 : k * 8 + 8] for k in range(3)]
            value = centre + time_step * tendency(centre, velocity, xm, xp, ym, yp)
            face_ref[side, mine] = value * edge_ref[side]
        for side in range(2):
            halo = ylo if side == 0 else yhi
            near = 1 if side == 0 else 0
            centre = halo[near, mine]
            outer = halo[1 - near, mine]
            inner = fields_ref[f, :, 0 if side == 0 else 7, :]
            ym, yp = (outer, inner) if side == 0 else (inner, outer)
            xm, xp = shifted(centre, clo[side, pl.ds(f, 1)], chi[side, pl.ds(f, 1)])
            velocity = [halo[near, k * 8 : k * 8 + 8] for k in range(3)]
            value = centre + time_step * tendency(centre, velocity, xm, xp, ym, yp)
            face_ref[2 + side, mine] = value * edge_ref[2 + side]
        return carry

    lax.fori_loop(0, 16, first_stage, 0)

    def second_stage(f, with_source):
        mine = at8(f)
        for i in range(8):
            centre = one_ref[f, i]
            xm = one_ref[f, i - 1] if i > 0 else face_ref[0, mine]
            xp = one_ref[f, i + 1] if i < 7 else face_ref[1, mine]
            low = face_ref[2, pl.ds(f * 8 + i, 1)]
            high = face_ref[3, pl.ds(f * 8 + i, 1)]
            ym, yp = shifted(centre, low, high)
            velocity = [one_ref[k, i] for k in range(3)]
            value = 0.5 * (fields_ref[f, i] + centre + time_step * tendency(centre, velocity, xm, xp, ym, yp))
            if with_source:
                value = value + time_step * source_ref[f - 3, i].astype(F32)
            out_ref[f, i] = value

    for f in range(3):
        second_stage(f, False)

    def species(f, carry):
        second_stage(f, True)
        return carry

    lax.fori_loop(3, 16, species, 0)


def advance(edges, fields, lagged_source, y_low, y_high, x_low, x_high):
    return pl.pallas_call(
        advance_kernel,
        in_specs=[pl.BlockSpec(memory_space=pltpu.SMEM)] + [VMEM] * 6,
        out_specs=VMEM,
        out_shape=jax.ShapeDtypeStruct((16, 8, 8, 256), F32),
        scratch_shapes=[pltpu.VMEM((2, 128, 256), F32)] * 4
        + [pltpu.VMEM((2, 16, 256), F32)] * 2
        + [pltpu.VMEM((16, 8, 8, 256), F32), pltpu.VMEM((4, 128, 256), F32)],
        cost_estimate=pl.CostEstimate(flops=100000000, bytes_accessed=4 << 20, transcendentals=0),
    )(edges, fields, lagged_source, y_low, y_high, x_low, x_high)


def along(value, axes, step):
    count = 1
    for axis in axes:
        count *= lax.axis_size(axis)
    pairs = [(i, i + step) for i in range(count) if 0 <= i + step < count]
    return lax.ppermute(value, axes, pairs)


SWAP = [
    (s * 32 + route(s, t)[0], t * 32 + route(s, t)[1]) for s in range(32) for t in range(32)
]


def on_device(fields, lagged_source, embed_weight, position, norm_gain, head_weight):
    core = lax.axis_index("core")
    mp = lax.axis_index("mp")
    seq = lax.axis_index("sq") * 2 + core
    x_axes = ("sq", "core")

    patches = lax.all_to_all(pack(fields), "mp", 0, 0, tiled=True)

    y_first, y_last = y_edges(fields)
    y_low = along(y_last, ("mp",), 1)
    y_high = along(y_first, ("mp",), -1)
    who = jnp.stack([seq, mp]).astype(jnp.int32)
    edges = jnp.stack([seq > 0, seq < 31, mp > 0, mp < 31]).astype(F32)
    weight = lax.dynamic_slice_in_dim(embed_weight, core * 1024, 1024, 0).reshape(2, 512, 1024)
    patches, who, edges, weight, y_low, y_high = lax.optimization_barrier(
        (patches, who, edges, weight, y_low, y_high)
    )

    patches = patches.reshape(16, 2, 16, 512)
    keep, send = embed(who, patches, weight)
    theirs = lax.ppermute(send, "core", [(0, 1), (1, 0)])
    partial_sums = (keep + theirs.astype(F32)).astype(BF16)
    pieces = lax.all_to_all(partial_sums, "mp", 0, 0, tiled=True)

    x_first, x_last = x_edges(fields, y_low, y_high)
    x_low = along(x_last, x_axes, 1)
    x_high = along(x_first, x_axes, -1)
    pieces, x_low, x_high = lax.optimization_barrier((pieces, x_low, x_high))

    rows = jnp.sum(pieces.astype(F32), 0)
    rows = lax.ppermute(rows, ALL, SWAP)
    everyone = norm(who, rows, position, norm_gain)
    normed = lax.all_to_all(everyone, "mp", 0, 0, tiled=True)

    edges, _ = lax.optimization_barrier((edges, everyone))
    fields_next = advance(edges, fields, lagged_source, y_low, y_high, x_low, x_high)
    normed, fields_next = lax.optimization_barrier((normed, fields_next))

    return fields_next, head(who, normed, head_weight)


def solution(mesh):
    split = Mesh(mesh.devices.reshape(16, 2, 32), ALL)
    seq = ("sq", "core")
    placed = (
        P(None, seq, "mp", None),
        P(None, seq, "mp", None),
        P("mp", None),
        P(seq, None),
        P(),
        P(None, "mp"),
    )
    return jax.shard_map(
        on_device,
        mesh=split,
        in_specs=placed,
        out_specs=(P(None, seq, "mp", None), P(seq, "mp")),
        check_vma=False,
    )
```

```python
import jax
import jax.numpy as jnp
from jax import lax
from jax.experimental import pallas as pl
from jax.experimental.pallas import tpu as pltpu
from jax.sharding import Mesh
from jax.sharding import PartitionSpec as P

PATCH = 16
time_step = 0.25
diffusivity = 0.2
epsilon = 1e-05

F32 = jnp.float32
BF16 = jnp.bfloat16
ALL = ("sq", "core", "mp")


def block_transpose(tiles):
    row = lax.broadcasted_iota(jnp.int32, (8, 128), 0)
    lane_block = lax.broadcasted_iota(jnp.int32, (8, 128), 1) // PATCH
    for s in (4, 2, 1):
        row_bit = (row // s) & 1
        keep, down = row_bit == ((lane_block // s) & 1), row_bit == 1
        after = [pltpu.roll(t, s, 0) for t in tiles]
        after = [pltpu.roll(t, 128 - PATCH * s, 1) for t in after]
        if s == 4:
            tiles = [jnp.where(keep, t, a) for t, a in zip(tiles, after)]
        else:
            before = [pltpu.roll(t, 8 - s, 0) for t in tiles]
            before = [pltpu.roll(t, PATCH * s, 1) for t in before]
            tiles = [
                jnp.where(keep, t, jnp.where(down, a, b)) for t, a, b in zip(tiles, after, before)
            ]
    return tiles


PACK_STEPS = 4


def pack_kernel(fields_hbm, packed_hbm, fields_ref, packed_ref, in_sem, out_sem):
    count = 16 // PACK_STEPS
    loads, stores = [], []
    for step in range(PACK_STEPS):
        some = pl.ds(step * count, count)
        loads.append(pltpu.make_async_copy(fields_hbm.at[some], fields_ref.at[some], in_sem.at[step]))
        some = pl.ds(step * 2 * count, 2 * count)
        stores.append(pltpu.make_async_copy(packed_ref.at[some], packed_hbm.at[some], out_sem.at[step]))
    for load in loads:
        load.start()
    for step in range(PACK_STEPS):
        loads[step].wait()
        places = [
            (step * count + k, half, g) for k in range(count) for half in range(2) for g in range(4)
        ]
        tiles = block_transpose(
            [
                fields_ref[f, half * 4 + g, :, c * 128 : (c + 1) * 128]
                for f, half, g in places
                for c in range(2)
            ]
        )
        for n, (f, half, g) in enumerate(places):
            both = jnp.concatenate(tiles[2 * n : 2 * n + 2], axis=0)
            packed_ref[f * 2 + half, :, g * 128 : (g + 1) * 128] = both.astype(BF16)
        stores[step].start()
    for store in stores:
        store.wait()


def pack(fields):
    return pl.pallas_call(
        pack_kernel,
        in_specs=[pl.BlockSpec(memory_space=pl.ANY)],
        out_specs=pl.BlockSpec(memory_space=pl.ANY),
        out_shape=jax.ShapeDtypeStruct((32, 16, 512), BF16),
        scratch_shapes=[
            pltpu.VMEM((16, 8, 8, 256), F32),
            pltpu.VMEM((32, 16, 512), BF16),
            pltpu.SemaphoreType.DMA((PACK_STEPS,)),
            pltpu.SemaphoreType.DMA((PACK_STEPS,)),
        ],
        cost_estimate=pl.CostEstimate(flops=1000000, bytes_accessed=2 << 20, transcendentals=0),
    )(fields)


VMEM = pl.BlockSpec(memory_space=pltpu.VMEM)
ROOM = pltpu.CompilerParams(vmem_limit_bytes=16 << 20)


def y_edge_kernel(fields_ref, first_ref, last_ref):
    for k in range(2):
        first_ref[k] = fields_ref[:, :, k, :].reshape(128, 256).astype(BF16)
        last_ref[k] = fields_ref[:, :, 6 + k, :].reshape(128, 256).astype(BF16)


def y_edges(fields):
    return pl.pallas_call(
        y_edge_kernel,
        in_specs=[VMEM],
        out_specs=[VMEM, VMEM],
        out_shape=[jax.ShapeDtypeStruct((2, 128, 256), BF16)] * 2,
        cost_estimate=pl.CostEstimate(flops=100000, bytes_accessed=2 << 20, transcendentals=0),
    )(fields)


def x_edge_kernel(head_ref, tail_ref, y_low_ref, y_high_ref, first_ref, last_ref, rows):
    rows[0] = y_low_ref[1].astype(F32)
    rows[1] = y_high_ref[0].astype(F32)
    for cells, out_ref, i in ((head_ref, first_ref, 0), (tail_ref, last_ref, 7)):
        for k in range(2):
            out_ref[k * 128 : (k + 1) * 128] = cells[:, k].reshape(128, 256).astype(BF16)
        for k in range(2):
            corner = rows[k].reshape(16, 8, 256)[:, i]
            out_ref[256 + k * 16 : 272 + k * 16] = corner.astype(BF16)


def x_edges(fields, y_low, y_high):
    return pl.pallas_call(
        x_edge_kernel,
        grid=(1,),
        in_specs=[
            pl.BlockSpec((16, 2, 8, 256), lambda n: (0, 0, 0, 0)),
            pl.BlockSpec((16, 2, 8, 256), lambda n: (0, 3, 0, 0)),
            pl.BlockSpec((2, 128, 256), lambda n: (0, 0, 0)),
            pl.BlockSpec((2, 128, 256), lambda n: (0, 0, 0)),
        ],
        out_specs=[pl.BlockSpec((288, 256), lambda n: (0, 0))] * 2,
        out_shape=[jax.ShapeDtypeStruct((288, 256), BF16)] * 2,
        scratch_shapes=[pltpu.VMEM((2, 128, 256), F32)],
        cost_estimate=pl.CostEstimate(flops=100000, bytes_accessed=1 << 20, transcendentals=0),
    )(fields, fields, y_low, y_high)


def route(s, t):
    z = ((t >> 2) - (s >> 2)) & 7
    differ = (s ^ t) & 1
    cross = ((s ^ t) >> 1) & 1
    near = 1 + differ
    m = z * 4 + near + cross * (2 * differ - 1)
    mu = z * 4 + near + cross * (2 - 4 * differ)
    return m, mu


def arrived_from(t, mu):
    y = ((t >> 2) - (mu >> 2)) & 7
    cross = 1 - ((mu ^ (mu >> 1)) & 1)
    differ = (mu & 1) ^ 1
    return y * 4 + (((t >> 1) ^ cross) & 1) * 2 + ((t ^ differ) & 1)


def embed_kernel(who_ref, patches_ref, weight_ref, keep_ref, send_hbm, send_ref, out_sem):
    seq = who_ref[0]
    other = (seq & 1) == 1
    left = [patches_ref[:, b].reshape(256, 512) for b in range(2)]
    size = 256
    stores = []
    for n in range(4):
        columns = pl.ds(n * size, size)
        total = jnp.dot(left[0], weight_ref[0, :, columns], preferred_element_type=F32)
        total = total + jnp.dot(left[1], weight_ref[1, :, columns], preferred_element_type=F32)
        total = total.reshape(16, 2, 8, size)
        for t in range(32):
            rows = total[t % 16, t // 16]
            rows = jnp.where(other, pltpu.roll(rows, 4, 0), rows)
            keep_ref[route(seq, t)[0], :, columns] = rows[0:4]
            send_ref[route(seq ^ 1, t)[0], :, columns] = rows[4:8].astype(BF16)
        store = pltpu.make_async_copy(
            send_ref.at[:, :, columns], send_hbm.at[:, :, columns], out_sem.at[n]
        )
        store.start()
        stores.append(store)
    for store in stores:
        store.wait()


def embed(who, patches, weight):
    return pl.pallas_call(
        embed_kernel,
        in_specs=[pl.BlockSpec(memory_space=pltpu.SMEM), VMEM, VMEM],
        out_specs=[VMEM, pl.BlockSpec(memory_space=pl.ANY)],
        out_shape=[
            jax.ShapeDtypeStruct((32, 4, 1024), F32),
            pltpu.HBM((32, 4, 1024), BF16),
        ],
        scratch_shapes=[pltpu.VMEM((32, 4, 1024), BF16), pltpu.SemaphoreType.DMA((4,))],
        compiler_params=ROOM,
        cost_estimate=pl.CostEstimate(flops=540000000, bytes_accessed=3 << 20, transcendentals=0),
    )(who, patches, weight)


def norm_kernel(who_ref, rows_ref, position_ref, gain_ref, out_ref):
    part = arrived_from(who_ref[0], who_ref[1]) & 3
    block = position_ref[...].astype(F32).reshape(4, 4, 1024)
    hidden = rows_ref[...]
    for k in range(4):
        hidden = hidden + jnp.where(part == k, block[k], 0.0)
    row_mean = jnp.mean(hidden, -1, keepdims=True)
    row_square = jnp.mean(hidden * hidden, -1, keepdims=True)
    variance = row_square - row_mean * row_mean
    normed = (hidden - row_mean) * lax.rsqrt(variance + epsilon) * gain_ref[...]
    out_ref[...] = jnp.broadcast_to(normed.astype(BF16)[None], (32, 4, 1024))


def norm(who, rows, position, norm_gain):
    return pl.pallas_call(
        norm_kernel,
        grid_spec=pltpu.PrefetchScalarGridSpec(
            num_scalar_prefetch=1,
            grid=(1,),
            in_specs=[
                pl.BlockSpec((4, 1024), lambda n, who: (0, 0)),
                pl.BlockSpec((16, 1024), lambda n, who: (arrived_from(who[0], who[1]) >> 2, 0)),
                pl.BlockSpec((1, 1024), lambda n, who: (0, 0)),
            ],
            out_specs=pl.BlockSpec((32, 4, 1024), lambda n, who: (0, 0, 0)),
        ),
        out_shape=jax.ShapeDtypeStruct((32, 4, 1024), BF16),
        compiler_params=ROOM,
        cost_estimate=pl.CostEstimate(flops=100000, bytes_accessed=300000, transcendentals=0),
    )(who, rows, position, norm_gain.reshape(1, 1024))


def head_kernel(who_ref, normed_ref, weight_ref, out_hbm, out_ref, out_sem):
    gathered = normed_ref[...].astype(F32).reshape(128, 1024).astype(BF16)
    row = lax.broadcasted_iota(jnp.int32, (128, 128), 0)
    column = lax.broadcasted_iota(jnp.int32, (128, 128), 1)
    _, mu = route(row >> 2, who_ref[0])
    order = jnp.where(column == mu * 4 + (row & 3), 1.0, 0.0).astype(BF16)
    left = jnp.dot(order, gathered, preferred_element_type=F32).astype(BF16)
    stores = []
    for n, (start, size) in enumerate(HEAD_COLUMNS):
        columns = pl.ds(start, size)
        product = jnp.dot(left, weight_ref[:, columns], preferred_element_type=F32)
        out_ref[:, columns] = product.astype(BF16)
        store = pltpu.make_async_copy(out_ref.at[:, columns], out_hbm.at[:, columns], out_sem.at[n])
        store.start()
        stores.append(store)
    for store in stores:
        store.wait()


HEAD_COLUMNS = ((0, 512), (512, 512), (1024, 384))


def head(who, normed, head_weight):
    return pl.pallas_call(
        head_kernel,
        in_specs=[pl.BlockSpec(memory_space=pltpu.SMEM), VMEM, VMEM],
        out_specs=pl.BlockSpec(memory_space=pl.ANY),
        out_shape=jax.ShapeDtypeStruct((128, 1408), BF16),
        scratch_shapes=[
            pltpu.VMEM((128, 1408), BF16),
            pltpu.SemaphoreType.DMA((len(HEAD_COLUMNS),)),
        ],
        compiler_params=ROOM,
        cost_estimate=pl.CostEstimate(flops=370000000, bytes_accessed=4 << 20, transcendentals=0),
    )(who, normed, head_weight)


def advance_kernel(
    edge_ref, fields_ref, source_ref, yl_ref, yh_ref, xl_ref, xh_ref,
    out_ref, ylo, yhi, xlo, xhi, clo, chi, one_ref, face_ref,
):
    ylo[...] = yl_ref[...].astype(F32)
    yhi[...] = yh_ref[...].astype(F32)
    for payload, cells, corners in ((xl_ref, xlo, clo), (xh_ref, xhi, chi)):
        cells[...] = payload[0:256].astype(F32).reshape(2, 128, 256)
        corners[...] = payload[256:288].astype(F32).reshape(2, 16, 256)
    row = lax.broadcasted_iota(jnp.int32, (8, 256), 0)
    lane = lax.broadcasted_iota(jnp.int32, (8, 256), 1)
    first_row, last_row = row == 0, row == 7
    first_lane, last_lane = lane == 0, lane == 255

    def shifted(tile, low, high):
        before = jnp.where(first_row, low, pltpu.roll(tile, 1, 0))
        after = jnp.where(last_row, high, pltpu.roll(tile, 7, 0))
        return before, after

    def tendency(centre, velocity, xm, xp, ym, yp):
        zm = jnp.where(first_lane, 0.0, pltpu.roll(centre, 1, 1))
        zp = jnp.where(last_lane, 0.0, pltpu.roll(centre, 255, 1))
        laplacian = xp + xm + yp + ym + zp + zm - 6.0 * centre
        advection = velocity[0] * (xp - xm) + velocity[1] * (yp - ym) + velocity[2] * (zp - zm)
        return diffusivity * laplacian - 0.5 * advection

    def at8(f):
        return pl.ds(pl.multiple_of(f * 8, 8), 8)

    def first_stage(f, carry):
        mine = at8(f)
        for i in range(8):
            centre = fields_ref[f, i]
            xm = fields_ref[f, i - 1] if i > 0 else xlo[1, mine]
            xp = fields_ref[f, i + 1] if i < 7 else xhi[0, mine]
            low = ylo[1, pl.ds(f * 8 + i, 1)]
            high = yhi[0, pl.ds(f * 8 + i, 1)]
            ym, yp = shifted(centre, low, high)
            velocity = [fields_ref[k, i] for k in range(3)]
            one_ref[f, i] = centre + time_step * tendency(centre, velocity, xm, xp, ym, yp)
        for side in range(2):
            halo = xlo if side == 0 else xhi
            corner = clo if side == 0 else chi
            near = 1 if side == 0 else 0
            centre = halo[near, mine]
            outer = halo[1 - near, mine]
            inner = fields_ref[f, 0 if side == 0 else 7]
            xm, xp = (outer, inner) if side == 0 else (inner, outer)
            ym, yp = shifted(centre, corner[0, pl.ds(f, 1)], corner[1, pl.ds(f, 1)])
            velocity = [halo[near, k * 8 : k * 8 + 8] for k in range(3)]
            value = centre + time_step * tendency(centre, velocity, xm, xp, ym, yp)
            face_ref[side, mine] = value * edge_ref[side]
        for side in range(2):
            halo = ylo if side == 0 else yhi
            near = 1 if side == 0 else 0
            centre = halo[near, mine]
            outer = halo[1 - near, mine]
            inner = fields_ref[f, :, 0 if side == 0 else 7, :]
            ym, yp = (outer, inner) if side == 0 else (inner, outer)
            xm, xp = shifted(centre, clo[side, pl.ds(f, 1)], chi[side, pl.ds(f, 1)])
            velocity = [halo[near, k * 8 : k * 8 + 8] for k in range(3)]
            value = centre + time_step * tendency(centre, velocity, xm, xp, ym, yp)
            face_ref[2 + side, mine] = value * edge_ref[2 + side]
        return carry

    lax.fori_loop(0, 16, first_stage, 0)

    def second_stage(f, with_source):
        mine = at8(f)
        for i in range(8):
            centre = one_ref[f, i]
            xm = one_ref[f, i - 1] if i > 0 else face_ref[0, mine]
            xp = one_ref[f, i + 1] if i < 7 else face_ref[1, mine]
            low = face_ref[2, pl.ds(f * 8 + i, 1)]
            high = face_ref[3, pl.ds(f * 8 + i, 1)]
            ym, yp = shifted(centre, low, high)
            velocity = [one_ref[k, i] for k in range(3)]
            value = 0.5 * (fields_ref[f, i] + centre + time_step * tendency(centre, velocity, xm, xp, ym, yp))
            if with_source:
                value = value + time_step * source_ref[f - 3, i].astype(F32)
            out_ref[f, i] = value

    for f in range(3):
        second_stage(f, False)

    def species(f, carry):
        second_stage(f, True)
        return carry

    lax.fori_loop(3, 16, species, 0)


def advance(edges, fields, lagged_source, y_low, y_high, x_low, x_high):
    return pl.pallas_call(
        advance_kernel,
        in_specs=[pl.BlockSpec(memory_space=pltpu.SMEM)] + [VMEM] * 6,
        out_specs=VMEM,
        out_shape=jax.ShapeDtypeStruct((16, 8, 8, 256), F32),
        scratch_shapes=[pltpu.VMEM((2, 128, 256), F32)] * 4
        + [pltpu.VMEM((2, 16, 256), F32)] * 2
        + [pltpu.VMEM((16, 8, 8, 256), F32), pltpu.VMEM((4, 128, 256), F32)],
        cost_estimate=pl.CostEstimate(flops=100000000, bytes_accessed=4 << 20, transcendentals=0),
    )(edges, fields, lagged_source, y_low, y_high, x_low, x_high)


def along(value, axes, step):
    count = 1
    for axis in axes:
        count *= lax.axis_size(axis)
    pairs = [(i, i + step) for i in range(count) if 0 <= i + step < count]
    return lax.ppermute(value, axes, pairs)


SWAP = [
    (s * 32 + route(s, t)[0], t * 32 + route(s, t)[1]) for s in range(32) for t in range(32)
]


def on_device(fields, lagged_source, embed_weight, position, norm_gain, head_weight):
    core = lax.axis_index("core")
    mp = lax.axis_index("mp")
    seq = lax.axis_index("sq") * 2 + core
    x_axes = ("sq", "core")

    patches = lax.all_to_all(pack(fields), "mp", 0, 0, tiled=True)

    y_first, y_last = y_edges(fields)
    y_low = along(y_last, ("mp",), 1)
    y_high = along(y_first, ("mp",), -1)
    who = jnp.stack([seq, mp]).astype(jnp.int32)
    edges = jnp.stack([seq > 0, seq < 31, mp > 0, mp < 31]).astype(F32)
    weight = lax.dynamic_slice_in_dim(embed_weight, core * 1024, 1024, 0).reshape(2, 512, 1024)
    patches, who, edges, weight, y_low, y_high = lax.optimization_barrier(
        (patches, who, edges, weight, y_low, y_high)
    )

    patches = patches.reshape(16, 2, 16, 512)
    keep, send = embed(who, patches, weight)
    theirs = lax.ppermute(send, "core", [(0, 1), (1, 0)])
    partial_sums = (keep + theirs.astype(F32)).astype(BF16)
    pieces = lax.all_to_all(partial_sums, "mp", 0, 0, tiled=True)

    x_first, x_last = x_edges(fields, y_low, y_high)
    pieces, x_first, x_last = lax.optimization_barrier((pieces, x_first, x_last))

    rows = jnp.sum(pieces.astype(F32), 0)
    rows = lax.ppermute(rows, ALL, SWAP)
    everyone = norm(who, rows, position, norm_gain)
    normed = lax.all_to_all(everyone, "mp", 0, 0, tiled=True)

    x_low = along(x_last, x_axes, 1)
    x_high = along(x_first, x_axes, -1)
    edges, _ = lax.optimization_barrier((edges, everyone))
    fields_next = advance(edges, fields, lagged_source, y_low, y_high, x_low, x_high)
    normed, fields_next = lax.optimization_barrier((normed, fields_next))

    return fields_next, head(who, normed, head_weight)


def solution(mesh):
    split = Mesh(mesh.devices.reshape(16, 2, 32), ALL)
    seq = ("sq", "core")
    placed = (
        P(None, seq, "mp", None),
        P(None, seq, "mp", None),
        P("mp", None),
        P(seq, None),
        P(),
        P(None, "mp"),
    )
    return jax.shard_map(
        on_device,
        mesh=split,
        in_specs=placed,
        out_specs=(P(None, seq, "mp", None), P(seq, "mp")),
        check_vma=False,
    )
```

```python
import jax
import jax.numpy as jnp
from jax import lax
from jax.experimental import pallas as pl
from jax.experimental.pallas import tpu as pltpu
from jax.sharding import Mesh
from jax.sharding import PartitionSpec as P

PATCH = 16
time_step = 0.25
diffusivity = 0.2
epsilon = 1e-05

F32 = jnp.float32
BF16 = jnp.bfloat16
ALL = ("sq", "core", "mp")


def block_transpose(tiles):
    row = lax.broadcasted_iota(jnp.int32, (8, 128), 0)
    lane_block = lax.broadcasted_iota(jnp.int32, (8, 128), 1) // PATCH
    for s in (4, 2, 1):
        row_bit = (row // s) & 1
        keep, down = row_bit == ((lane_block // s) & 1), row_bit == 1
        after = [pltpu.roll(t, s, 0) for t in tiles]
        after = [pltpu.roll(t, 128 - PATCH * s, 1) for t in after]
        if s == 4:
            tiles = [jnp.where(keep, t, a) for t, a in zip(tiles, after)]
        else:
            before = [pltpu.roll(t, 8 - s, 0) for t in tiles]
            before = [pltpu.roll(t, PATCH * s, 1) for t in before]
            tiles = [
                jnp.where(keep, t, jnp.where(down, a, b)) for t, a, b in zip(tiles, after, before)
            ]
    return tiles


PACK_STEPS = 4


def pack_kernel(fields_hbm, packed_hbm, fields_ref, packed_ref, in_sem, out_sem):
    count = 16 // PACK_STEPS
    loads, stores = [], []
    for step in range(PACK_STEPS):
        some = pl.ds(step * count, count)
        loads.append(pltpu.make_async_copy(fields_hbm.at[some], fields_ref.at[some], in_sem.at[step]))
        some = pl.ds(step * 2 * count, 2 * count)
        stores.append(pltpu.make_async_copy(packed_ref.at[some], packed_hbm.at[some], out_sem.at[step]))
    for load in loads:
        load.start()
    for step in range(PACK_STEPS):
        loads[step].wait()
        places = [
            (step * count + k, half, g) for k in range(count) for half in range(2) for g in range(4)
        ]
        tiles = block_transpose(
            [
                fields_ref[f, half * 4 + g, :, c * 128 : (c + 1) * 128]
                for f, half, g in places
                for c in range(2)
            ]
        )
        for n, (f, half, g) in enumerate(places):
            both = jnp.concatenate(tiles[2 * n : 2 * n + 2], axis=0)
            packed_ref[f * 2 + half, :, g * 128 : (g + 1) * 128] = both.astype(BF16)
        stores[step].start()
    for store in stores:
        store.wait()


def pack(fields):
    return pl.pallas_call(
        pack_kernel,
        in_specs=[pl.BlockSpec(memory_space=pl.ANY)],
        out_specs=pl.BlockSpec(memory_space=pl.ANY),
        out_shape=jax.ShapeDtypeStruct((32, 16, 512), BF16),
        scratch_shapes=[
            pltpu.VMEM((16, 8, 8, 256), F32),
            pltpu.VMEM((32, 16, 512), BF16),
            pltpu.SemaphoreType.DMA((PACK_STEPS,)),
            pltpu.SemaphoreType.DMA((PACK_STEPS,)),
        ],
        cost_estimate=pl.CostEstimate(flops=1000000, bytes_accessed=2 << 20, transcendentals=0),
    )(fields)


VMEM = pl.BlockSpec(memory_space=pltpu.VMEM)
ROOM = pltpu.CompilerParams(vmem_limit_bytes=16 << 20)


def y_edge_kernel(fields_ref, first_ref, last_ref):
    for k in range(2):
        first_ref[k] = fields_ref[:, :, k, :].reshape(128, 256).astype(BF16)
        last_ref[k] = fields_ref[:, :, 6 + k, :].reshape(128, 256).astype(BF16)


def y_edges(fields):
    return pl.pallas_call(
        y_edge_kernel,
        in_specs=[VMEM],
        out_specs=[VMEM, VMEM],
        out_shape=[jax.ShapeDtypeStruct((2, 128, 256), BF16)] * 2,
        cost_estimate=pl.CostEstimate(flops=100000, bytes_accessed=2 << 20, transcendentals=0),
    )(fields)


def x_edge_kernel(head_ref, tail_ref, y_low_ref, y_high_ref, first_ref, last_ref, rows):
    rows[0] = y_low_ref[1].astype(F32)
    rows[1] = y_high_ref[0].astype(F32)
    for cells, out_ref, i in ((head_ref, first_ref, 0), (tail_ref, last_ref, 7)):
        for k in range(2):
            out_ref[k * 128 : (k + 1) * 128] = cells[:, k].reshape(128, 256).astype(BF16)
        for k in range(2):
            corner = rows[k].reshape(16, 8, 256)[:, i]
            out_ref[256 + k * 16 : 272 + k * 16] = corner.astype(BF16)


def x_edges(fields, y_low, y_high):
    return pl.pallas_call(
        x_edge_kernel,
        grid=(1,),
        in_specs=[
            pl.BlockSpec((16, 2, 8, 256), lambda n: (0, 0, 0, 0)),
            pl.BlockSpec((16, 2, 8, 256), lambda n: (0, 3, 0, 0)),
            pl.BlockSpec((2, 128, 256), lambda n: (0, 0, 0)),
            pl.BlockSpec((2, 128, 256), lambda n: (0, 0, 0)),
        ],
        out_specs=[pl.BlockSpec((288, 256), lambda n: (0, 0))] * 2,
        out_shape=[jax.ShapeDtypeStruct((288, 256), BF16)] * 2,
        scratch_shapes=[pltpu.VMEM((2, 128, 256), F32)],
        cost_estimate=pl.CostEstimate(flops=100000, bytes_accessed=1 << 20, transcendentals=0),
    )(fields, fields, y_low, y_high)


def route(s, t):
    z = ((t >> 2) - (s >> 2)) & 7
    differ = (s ^ t) & 1
    cross = ((s ^ t) >> 1) & 1
    near = 1 + differ
    m = z * 4 + near + cross * (2 * differ - 1)
    mu = z * 4 + near + cross * (2 - 4 * differ)
    return m, mu


def arrived_from(t, mu):
    y = ((t >> 2) - (mu >> 2)) & 7
    cross = 1 - ((mu ^ (mu >> 1)) & 1)
    differ = (mu & 1) ^ 1
    return y * 4 + (((t >> 1) ^ cross) & 1) * 2 + ((t ^ differ) & 1)


def embed_kernel(who_ref, patches_ref, weight_ref, keep_ref, send_hbm, send_ref, out_sem):
    seq = who_ref[0]
    other = (seq & 1) == 1
    left = [patches_ref[:, b].reshape(256, 512) for b in range(2)]
    size = 256
    stores = []
    for n in range(4):
        columns = pl.ds(n * size, size)
        total = jnp.dot(left[0], weight_ref[0, :, columns], preferred_element_type=F32)
        total = total + jnp.dot(left[1], weight_ref[1, :, columns], preferred_element_type=F32)
        total = total.reshape(16, 2, 8, size)
        for t in range(32):
            rows = total[t % 16, t // 16]
            rows = jnp.where(other, pltpu.roll(rows, 4, 0), rows)
            keep_ref[route(seq, t)[0], :, columns] = rows[0:4]
            send_ref[route(seq ^ 1, t)[0], :, columns] = rows[4:8].astype(BF16)
        store = pltpu.make_async_copy(
            send_ref.at[:, :, columns], send_hbm.at[:, :, columns], out_sem.at[n]
        )
        store.start()
        stores.append(store)
    for store in stores:
        store.wait()


def embed(who, patches, weight):
    return pl.pallas_call(
        embed_kernel,
        in_specs=[pl.BlockSpec(memory_space=pltpu.SMEM), VMEM, VMEM],
        out_specs=[VMEM, pl.BlockSpec(memory_space=pl.ANY)],
        out_shape=[
            jax.ShapeDtypeStruct((32, 4, 1024), F32),
            pltpu.HBM((32, 4, 1024), BF16),
        ],
        scratch_shapes=[pltpu.VMEM((32, 4, 1024), BF16), pltpu.SemaphoreType.DMA((4,))],
        compiler_params=ROOM,
        cost_estimate=pl.CostEstimate(flops=540000000, bytes_accessed=3 << 20, transcendentals=0),
    )(who, patches, weight)


def norm_kernel(who_ref, rows_ref, position_ref, gain_ref, out_ref):
    part = arrived_from(who_ref[0], who_ref[1]) & 3
    block = position_ref[...].astype(F32).reshape(4, 4, 1024)
    hidden = rows_ref[...]
    for k in range(4):
        hidden = hidden + jnp.where(part == k, block[k], 0.0)
    row_mean = jnp.mean(hidden, -1, keepdims=True)
    row_square = jnp.mean(hidden * hidden, -1, keepdims=True)
    variance = row_square - row_mean * row_mean
    normed = (hidden - row_mean) * lax.rsqrt(variance + epsilon) * gain_ref[...]
    out_ref[...] = jnp.broadcast_to(normed.astype(BF16)[None], (32, 4, 1024))


def norm(who, rows, position, norm_gain):
    return pl.pallas_call(
        norm_kernel,
        grid_spec=pltpu.PrefetchScalarGridSpec(
            num_scalar_prefetch=1,
            grid=(1,),
            in_specs=[
                pl.BlockSpec((4, 1024), lambda n, who: (0, 0)),
                pl.BlockSpec((16, 1024), lambda n, who: (arrived_from(who[0], who[1]) >> 2, 0)),
                pl.BlockSpec((1, 1024), lambda n, who: (0, 0)),
            ],
            out_specs=pl.BlockSpec((32, 4, 1024), lambda n, who: (0, 0, 0)),
        ),
        out_shape=jax.ShapeDtypeStruct((32, 4, 1024), BF16),
        compiler_params=ROOM,
        cost_estimate=pl.CostEstimate(flops=100000, bytes_accessed=300000, transcendentals=0),
    )(who, rows, position, norm_gain.reshape(1, 1024))


def head_kernel(who_ref, normed_ref, weight_ref, out_hbm, out_ref, out_sem):
    gathered = normed_ref[...].astype(F32).reshape(128, 1024).astype(BF16)
    row = lax.broadcasted_iota(jnp.int32, (128, 128), 0)
    column = lax.broadcasted_iota(jnp.int32, (128, 128), 1)
    _, mu = route(row >> 2, who_ref[0])
    order = jnp.where(column == mu * 4 + (row & 3), 1.0, 0.0).astype(BF16)
    left = jnp.dot(order, gathered, preferred_element_type=F32).astype(BF16)
    stores = []
    for n, (start, size) in enumerate(HEAD_COLUMNS):
        columns = pl.ds(start, size)
        product = jnp.dot(left, weight_ref[:, columns], preferred_element_type=F32)
        out_ref[:, columns] = product.astype(BF16)
        store = pltpu.make_async_copy(out_ref.at[:, columns], out_hbm.at[:, columns], out_sem.at[n])
        store.start()
        stores.append(store)
    for store in stores:
        store.wait()


HEAD_COLUMNS = ((0, 512), (512, 512), (1024, 384))


def head(who, normed, head_weight):
    return pl.pallas_call(
        head_kernel,
        in_specs=[pl.BlockSpec(memory_space=pltpu.SMEM), VMEM, VMEM],
        out_specs=pl.BlockSpec(memory_space=pl.ANY),
        out_shape=jax.ShapeDtypeStruct((128, 1408), BF16),
        scratch_shapes=[
            pltpu.VMEM((128, 1408), BF16),
            pltpu.SemaphoreType.DMA((len(HEAD_COLUMNS),)),
        ],
        compiler_params=ROOM,
        cost_estimate=pl.CostEstimate(flops=370000000, bytes_accessed=4 << 20, transcendentals=0),
    )(who, normed, head_weight)


def advance_kernel(
    edge_ref, fields_ref, source_ref, yl_ref, yh_ref, xl_ref, xh_ref,
    out_ref, ylo, yhi, xlo, xhi, clo, chi, one_ref, face_ref,
):
    ylo[...] = yl_ref[...].astype(F32)
    yhi[...] = yh_ref[...].astype(F32)
    for payload, cells, corners in ((xl_ref, xlo, clo), (xh_ref, xhi, chi)):
        cells[...] = payload[0:256].astype(F32).reshape(2, 128, 256)
        corners[...] = payload[256:288].astype(F32).reshape(2, 16, 256)
    row = lax.broadcasted_iota(jnp.int32, (8, 256), 0)
    lane = lax.broadcasted_iota(jnp.int32, (8, 256), 1)
    first_row, last_row = row == 0, row == 7
    first_lane, last_lane = lane == 0, lane == 255

    def shifted(tile, low, high):
        before = jnp.where(first_row, low, pltpu.roll(tile, 1, 0))
        after = jnp.where(last_row, high, pltpu.roll(tile, 7, 0))
        return before, after

    def tendency(centre, velocity, xm, xp, ym, yp):
        zm = jnp.where(first_lane, 0.0, pltpu.roll(centre, 1, 1))
        zp = jnp.where(last_lane, 0.0, pltpu.roll(centre, 255, 1))
        laplacian = xp + xm + yp + ym + zp + zm - 6.0 * centre
        advection = velocity[0] * (xp - xm) + velocity[1] * (yp - ym) + velocity[2] * (zp - zm)
        return diffusivity * laplacian - 0.5 * advection

    def at8(f):
        return pl.ds(pl.multiple_of(f * 8, 8), 8)

    def first_stage(f, carry):
        mine = at8(f)
        for i in range(8):
            centre = fields_ref[f, i]
            xm = fields_ref[f, i - 1] if i > 0 else xlo[1, mine]
            xp = fields_ref[f, i + 1] if i < 7 else xhi[0, mine]
            low = ylo[1, pl.ds(f * 8 + i, 1)]
            high = yhi[0, pl.ds(f * 8 + i, 1)]
            ym, yp = shifted(centre, low, high)
            velocity = [fields_ref[k, i] for k in range(3)]
            one_ref[f, i] = centre + time_step * tendency(centre, velocity, xm, xp, ym, yp)
        for side in range(2):
            halo = xlo if side == 0 else xhi
            corner = clo if side == 0 else chi
            near = 1 if side == 0 else 0
            centre = halo[near, mine]
            outer = halo[1 - near, mine]
            inner = fields_ref[f, 0 if side == 0 else 7]
            xm, xp = (outer, inner) if side == 0 else (inner, outer)
            ym, yp = shifted(centre, corner[0, pl.ds(f, 1)], corner[1, pl.ds(f, 1)])
            velocity = [halo[near, k * 8 : k * 8 + 8] for k in range(3)]
            value = centre + time_step * tendency(centre, velocity, xm, xp, ym, yp)
            face_ref[side, mine] = value * edge_ref[side]
        for side in range(2):
            halo = ylo if side == 0 else yhi
            near = 1 if side == 0 else 0
            centre = halo[near, mine]
            outer = halo[1 - near, mine]
            inner = fields_ref[f, :, 0 if side == 0 else 7, :]
            ym, yp = (outer, inner) if side == 0 else (inner, outer)
            xm, xp = shifted(centre, clo[side, pl.ds(f, 1)], chi[side, pl.ds(f, 1)])
            velocity = [halo[near, k * 8 : k * 8 + 8] for k in range(3)]
            value = centre + time_step * tendency(centre, velocity, xm, xp, ym, yp)
            face_ref[2 + side, mine] = value * edge_ref[2 + side]
        return carry

    lax.fori_loop(0, 16, first_stage, 0)

    def second_stage(f, with_source):
        mine = at8(f)
        for i in range(8):
            centre = one_ref[f, i]
            xm = one_ref[f, i - 1] if i > 0 else face_ref[0, mine]
            xp = one_ref[f, i + 1] if i < 7 else face_ref[1, mine]
            low = face_ref[2, pl.ds(f * 8 + i, 1)]
            high = face_ref[3, pl.ds(f * 8 + i, 1)]
            ym, yp = shifted(centre, low, high)
            velocity = [one_ref[k, i] for k in range(3)]
            value = 0.5 * (fields_ref[f, i] + centre + time_step * tendency(centre, velocity, xm, xp, ym, yp))
            if with_source:
                value = value + time_step * source_ref[f - 3, i].astype(F32)
            out_ref[f, i] = value

    for f in range(3):
        second_stage(f, False)

    def species(f, carry):
        second_stage(f, True)
        return carry

    lax.fori_loop(3, 16, species, 0)


def advance(edges, fields, lagged_source, y_low, y_high, x_low, x_high):
    return pl.pallas_call(
        advance_kernel,
        in_specs=[pl.BlockSpec(memory_space=pltpu.SMEM)] + [VMEM] * 6,
        out_specs=VMEM,
        out_shape=jax.ShapeDtypeStruct((16, 8, 8, 256), F32),
        scratch_shapes=[pltpu.VMEM((2, 128, 256), F32)] * 4
        + [pltpu.VMEM((2, 16, 256), F32)] * 2
        + [pltpu.VMEM((16, 8, 8, 256), F32), pltpu.VMEM((4, 128, 256), F32)],
        cost_estimate=pl.CostEstimate(flops=100000000, bytes_accessed=4 << 20, transcendentals=0),
    )(edges, fields, lagged_source, y_low, y_high, x_low, x_high)


def along(value, axes, step):
    count = 1
    for axis in axes:
        count *= lax.axis_size(axis)
    pairs = [(i, i + step) for i in range(count) if 0 <= i + step < count]
    return lax.ppermute(value, axes, pairs)


SWAP = [
    (s * 32 + route(s, t)[0], t * 32 + route(s, t)[1]) for s in range(32) for t in range(32)
]


def on_device(fields, lagged_source, embed_weight, position, norm_gain, head_weight):
    core = lax.axis_index("core")
    mp = lax.axis_index("mp")
    seq = lax.axis_index("sq") * 2 + core
    x_axes = ("sq", "core")

    patches = lax.all_to_all(pack(fields), "mp", 0, 0, tiled=True)

    y_first, y_last = y_edges(fields)
    y_low = along(y_last, ("mp",), 1)
    y_high = along(y_first, ("mp",), -1)
    who = jnp.stack([seq, mp]).astype(jnp.int32)
    edges = jnp.stack([seq > 0, seq < 31, mp > 0, mp < 31]).astype(F32)
    weight = lax.dynamic_slice_in_dim(embed_weight, core * 1024, 1024, 0).reshape(2, 512, 1024)
    x_first, x_last = x_edges(fields, y_low, y_high)
    patches, who, edges, weight, x_first, x_last = lax.optimization_barrier(
        (patches, who, edges, weight, x_first, x_last)
    )

    patches = patches.reshape(16, 2, 16, 512)
    keep, send = embed(who, patches, weight)
    theirs = lax.ppermute(send, "core", [(0, 1), (1, 0)])
    partial_sums = (keep + theirs.astype(F32)).astype(BF16)
    pieces = lax.all_to_all(partial_sums, "mp", 0, 0, tiled=True)

    x_low = along(x_last, x_axes, 1)
    x_high = along(x_first, x_axes, -1)

    rows = jnp.sum(pieces.astype(F32), 0)
    rows = lax.ppermute(rows, ALL, SWAP)
    rows, x_low, x_high = lax.optimization_barrier((rows, x_low, x_high))
    everyone = norm(who, rows, position, norm_gain)
    normed = lax.all_to_all(everyone, "mp", 0, 0, tiled=True)

    edges, _ = lax.optimization_barrier((edges, everyone))
    fields_next = advance(edges, fields, lagged_source, y_low, y_high, x_low, x_high)
    normed, fields_next = lax.optimization_barrier((normed, fields_next))

    return fields_next, head(who, normed, head_weight)


def solution(mesh):
    split = Mesh(mesh.devices.reshape(16, 2, 32), ALL)
    seq = ("sq", "core")
    placed = (
        P(None, seq, "mp", None),
        P(None, seq, "mp", None),
        P("mp", None),
        P(seq, None),
        P(),
        P(None, "mp"),
    )
    return jax.shard_map(
        on_device,
        mesh=split,
        in_specs=placed,
        out_specs=(P(None, seq, "mp", None), P(seq, "mp")),
        check_vma=False,
    )
```

```python
import jax
import jax.numpy as jnp
from jax import lax
from jax.experimental import pallas as pl
from jax.experimental.pallas import tpu as pltpu
from jax.sharding import Mesh
from jax.sharding import PartitionSpec as P

PATCH = 16
time_step = 0.25
diffusivity = 0.2
epsilon = 1e-05

F32 = jnp.float32
BF16 = jnp.bfloat16
ALL = ("sq", "core", "mp")


def block_transpose(tiles):
    row = lax.broadcasted_iota(jnp.int32, (8, 128), 0)
    lane_block = lax.broadcasted_iota(jnp.int32, (8, 128), 1) // PATCH
    for s in (4, 2, 1):
        row_bit = (row // s) & 1
        keep, down = row_bit == ((lane_block // s) & 1), row_bit == 1
        after = [pltpu.roll(t, s, 0) for t in tiles]
        after = [pltpu.roll(t, 128 - PATCH * s, 1) for t in after]
        if s == 4:
            tiles = [jnp.where(keep, t, a) for t, a in zip(tiles, after)]
        else:
            before = [pltpu.roll(t, 8 - s, 0) for t in tiles]
            before = [pltpu.roll(t, PATCH * s, 1) for t in before]
            tiles = [
                jnp.where(keep, t, jnp.where(down, a, b)) for t, a, b in zip(tiles, after, before)
            ]
    return tiles


PACK_STEPS = 4


def pack_kernel(fields_hbm, packed_hbm, fields_ref, packed_ref, in_sem, out_sem):
    count = 16 // PACK_STEPS
    loads, stores = [], []
    for step in range(PACK_STEPS):
        some = pl.ds(step * count, count)
        loads.append(pltpu.make_async_copy(fields_hbm.at[some], fields_ref.at[some], in_sem.at[step]))
        some = pl.ds(step * 2 * count, 2 * count)
        stores.append(pltpu.make_async_copy(packed_ref.at[some], packed_hbm.at[some], out_sem.at[step]))
    for load in loads:
        load.start()
    for step in range(PACK_STEPS):
        loads[step].wait()
        places = [
            (step * count + k, half, g) for k in range(count) for half in range(2) for g in range(4)
        ]
        tiles = block_transpose(
            [
                fields_ref[f, half * 4 + g, :, c * 128 : (c + 1) * 128]
                for f, half, g in places
                for c in range(2)
            ]
        )
        for n, (f, half, g) in enumerate(places):
            both = jnp.concatenate(tiles[2 * n : 2 * n + 2], axis=0)
            packed_ref[f * 2 + half, :, g * 128 : (g + 1) * 128] = both.astype(BF16)
        stores[step].start()
    for store in stores:
        store.wait()


def pack(fields):
    return pl.pallas_call(
        pack_kernel,
        in_specs=[pl.BlockSpec(memory_space=pl.ANY)],
        out_specs=pl.BlockSpec(memory_space=pl.ANY),
        out_shape=jax.ShapeDtypeStruct((32, 16, 512), BF16),
        scratch_shapes=[
            pltpu.VMEM((16, 8, 8, 256), F32),
            pltpu.VMEM((32, 16, 512), BF16),
            pltpu.SemaphoreType.DMA((PACK_STEPS,)),
            pltpu.SemaphoreType.DMA((PACK_STEPS,)),
        ],
        cost_estimate=pl.CostEstimate(flops=1000000, bytes_accessed=2 << 20, transcendentals=0),
    )(fields)


VMEM = pl.BlockSpec(memory_space=pltpu.VMEM)
ROOM = pltpu.CompilerParams(vmem_limit_bytes=16 << 20)


def y_edge_kernel(fields_ref, first_ref, last_ref):
    for k in range(2):
        first_ref[k] = fields_ref[:, :, k, :].reshape(128, 256).astype(BF16)
        last_ref[k] = fields_ref[:, :, 6 + k, :].reshape(128, 256).astype(BF16)


def y_edges(fields):
    return pl.pallas_call(
        y_edge_kernel,
        in_specs=[VMEM],
        out_specs=[VMEM, VMEM],
        out_shape=[jax.ShapeDtypeStruct((2, 128, 256), BF16)] * 2,
        cost_estimate=pl.CostEstimate(flops=100000, bytes_accessed=2 << 20, transcendentals=0),
    )(fields)


def x_edge_kernel(head_ref, tail_ref, y_low_ref, y_high_ref, first_ref, last_ref, rows):
    rows[0] = y_low_ref[1].astype(F32)
    rows[1] = y_high_ref[0].astype(F32)
    for cells, out_ref, i in ((head_ref, first_ref, 0), (tail_ref, last_ref, 7)):
        for k in range(2):
            out_ref[k * 128 : (k + 1) * 128] = cells[:, k].reshape(128, 256).astype(BF16)
        for k in range(2):
            corner = rows[k].reshape(16, 8, 256)[:, i]
            out_ref[256 + k * 16 : 272 + k * 16] = corner.astype(BF16)


def x_edges(fields, y_low, y_high):
    return pl.pallas_call(
        x_edge_kernel,
        grid=(1,),
        in_specs=[
            pl.BlockSpec((16, 2, 8, 256), lambda n: (0, 0, 0, 0)),
            pl.BlockSpec((16, 2, 8, 256), lambda n: (0, 3, 0, 0)),
            pl.BlockSpec((2, 128, 256), lambda n: (0, 0, 0)),
            pl.BlockSpec((2, 128, 256), lambda n: (0, 0, 0)),
        ],
        out_specs=[pl.BlockSpec((288, 256), lambda n: (0, 0))] * 2,
        out_shape=[jax.ShapeDtypeStruct((288, 256), BF16)] * 2,
        scratch_shapes=[pltpu.VMEM((2, 128, 256), F32)],
        cost_estimate=pl.CostEstimate(flops=100000, bytes_accessed=1 << 20, transcendentals=0),
    )(fields, fields, y_low, y_high)


def route(s, t):
    z = ((t >> 2) - (s >> 2)) & 7
    differ = (s ^ t) & 1
    cross = ((s ^ t) >> 1) & 1
    near = 1 + differ
    m = z * 4 + near + cross * (2 * differ - 1)
    mu = z * 4 + near + cross * (2 - 4 * differ)
    return m, mu


def arrived_from(t, mu):
    y = ((t >> 2) - (mu >> 2)) & 7
    cross = 1 - ((mu ^ (mu >> 1)) & 1)
    differ = (mu & 1) ^ 1
    return y * 4 + (((t >> 1) ^ cross) & 1) * 2 + ((t ^ differ) & 1)


def embed_kernel(who_ref, patches_ref, weight_ref, keep_ref, send_hbm, send_ref, out_sem):
    seq = who_ref[0]
    other = (seq & 1) == 1
    left = [patches_ref[:, b].reshape(256, 512) for b in range(2)]
    size = 256
    stores = []
    for n in range(4):
        columns = pl.ds(n * size, size)
        total = jnp.dot(left[0], weight_ref[0, :, columns], preferred_element_type=F32)
        total = total + jnp.dot(left[1], weight_ref[1, :, columns], preferred_element_type=F32)
        total = total.reshape(16, 2, 8, size)
        for t in range(32):
            rows = total[t % 16, t // 16]
            rows = jnp.where(other, pltpu.roll(rows, 4, 0), rows)
            keep_ref[route(seq, t)[0], :, columns] = rows[0:4]
            send_ref[route(seq ^ 1, t)[0], :, columns] = rows[4:8].astype(BF16)
        store = pltpu.make_async_copy(
            send_ref.at[:, :, columns], send_hbm.at[:, :, columns], out_sem.at[n]
        )
        store.start()
        stores.append(store)
    for store in stores:
        store.wait()


def embed(who, patches, weight):
    return pl.pallas_call(
        embed_kernel,
        in_specs=[pl.BlockSpec(memory_space=pltpu.SMEM), VMEM, VMEM],
        out_specs=[VMEM, pl.BlockSpec(memory_space=pl.ANY)],
        out_shape=[
            jax.ShapeDtypeStruct((32, 4, 1024), F32),
            pltpu.HBM((32, 4, 1024), BF16),
        ],
        scratch_shapes=[pltpu.VMEM((32, 4, 1024), BF16), pltpu.SemaphoreType.DMA((4,))],
        compiler_params=ROOM,
        cost_estimate=pl.CostEstimate(flops=540000000, bytes_accessed=3 << 20, transcendentals=0),
    )(who, patches, weight)


def norm_kernel(who_ref, rows_ref, position_ref, gain_ref, out_ref):
    part = arrived_from(who_ref[0], who_ref[1]) & 3
    block = position_ref[...].astype(F32).reshape(4, 4, 1024)
    hidden = rows_ref[...]
    for k in range(4):
        hidden = hidden + jnp.where(part == k, block[k], 0.0)
    row_mean = jnp.mean(hidden, -1, keepdims=True)
    row_square = jnp.mean(hidden * hidden, -1, keepdims=True)
    variance = row_square - row_mean * row_mean
    normed = (hidden - row_mean) * lax.rsqrt(variance + epsilon) * gain_ref[...]
    out_ref[...] = jnp.broadcast_to(normed.astype(BF16)[None], (32, 4, 1024))


def norm(who, rows, position, norm_gain):
    return pl.pallas_call(
        norm_kernel,
        grid_spec=pltpu.PrefetchScalarGridSpec(
            num_scalar_prefetch=1,
            grid=(1,),
            in_specs=[
                pl.BlockSpec((4, 1024), lambda n, who: (0, 0)),
                pl.BlockSpec((16, 1024), lambda n, who: (arrived_from(who[0], who[1]) >> 2, 0)),
                pl.BlockSpec((1, 1024), lambda n, who: (0, 0)),
            ],
            out_specs=pl.BlockSpec((32, 4, 1024), lambda n, who: (0, 0, 0)),
        ),
        out_shape=jax.ShapeDtypeStruct((32, 4, 1024), BF16),
        compiler_params=ROOM,
        cost_estimate=pl.CostEstimate(flops=100000, bytes_accessed=300000, transcendentals=0),
    )(who, rows, position, norm_gain.reshape(1, 1024))


def head_kernel(who_ref, normed_ref, weight_ref, out_hbm, out_ref, out_sem):
    gathered = normed_ref[...].astype(F32).reshape(128, 1024).astype(BF16)
    row = lax.broadcasted_iota(jnp.int32, (128, 128), 0)
    column = lax.broadcasted_iota(jnp.int32, (128, 128), 1)
    _, mu = route(row >> 2, who_ref[0])
    order = jnp.where(column == mu * 4 + (row & 3), 1.0, 0.0).astype(BF16)
    left = jnp.dot(order, gathered, preferred_element_type=F32).astype(BF16)
    stores = []
    for n, (start, size) in enumerate(HEAD_COLUMNS):
        columns = pl.ds(start, size)
        product = jnp.dot(left, weight_ref[:, columns], preferred_element_type=F32)
        out_ref[:, columns] = product.astype(BF16)
        store = pltpu.make_async_copy(out_ref.at[:, columns], out_hbm.at[:, columns], out_sem.at[n])
        store.start()
        stores.append(store)
    for store in stores:
        store.wait()


HEAD_COLUMNS = ((0, 512), (512, 512), (1024, 384))


def head(who, normed, head_weight):
    return pl.pallas_call(
        head_kernel,
        in_specs=[pl.BlockSpec(memory_space=pltpu.SMEM), VMEM, VMEM],
        out_specs=pl.BlockSpec(memory_space=pl.ANY),
        out_shape=jax.ShapeDtypeStruct((128, 1408), BF16),
        scratch_shapes=[
            pltpu.VMEM((128, 1408), BF16),
            pltpu.SemaphoreType.DMA((len(HEAD_COLUMNS),)),
        ],
        compiler_params=ROOM,
        cost_estimate=pl.CostEstimate(flops=370000000, bytes_accessed=4 << 20, transcendentals=0),
    )(who, normed, head_weight)


def advance_kernel(
    edge_ref, fields_ref, source_ref, yl_ref, yh_ref, xl_ref, xh_ref,
    out_ref, ylo, yhi, xlo, xhi, clo, chi, one_ref, face_ref,
):
    ylo[...] = yl_ref[...].astype(F32)
    yhi[...] = yh_ref[...].astype(F32)
    for payload, cells, corners in ((xl_ref, xlo, clo), (xh_ref, xhi, chi)):
        cells[...] = payload[0:256].astype(F32).reshape(2, 128, 256)
        corners[...] = payload[256:288].astype(F32).reshape(2, 16, 256)
    row = lax.broadcasted_iota(jnp.int32, (8, 256), 0)
    lane = lax.broadcasted_iota(jnp.int32, (8, 256), 1)
    first_row, last_row = row == 0, row == 7
    first_lane, last_lane = lane == 0, lane == 255

    def shifted(tile, low, high):
        before = jnp.where(first_row, low, pltpu.roll(tile, 1, 0))
        after = jnp.where(last_row, high, pltpu.roll(tile, 7, 0))
        return before, after

    def tendency(centre, velocity, xm, xp, ym, yp):
        zm = jnp.where(first_lane, 0.0, pltpu.roll(centre, 1, 1))
        zp = jnp.where(last_lane, 0.0, pltpu.roll(centre, 255, 1))
        laplacian = xp + xm + yp + ym + zp + zm - 6.0 * centre
        advection = velocity[0] * (xp - xm) + velocity[1] * (yp - ym) + velocity[2] * (zp - zm)
        return diffusivity * laplacian - 0.5 * advection

    def at8(f):
        return pl.ds(pl.multiple_of(f * 8, 8), 8)

    def first_stage(f, carry):
        mine = at8(f)
        for i in range(8):
            centre = fields_ref[f, i]
            xm = fields_ref[f, i - 1] if i > 0 else xlo[1, mine]
            xp = fields_ref[f, i + 1] if i < 7 else xhi[0, mine]
            low = ylo[1, pl.ds(f * 8 + i, 1)]
            high = yhi[0, pl.ds(f * 8 + i, 1)]
            ym, yp = shifted(centre, low, high)
            velocity = [fields_ref[k, i] for k in range(3)]
            one_ref[f, i] = centre + time_step * tendency(centre, velocity, xm, xp, ym, yp)
        for side in range(2):
            halo = xlo if side == 0 else xhi
            corner = clo if side == 0 else chi
            near = 1 if side == 0 else 0
            centre = halo[near, mine]
            outer = halo[1 - near, mine]
            inner = fields_ref[f, 0 if side == 0 else 7]
            xm, xp = (outer, inner) if side == 0 else (inner, outer)
            ym, yp = shifted(centre, corner[0, pl.ds(f, 1)], corner[1, pl.ds(f, 1)])
            velocity = [halo[near, k * 8 : k * 8 + 8] for k in range(3)]
            value = centre + time_step * tendency(centre, velocity, xm, xp, ym, yp)
            face_ref[side, mine] = value * edge_ref[side]
        for side in range(2):
            halo = ylo if side == 0 else yhi
            near = 1 if side == 0 else 0
            centre = halo[near, mine]
            outer = halo[1 - near, mine]
            inner = fields_ref[f, :, 0 if side == 0 else 7, :]
            ym, yp = (outer, inner) if side == 0 else (inner, outer)
            xm, xp = shifted(centre, clo[side, pl.ds(f, 1)], chi[side, pl.ds(f, 1)])
            velocity = [halo[near, k * 8 : k * 8 + 8] for k in range(3)]
            value = centre + time_step * tendency(centre, velocity, xm, xp, ym, yp)
            face_ref[2 + side, mine] = value * edge_ref[2 + side]
        return carry

    lax.fori_loop(0, 16, first_stage, 0)

    def second_stage(f, with_source):
        mine = at8(f)
        for i in range(8):
            centre = one_ref[f, i]
            xm = one_ref[f, i - 1] if i > 0 else face_ref[0, mine]
            xp = one_ref[f, i + 1] if i < 7 else face_ref[1, mine]
            low = face_ref[2, pl.ds(f * 8 + i, 1)]
            high = face_ref[3, pl.ds(f * 8 + i, 1)]
            ym, yp = shifted(centre, low, high)
            velocity = [one_ref[k, i] for k in range(3)]
            value = 0.5 * (fields_ref[f, i] + centre + time_step * tendency(centre, velocity, xm, xp, ym, yp))
            if with_source:
                value = value + time_step * source_ref[f - 3, i].astype(F32)
            out_ref[f, i] = value

    for f in range(3):
        second_stage(f, False)

    def species(f, carry):
        second_stage(f, True)
        return carry

    lax.fori_loop(3, 16, species, 0)


def advance(edges, fields, lagged_source, y_low, y_high, x_low, x_high):
    return pl.pallas_call(
        advance_kernel,
        in_specs=[pl.BlockSpec(memory_space=pltpu.SMEM)] + [VMEM] * 6,
        out_specs=VMEM,
        out_shape=jax.ShapeDtypeStruct((16, 8, 8, 256), F32),
        scratch_shapes=[pltpu.VMEM((2, 128, 256), F32)] * 4
        + [pltpu.VMEM((2, 16, 256), F32)] * 2
        + [pltpu.VMEM((16, 8, 8, 256), F32), pltpu.VMEM((4, 128, 256), F32)],
        cost_estimate=pl.CostEstimate(flops=100000000, bytes_accessed=4 << 20, transcendentals=0),
    )(edges, fields, lagged_source, y_low, y_high, x_low, x_high)


def along(value, axes, step):
    count = 1
    for axis in axes:
        count *= lax.axis_size(axis)
    pairs = [(i, i + step) for i in range(count) if 0 <= i + step < count]
    return lax.ppermute(value, axes, pairs)


SWAP = [
    (s * 32 + route(s, t)[0], t * 32 + route(s, t)[1]) for s in range(32) for t in range(32)
]


def on_device(fields, lagged_source, embed_weight, position, norm_gain, head_weight):
    core = lax.axis_index("core")
    mp = lax.axis_index("mp")
    seq = lax.axis_index("sq") * 2 + core
    x_axes = ("sq", "core")

    patches = lax.all_to_all(pack(fields), "mp", 0, 0, tiled=True)

    y_first, y_last = y_edges(fields)
    y_low = along(y_last, ("mp",), 1)
    y_high = along(y_first, ("mp",), -1)
    who = jnp.stack([seq, mp]).astype(jnp.int32)
    edges = jnp.stack([seq > 0, seq < 31, mp > 0, mp < 31]).astype(F32)
    weight = lax.dynamic_slice_in_dim(embed_weight, core * 1024, 1024, 0).reshape(2, 512, 1024)
    patches, who, edges, weight, y_low, y_high = lax.optimization_barrier(
        (patches, who, edges, weight, y_low, y_high)
    )

    patches = patches.reshape(16, 2, 16, 512)
    keep, send = embed(who, patches, weight)
    theirs = lax.ppermute(send, "core", [(0, 1), (1, 0)])
    partial_sums = (keep + theirs.astype(F32)).astype(BF16)
    pieces = lax.all_to_all(partial_sums, "mp", 0, 0, tiled=True)

    x_first, x_last = x_edges(fields, y_low, y_high)
    x_low = along(x_last, x_axes, 1)
    x_high = along(x_first, x_axes, -1)

    rows = jnp.sum(pieces.astype(F32), 0)
    rows = lax.ppermute(rows, ALL, SWAP)
    rows, x_low, x_high = lax.optimization_barrier((rows, x_low, x_high))
    everyone = norm(who, rows, position, norm_gain)
    normed = lax.all_to_all(everyone, "mp", 0, 0, tiled=True)

    edges, _ = lax.optimization_barrier((edges, everyone))
    fields_next = advance(edges, fields, lagged_source, y_low, y_high, x_low, x_high)
    normed, fields_next = lax.optimization_barrier((normed, fields_next))

    return fields_next, head(who, normed, head_weight)


def solution(mesh):
    split = Mesh(mesh.devices.reshape(16, 2, 32), ALL)
    seq = ("sq", "core")
    placed = (
        P(None, seq, "mp", None),
        P(None, seq, "mp", None),
        P("mp", None),
        P(seq, None),
        P(),
        P(None, "mp"),
    )
    return jax.shard_map(
        on_device,
        mesh=split,
        in_specs=placed,
        out_specs=(P(None, seq, "mp", None), P(seq, "mp")),
        check_vma=False,
    )
```

```python
import jax
import jax.numpy as jnp
from jax import lax
from jax.experimental import pallas as pl
from jax.experimental.pallas import tpu as pltpu
from jax.sharding import Mesh
from jax.sharding import PartitionSpec as P

PATCH = 16
time_step = 0.25
diffusivity = 0.2
epsilon = 1e-05

F32 = jnp.float32
BF16 = jnp.bfloat16
ALL = ("sq", "core", "mp")


def block_transpose(tiles):
    row = lax.broadcasted_iota(jnp.int32, (8, 128), 0)
    lane_block = lax.broadcasted_iota(jnp.int32, (8, 128), 1) // PATCH
    for s in (4, 2, 1):
        row_bit = (row // s) & 1
        keep, down = row_bit == ((lane_block // s) & 1), row_bit == 1
        after = [pltpu.roll(t, s, 0) for t in tiles]
        after = [pltpu.roll(t, 128 - PATCH * s, 1) for t in after]
        if s == 4:
            tiles = [jnp.where(keep, t, a) for t, a in zip(tiles, after)]
        else:
            before = [pltpu.roll(t, 8 - s, 0) for t in tiles]
            before = [pltpu.roll(t, PATCH * s, 1) for t in before]
            tiles = [
                jnp.where(keep, t, jnp.where(down, a, b)) for t, a, b in zip(tiles, after, before)
            ]
    return tiles


PACK_STEPS = 4


def pack_kernel(fields_hbm, packed_hbm, fields_ref, packed_ref, in_sem, out_sem):
    count = 16 // PACK_STEPS
    loads, stores = [], []
    for step in range(PACK_STEPS):
        some = pl.ds(step * count, count)
        loads.append(pltpu.make_async_copy(fields_hbm.at[some], fields_ref.at[some], in_sem.at[step]))
        some = pl.ds(step * 2 * count, 2 * count)
        stores.append(pltpu.make_async_copy(packed_ref.at[some], packed_hbm.at[some], out_sem.at[step]))
    for load in loads:
        load.start()
    for step in range(PACK_STEPS):
        loads[step].wait()
        places = [
            (step * count + k, half, g) for k in range(count) for half in range(2) for g in range(4)
        ]
        tiles = block_transpose(
            [
                fields_ref[f, half * 4 + g, :, c * 128 : (c + 1) * 128]
                for f, half, g in places
                for c in range(2)
            ]
        )
        for n, (f, half, g) in enumerate(places):
            both = jnp.concatenate(tiles[2 * n : 2 * n + 2], axis=0)
            packed_ref[f * 2 + half, :, g * 128 : (g + 1) * 128] = both.astype(BF16)
        stores[step].start()
    for store in stores:
        store.wait()


def pack(fields):
    return pl.pallas_call(
        pack_kernel,
        in_specs=[pl.BlockSpec(memory_space=pl.ANY)],
        out_specs=pl.BlockSpec(memory_space=pl.ANY),
        out_shape=jax.ShapeDtypeStruct((32, 16, 512), BF16),
        scratch_shapes=[
            pltpu.VMEM((16, 8, 8, 256), F32),
            pltpu.VMEM((32, 16, 512), BF16),
            pltpu.SemaphoreType.DMA((PACK_STEPS,)),
            pltpu.SemaphoreType.DMA((PACK_STEPS,)),
        ],
        cost_estimate=pl.CostEstimate(flops=1000000, bytes_accessed=2 << 20, transcendentals=0),
    )(fields)


VMEM = pl.BlockSpec(memory_space=pltpu.VMEM)
ROOM = pltpu.CompilerParams(vmem_limit_bytes=16 << 20)


def y_edge_kernel(fields_ref, first_ref, last_ref):
    for k in range(2):
        first_ref[k] = fields_ref[:, :, k, :].reshape(128, 256).astype(BF16)
        last_ref[k] = fields_ref[:, :, 6 + k, :].reshape(128, 256).astype(BF16)


def y_edges(fields):
    return pl.pallas_call(
        y_edge_kernel,
        in_specs=[VMEM],
        out_specs=[VMEM, VMEM],
        out_shape=[jax.ShapeDtypeStruct((2, 128, 256), BF16)] * 2,
        cost_estimate=pl.CostEstimate(flops=100000, bytes_accessed=2 << 20, transcendentals=0),
    )(fields)


def x_edge_kernel(head_ref, tail_ref, y_low_ref, y_high_ref, first_ref, last_ref, rows):
    rows[0] = y_low_ref[1].astype(F32)
    rows[1] = y_high_ref[0].astype(F32)
    for cells, out_ref, i in ((head_ref, first_ref, 0), (tail_ref, last_ref, 7)):
        for k in range(2):
            out_ref[k * 128 : (k + 1) * 128] = cells[:, k].reshape(128, 256).astype(BF16)
        for k in range(2):
            corner = rows[k].reshape(16, 8, 256)[:, i]
            out_ref[256 + k * 16 : 272 + k * 16] = corner.astype(BF16)


def x_edges(fields, y_low, y_high):
    return pl.pallas_call(
        x_edge_kernel,
        grid=(1,),
        in_specs=[
            pl.BlockSpec((16, 2, 8, 256), lambda n: (0, 0, 0, 0)),
            pl.BlockSpec((16, 2, 8, 256), lambda n: (0, 3, 0, 0)),
            pl.BlockSpec((2, 128, 256), lambda n: (0, 0, 0)),
            pl.BlockSpec((2, 128, 256), lambda n: (0, 0, 0)),
        ],
        out_specs=[pl.BlockSpec((288, 256), lambda n: (0, 0))] * 2,
        out_shape=[jax.ShapeDtypeStruct((288, 256), BF16)] * 2,
        scratch_shapes=[pltpu.VMEM((2, 128, 256), F32)],
        cost_estimate=pl.CostEstimate(flops=100000, bytes_accessed=1 << 20, transcendentals=0),
    )(fields, fields, y_low, y_high)


def route(s, t):
    z = ((t >> 2) - (s >> 2)) & 7
    differ = (s ^ t) & 1
    cross = ((s ^ t) >> 1) & 1
    near = 1 + differ
    m = z * 4 + near + cross * (2 * differ - 1)
    mu = z * 4 + near + cross * (2 - 4 * differ)
    return m, mu


def arrived_from(t, mu):
    y = ((t >> 2) - (mu >> 2)) & 7
    cross = 1 - ((mu ^ (mu >> 1)) & 1)
    differ = (mu & 1) ^ 1
    return y * 4 + (((t >> 1) ^ cross) & 1) * 2 + ((t ^ differ) & 1)


def embed_kernel(who_ref, patches_ref, weight_ref, keep_ref, send_hbm, send_ref, out_sem):
    seq = who_ref[0]
    other = (seq & 1) == 1
    left = [patches_ref[:, b].reshape(256, 512) for b in range(2)]
    size = 256
    stores = []
    for n in range(4):
        columns = pl.ds(n * size, size)
        total = jnp.dot(left[0], weight_ref[0, :, columns], preferred_element_type=F32)
        total = total + jnp.dot(left[1], weight_ref[1, :, columns], preferred_element_type=F32)
        total = total.reshape(16, 2, 8, size)
        for t in range(32):
            rows = total[t % 16, t // 16]
            rows = jnp.where(other, pltpu.roll(rows, 4, 0), rows)
            keep_ref[route(seq, t)[0], :, columns] = rows[0:4]
            send_ref[route(seq ^ 1, t)[0], :, columns] = rows[4:8].astype(BF16)
        store = pltpu.make_async_copy(
            send_ref.at[:, :, columns], send_hbm.at[:, :, columns], out_sem.at[n]
        )
        store.start()
        stores.append(store)
    for store in stores:
        store.wait()


def embed(who, patches, weight):
    return pl.pallas_call(
        embed_kernel,
        in_specs=[pl.BlockSpec(memory_space=pltpu.SMEM), VMEM, VMEM],
        out_specs=[VMEM, pl.BlockSpec(memory_space=pl.ANY)],
        out_shape=[
            jax.ShapeDtypeStruct((32, 4, 1024), F32),
            pltpu.HBM((32, 4, 1024), BF16),
        ],
        scratch_shapes=[pltpu.VMEM((32, 4, 1024), BF16), pltpu.SemaphoreType.DMA((4,))],
        compiler_params=ROOM,
        cost_estimate=pl.CostEstimate(flops=540000000, bytes_accessed=3 << 20, transcendentals=0),
    )(who, patches, weight)


def norm_kernel(who_ref, rows_ref, position_ref, gain_ref, out_ref):
    part = arrived_from(who_ref[0], who_ref[1]) & 3
    block = position_ref[...].astype(F32).reshape(4, 4, 1024)
    hidden = rows_ref[...]
    for k in range(4):
        hidden = hidden + jnp.where(part == k, block[k], 0.0)
    row_mean = jnp.mean(hidden, -1, keepdims=True)
    row_square = jnp.mean(hidden * hidden, -1, keepdims=True)
    variance = row_square - row_mean * row_mean
    normed = (hidden - row_mean) * lax.rsqrt(variance + epsilon) * gain_ref[...]
    out_ref[...] = jnp.broadcast_to(normed.astype(BF16)[None], (32, 4, 1024))


def norm(who, rows, position, norm_gain):
    return pl.pallas_call(
        norm_kernel,
        grid_spec=pltpu.PrefetchScalarGridSpec(
            num_scalar_prefetch=1,
            grid=(1,),
            in_specs=[
                pl.BlockSpec((4, 1024), lambda n, who: (0, 0)),
                pl.BlockSpec((16, 1024), lambda n, who: (arrived_from(who[0], who[1]) >> 2, 0)),
                pl.BlockSpec((1, 1024), lambda n, who: (0, 0)),
            ],
            out_specs=pl.BlockSpec((32, 4, 1024), lambda n, who: (0, 0, 0)),
        ),
        out_shape=jax.ShapeDtypeStruct((32, 4, 1024), BF16),
        compiler_params=ROOM,
        cost_estimate=pl.CostEstimate(flops=100000, bytes_accessed=300000, transcendentals=0),
    )(who, rows, position, norm_gain.reshape(1, 1024))


def head_kernel(who_ref, normed_ref, weight_ref, out_hbm, out_ref, out_sem):
    gathered = normed_ref[...].astype(F32).reshape(128, 1024).astype(BF16)
    row = lax.broadcasted_iota(jnp.int32, (128, 128), 0)
    column = lax.broadcasted_iota(jnp.int32, (128, 128), 1)
    _, mu = route(row >> 2, who_ref[0])
    order = jnp.where(column == mu * 4 + (row & 3), 1.0, 0.0).astype(BF16)
    left = jnp.dot(order, gathered, preferred_element_type=F32).astype(BF16)
    stores = []
    for n, (start, size) in enumerate(HEAD_COLUMNS):
        columns = pl.ds(start, size)
        product = jnp.dot(left, weight_ref[:, columns], preferred_element_type=F32)
        out_ref[:, columns] = product.astype(BF16)
        store = pltpu.make_async_copy(out_ref.at[:, columns], out_hbm.at[:, columns], out_sem.at[n])
        store.start()
        stores.append(store)
    for store in stores:
        store.wait()


HEAD_COLUMNS = ((0, 512), (512, 512), (1024, 384))


def head(who, normed, head_weight):
    return pl.pallas_call(
        head_kernel,
        in_specs=[pl.BlockSpec(memory_space=pltpu.SMEM), VMEM, VMEM],
        out_specs=pl.BlockSpec(memory_space=pl.ANY),
        out_shape=jax.ShapeDtypeStruct((128, 1408), BF16),
        scratch_shapes=[
            pltpu.VMEM((128, 1408), BF16),
            pltpu.SemaphoreType.DMA((len(HEAD_COLUMNS),)),
        ],
        compiler_params=ROOM,
        cost_estimate=pl.CostEstimate(flops=370000000, bytes_accessed=4 << 20, transcendentals=0),
    )(who, normed, head_weight)


def advance_kernel(
    edge_ref, fields_ref, source_ref, yl_ref, yh_ref, xl_ref, xh_ref,
    out_ref, ylo, yhi, xlo, xhi, clo, chi, one_ref, face_ref,
):
    ylo[...] = yl_ref[...].astype(F32)
    yhi[...] = yh_ref[...].astype(F32)
    for payload, cells, corners in ((xl_ref, xlo, clo), (xh_ref, xhi, chi)):
        cells[...] = payload[0:256].astype(F32).reshape(2, 128, 256)
        corners[...] = payload[256:288].astype(F32).reshape(2, 16, 256)
    row = lax.broadcasted_iota(jnp.int32, (8, 256), 0)
    lane = lax.broadcasted_iota(jnp.int32, (8, 256), 1)
    first_row, last_row = row == 0, row == 7
    first_lane, last_lane = lane == 0, lane == 255

    def shifted(tile, low, high):
        before = jnp.where(first_row, low, pltpu.roll(tile, 1, 0))
        after = jnp.where(last_row, high, pltpu.roll(tile, 7, 0))
        return before, after

    def tendency(centre, velocity, xm, xp, ym, yp):
        zm = jnp.where(first_lane, 0.0, pltpu.roll(centre, 1, 1))
        zp = jnp.where(last_lane, 0.0, pltpu.roll(centre, 255, 1))
        laplacian = xp + xm + yp + ym + zp + zm - 6.0 * centre
        advection = velocity[0] * (xp - xm) + velocity[1] * (yp - ym) + velocity[2] * (zp - zm)
        return diffusivity * laplacian - 0.5 * advection

    def at8(f):
        return pl.ds(pl.multiple_of(f * 8, 8), 8)

    def first_stage(f, carry):
        mine = at8(f)
        for i in range(8):
            centre = fields_ref[f, i]
            xm = fields_ref[f, i - 1] if i > 0 else xlo[1, mine]
            xp = fields_ref[f, i + 1] if i < 7 else xhi[0, mine]
            low = ylo[1, pl.ds(f * 8 + i, 1)]
            high = yhi[0, pl.ds(f * 8 + i, 1)]
            ym, yp = shifted(centre, low, high)
            velocity = [fields_ref[k, i] for k in range(3)]
            one_ref[f, i] = centre + time_step * tendency(centre, velocity, xm, xp, ym, yp)
        for side in range(2):
            halo = xlo if side == 0 else xhi
            corner = clo if side == 0 else chi
            near = 1 if side == 0 else 0
            centre = halo[near, mine]
            outer = halo[1 - near, mine]
            inner = fields_ref[f, 0 if side == 0 else 7]
            xm, xp = (outer, inner) if side == 0 else (inner, outer)
            ym, yp = shifted(centre, corner[0, pl.ds(f, 1)], corner[1, pl.ds(f, 1)])
            velocity = [halo[near, k * 8 : k * 8 + 8] for k in range(3)]
            value = centre + time_step * tendency(centre, velocity, xm, xp, ym, yp)
            face_ref[side, mine] = value * edge_ref[side]
        for side in range(2):
            halo = ylo if side == 0 else yhi
            near = 1 if side == 0 else 0
            centre = halo[near, mine]
            outer = halo[1 - near, mine]
            inner = fields_ref[f, :, 0 if side == 0 else 7, :]
            ym, yp = (outer, inner) if side == 0 else (inner, outer)
            xm, xp = shifted(centre, clo[side, pl.ds(f, 1)], chi[side, pl.ds(f, 1)])
            velocity = [halo[near, k * 8 : k * 8 + 8] for k in range(3)]
            value = centre + time_step * tendency(centre, velocity, xm, xp, ym, yp)
            face_ref[2 + side, mine] = value * edge_ref[2 + side]
        return carry

    lax.fori_loop(0, 16, first_stage, 0)

    def second_stage(f, with_source):
        mine = at8(f)
        for i in range(8):
            centre = one_ref[f, i]
            xm = one_ref[f, i - 1] if i > 0 else face_ref[0, mine]
            xp = one_ref[f, i + 1] if i < 7 else face_ref[1, mine]
            low = face_ref[2, pl.ds(f * 8 + i, 1)]
            high = face_ref[3, pl.ds(f * 8 + i, 1)]
            ym, yp = shifted(centre, low, high)
            velocity = [one_ref[k, i] for k in range(3)]
            value = 0.5 * (fields_ref[f, i] + centre + time_step * tendency(centre, velocity, xm, xp, ym, yp))
            if with_source:
                value = value + time_step * source_ref[f - 3, i].astype(F32)
            out_ref[f, i] = value

    for f in range(3):
        second_stage(f, False)

    def species(f, carry):
        second_stage(f, True)
        return carry

    lax.fori_loop(3, 16, species, 0)


def advance(edges, fields, lagged_source, y_low, y_high, x_low, x_high):
    return pl.pallas_call(
        advance_kernel,
        in_specs=[pl.BlockSpec(memory_space=pltpu.SMEM)] + [VMEM] * 6,
        out_specs=VMEM,
        out_shape=jax.ShapeDtypeStruct((16, 8, 8, 256), F32),
        scratch_shapes=[pltpu.VMEM((2, 128, 256), F32)] * 4
        + [pltpu.VMEM((2, 16, 256), F32)] * 2
        + [pltpu.VMEM((16, 8, 8, 256), F32), pltpu.VMEM((4, 128, 256), F32)],
        cost_estimate=pl.CostEstimate(flops=100000000, bytes_accessed=4 << 20, transcendentals=0),
    )(edges, fields, lagged_source, y_low, y_high, x_low, x_high)


def along(value, axes, step):
    count = 1
    for axis in axes:
        count *= lax.axis_size(axis)
    pairs = [(i, i + step) for i in range(count) if 0 <= i + step < count]
    return lax.ppermute(value, axes, pairs)


SWAP = [
    (s * 32 + route(s, t)[0], t * 32 + route(s, t)[1]) for s in range(32) for t in range(32)
]


def on_device(fields, lagged_source, embed_weight, position, norm_gain, head_weight):
    core = lax.axis_index("core")
    mp = lax.axis_index("mp")
    seq = lax.axis_index("sq") * 2 + core
    x_axes = ("sq", "core")

    patches = lax.all_to_all(pack(fields), "mp", 0, 0, tiled=True)

    y_first, y_last = y_edges(fields)
    y_low = along(y_last, ("mp",), 1)
    y_high = along(y_first, ("mp",), -1)
    who = jnp.stack([seq, mp]).astype(jnp.int32)
    edges = jnp.stack([seq > 0, seq < 31, mp > 0, mp < 31]).astype(F32)
    weight = lax.dynamic_slice_in_dim(embed_weight, core * 1024, 1024, 0).reshape(2, 512, 1024)
    patches, who, edges, weight, y_low, y_high = lax.optimization_barrier(
        (patches, who, edges, weight, y_low, y_high)
    )

    patches = patches.reshape(16, 2, 16, 512)
    keep, send = embed(who, patches, weight)
    theirs = lax.ppermute(send, "core", [(0, 1), (1, 0)])
    partial_sums = (keep + theirs.astype(F32)).astype(BF16)
    pieces = lax.all_to_all(partial_sums, "mp", 0, 0, tiled=True)

    x_first, x_last = x_edges(fields, y_low, y_high)
    first_core = core == 0
    far = [(i, i + 1) for i in range(1, 31, 2)]
    far = far + [(j, i) for i, j in far]
    from_far = lax.ppermute(jnp.where(first_core, x_first, x_last), x_axes, far)
    from_near = lax.ppermute(jnp.where(first_core, x_last, x_first), "core", [(0, 1), (1, 0)])

    rows = jnp.sum(pieces.astype(F32), 0)
    rows = lax.ppermute(rows, ALL, SWAP)
    rows, from_far, from_near = lax.optimization_barrier((rows, from_far, from_near))
    x_low = jnp.where(first_core, from_far, from_near)
    x_high = jnp.where(first_core, from_near, from_far)
    everyone = norm(who, rows, position, norm_gain)
    normed = lax.all_to_all(everyone, "mp", 0, 0, tiled=True)

    edges, _ = lax.optimization_barrier((edges, everyone))
    fields_next = advance(edges, fields, lagged_source, y_low, y_high, x_low, x_high)
    normed, fields_next = lax.optimization_barrier((normed, fields_next))

    return fields_next, head(who, normed, head_weight)


def solution(mesh):
    split = Mesh(mesh.devices.reshape(16, 2, 32), ALL)
    seq = ("sq", "core")
    placed = (
        P(None, seq, "mp", None),
        P(None, seq, "mp", None),
        P("mp", None),
        P(seq, None),
        P(),
        P(None, "mp"),
    )
    return jax.shard_map(
        on_device,
        mesh=split,
        in_specs=placed,
        out_specs=(P(None, seq, "mp", None), P(seq, "mp")),
        check_vma=False,
    )
```
